32 devices in a mesh: dir: 2 (over core), wide: 16 (over z, y, x).
Axes of the slice: x: 2, y: 2, z: 4, core: 2. Of those that a mesh axis runs over, the one named last changes fastest.
Arguments:
- tokens: bfloat16 [16, 1176, 384], P('wide'), may hold values from -6 to 6
- cotangent: bfloat16 [16, 1176, 384], P('wide', 'dir'), may hold values from -6 to 6
- view_counts: int32 [16], P('wide'), may hold values from 2 to 3, as said below
- view_strides: int32 [16, 3], P('wide'), may hold values from 1 to 4
- view_offsets: int32 [16, 3], P('wide'), may hold values from 0 to 1176, as said below
- in_proj: float32 [384, 1536], P('wide'), may hold values from -0.3125 to 0.3125
- in_proj_first: float32 [384, 1536], P('wide'), may hold values from -8 to 8
- in_proj_second: float32 [384, 1536], P('wide'), may hold values from 9.897216 to 39.5136
- out_proj: float32 [768, 384], P('wide'), may hold values from -0.625 to 0.625
- out_proj_first: float32 [768, 384], P('wide'), may hold values from -16 to 16
- out_proj_second: float32 [768, 384], P('wide'), may hold values from 39.5136 to 158.0544
- norm_gain: float32 [384], P('wide'), may hold values from 0.5 to 1.5
- norm_gain_first: float32 [384], P('wide'), may hold values from -48 to 48
- norm_gain_second: float32 [384], P('wide'), may hold values from 248.3712 to 989.7216
- state_proj: float32 [2, 768, 56], P('dir', 'wide'), may hold values from -0.21875 to 0.21875
- state_proj_first: float32 [2, 768, 56], P('dir', 'wide'), may hold values from -4 to 4
- state_proj_second: float32 [2, 768, 56], P('dir', 'wide'), may hold values from 2.483712 to 9.897216
- step_proj: float32 [2, 24, 768], P('dir', None, 'wide'), may hold values from -1.25 to 1.25
- step_proj_first: float32 [2, 24, 768], P('dir', None, 'wide'), may hold values from -1.75 to 1.75
- step_proj_second: float32 [2, 24, 768], P('dir', None, 'wide'), may hold values from 0.395136 to 1.580544
- log_decay: float32 [2, 16, 768], P('dir', None, 'wide'), may hold values from 0 to 2.8
- log_decay_first: float32 [2, 16, 768], P('dir', None, 'wide'), may hold values from -1.75 to 1.75
- log_decay_second: float32 [2, 16, 768], P('dir', None, 'wide'), may hold values from 0.395136 to 1.580544
- channels: float32 [2, 7, 768], P('dir', None, 'wide'), may hold values from -7 to 2
- channels_first: float32 [2, 7, 768], P('dir', None, 'wide'), may hold values from -4 to 4
- channels_second: float32 [2, 7, 768], P('dir', None, 'wide'), may hold values from 2.483712 to 9.897216
Outputs:
- block_out: float32 [16, 1176, 384], P('wide', 'dir')
- token_grad: float32 [16, 1176, 384], P('wide', 'dir')
- step_stats: float32 [2, 2, 768], P('dir', None, 'wide')
- new_in_proj: float32 [384, 1536], P('wide')
- new_in_first: float32 [384, 1536], P('wide')
- new_in_second: float32 [384, 1536], P('wide')
- new_out_proj: float32 [768, 384], P('wide')
- new_out_first: float32 [768, 384], P('wide')
- new_out_second: float32 [768, 384], P('wide')
- new_gain: float32 [384], P('wide')
- new_gain_first: float32 [384], P('wide')
- new_gain_second: float32 [384], P('wide')
- new_state_proj: float32 [2, 768, 56], P('dir', 'wide')
- new_state_first: float32 [2, 768, 56], P('dir', 'wide')
- new_state_second: float32 [2, 768, 56], P('dir', 'wide')
- new_step_proj: float32 [2, 24, 768], P('dir', None, 'wide')
- new_step_first: float32 [2, 24, 768], P('dir', None, 'wide')
- new_step_second: float32 [2, 24, 768], P('dir', None, 'wide')
- new_log_decay: float32 [2, 16, 768], P('dir', None, 'wide')
- new_decay_first: float32 [2, 16, 768], P('dir', None, 'wide')
- new_decay_second: float32 [2, 16, 768], P('dir', None, 'wide')
- new_channels: float32 [2, 7, 768], P('dir', None, 'wide')
- new_chan_first: float32 [2, 7, 768], P('dir', None, 'wide')
- new_chan_second: float32 [2, 7, 768], P('dir', None, 'wide')
The draws below stay inside these ranges and needn't reach their ends.
Inputs may be any that keep to these rules, and one draw needn't show every extreme that they name: `view_counts`: both counts occur in every draw. `view_offsets`: a video's views start at increasing offsets, lie inside its 1176 slots and do not intersect; entries at or past its view count equal 1176. `view_strides`: strides at or past a video's view count are not used.
All inputs are finite; a program needn't handle non-finite values.
Results may differ from the reference program's by a relative error of at most 0.015.
The reference program's roundings to bfloat16 on the way count: a program that leaves them out, or rounds other values in their place, can miss the bound.
Values may be sent and summed in bfloat16 or wider, within the bound.
A program may use at most 512 MiB of HBM per device.

```python
import math
from functools import partial
import jax
import jax.numpy as jnp
from jax import lax

D = 384
INNER = 768
STATE = 16
RANK = 24
CONV = 4
PATCHES = 196
MAX_VIEWS = 3
STEP = 10
VIEW_TOK = 392
SLOT_TOK = 1176
VIDEOS = 16
TOKENS = 18816
PROJ = 56
CHANNEL_ROWS = 7


def view_plan(key):
    count_key, pick_key, cut_key = jax.random.split(key, 3)
    view_counts = jax.random.randint(count_key, (VIDEOS,), 2, 4)
    chosen = jax.random.randint(pick_key, (), 0, VIDEOS)
    view_counts = view_counts.at[chosen].set(3).at[(chosen + 1) % VIDEOS].set(2)
    cuts = jax.random.randint(cut_key, (VIDEOS, 2), 0, VIEW_TOK + 1)
    lower = jnp.minimum(cuts[:, 0], cuts[:, 1])
    upper = jnp.maximum(cuts[:, 0], cuts[:, 1])
    spaced = jnp.stack([lower, upper + VIEW_TOK, jnp.full((VIDEOS,), SLOT_TOK, jnp.int32)], 1)
    packed = (jnp.arange(MAX_VIEWS, dtype=jnp.int32) * VIEW_TOK)[None, :] * jnp.ones((VIDEOS, 1), jnp.int32)
    offsets = jnp.where(view_counts[:, None] == 3, packed, spaced)
    return (view_counts.astype(jnp.int32), offsets.astype(jnp.int32))


def draw_view_counts(key, part):
    return view_plan(key)[0]


def draw_view_offsets(key, part):
    return view_plan(key)[1]


def draw_channels(key, part):
    key = jax.random.fold_in(key, 11)
    tap_key, bias_key, step_key, skip_key = jax.random.split(key, 4)
    tap_rows = jnp.clip(jax.random.normal(tap_key, (2, CONV, INNER), jnp.float32) * 0.5, -1.5, 1.5)
    bias_row = jnp.clip(jax.random.normal(bias_key, (2, 1, INNER), jnp.float32) * 0.3, -1.0, 1.0)
    step_size = jnp.exp(jax.random.uniform(step_key, (2, 1, INNER), jnp.float32, math.log(0.001), math.log(0.1)))
    step_bias = jnp.log(jnp.expm1(step_size))
    skip_row = jax.random.uniform(skip_key, (2, 1, INNER), jnp.float32, 0.5, 1.5)
    return jnp.concatenate([tap_rows, bias_row, step_bias, skip_row], 1)


def plant(entries, own_key, low, largest):
    longest = entries.shape.index(max(entries.shape))
    spots = []
    for shift in (0, 1):
        where = [jax.random.randint(jax.random.fold_in(own_key, axis), (), 0, length) for axis, length in enumerate(entries.shape)]
        where[longest] = (where[longest] + shift) % entries.shape[longest]
        spots.append(tuple(where))
    return entries.at[spots[0]].set(low).at[spots[1]].set(largest)


def shard_levels(own_key, extent, cuts, least, top_value):
    factor_of, own = 1.0, jax.random.fold_in(own_key, 6)
    for axis_at, parts in cuts:
        draws = jnp.exp(jax.random.uniform(jax.random.fold_in(own, axis_at), (parts,), jnp.float32, least / len(cuts), top_value / len(cuts)))
        factor_of = factor_of * jnp.repeat(draws, extent[axis_at] // parts).reshape([-1 if axis == axis_at else 1 for axis in range(len(extent))])
    return factor_of


def bell_draw(key, shape, scale, bound, shards=(), held_as=jnp.bfloat16):
    entries = scale * jax.random.normal(key, shape, jnp.float32)
    if shards:
        entries = entries * shard_levels(key, shape, shards, -0.22, 0.18)
    return jnp.clip(entries, -bound, bound).astype(held_as)


def setup_inputs(seed: int = 0) -> dict:
    splits = jax.random.split(jax.random.key(seed), 27)
    return {
        "tokens": bell_draw(splits[0], (VIDEOS, SLOT_TOK, D), 1.0, 6.0, ((0, 16),)),
        "cotangent": bell_draw(splits[1], (VIDEOS, SLOT_TOK, D), 1.0, 6.0, ((0, 16), (1, 2))),
        "view_counts": draw_view_counts(jax.random.fold_in(splits[26], 71), 0),
        "view_strides": plant(jax.random.randint(splits[3], (VIDEOS, MAX_VIEWS), 1, 5), jax.random.fold_in(splits[3], 1), 1, 4).astype(jnp.int32),
        "view_offsets": draw_view_offsets(jax.random.fold_in(splits[26], 71), 0),
        "in_proj": bell_draw(splits[5], (D, 2 * INNER), D ** -0.5, 0.3125, ((0, 16),), jnp.float32),
        "in_proj_first": bell_draw(splits[6], (D, 2 * INNER), (0.0111 * TOKENS ** 0.5), 8.0, ((0, 16),), jnp.float32),
        "in_proj_second": jnp.clip(jnp.exp(math.log(39.5136) - 1.3843914 * jax.random.uniform(splits[7], (D, 2 * INNER), jnp.float32) ** shard_levels(splits[7], (D, 2 * INNER), ((0, 16),), -0.2, 0.2)), 9.897216, 39.5136),
        "out_proj": bell_draw(splits[8], (INNER, D), (INNER // 8) ** -0.5, 0.625, ((0, 16),), jnp.float32),
        "out_proj_first": bell_draw(splits[9], (INNER, D), (0.0222 * TOKENS ** 0.5), 16.0, ((0, 16),), jnp.float32),
        "out_proj_second": jnp.clip(jnp.exp(math.log(158.0544) - 1.3862944 * jax.random.uniform(splits[10], (INNER, D), jnp.float32) ** shard_levels(splits[10], (INNER, D), ((0, 16),), -0.2, 0.2)), 39.5136, 158.0544),
        "norm_gain": jnp.clip(1.0 + 0.1 * jax.random.normal(splits[11], (D,), jnp.float32), 0.5, 1.5),
        "norm_gain_first": bell_draw(splits[12], (D,), (0.0555 * TOKENS ** 0.5), 48.0, ((0, 16),), jnp.float32),
        "norm_gain_second": jnp.clip(jnp.exp(math.log(989.7216) - 1.3824993 * jax.random.uniform(splits[13], (D,), jnp.float32) ** shard_levels(splits[13], (D,), ((0, 16),), -0.2, 0.2)), 248.3712, 989.7216),
        "state_proj": bell_draw(splits[14], (2, INNER, PROJ), INNER ** -0.5, 0.21875, ((0, 2), (1, 16)), jnp.float32),
        "state_proj_first": bell_draw(splits[15], (2, INNER, PROJ), (0.00555 * TOKENS ** 0.5), 4.0, ((0, 2), (1, 16)), jnp.float32),
        "state_proj_second": jnp.clip(jnp.exp(math.log(9.897216) - 1.3824993 * jax.random.uniform(splits[16], (2, INNER, PROJ), jnp.float32) ** shard_levels(splits[16], (2, INNER, PROJ), ((0, 2), (1, 16)), -0.2, 0.2)), 2.483712, 9.897216),
        "step_proj": bell_draw(splits[17], (2, RANK, INNER), RANK ** -0.5, 1.25, ((0, 2), (2, 16)), jnp.float32),
        "step_proj_first": bell_draw(splits[18], (2, RANK, INNER), (0.00222 * TOKENS ** 0.5), 1.75, ((0, 2), (2, 16)), jnp.float32),
        "step_proj_second": jnp.clip(jnp.exp(math.log(1.580544) - 1.3862944 * jax.random.uniform(splits[19], (2, RANK, INNER), jnp.float32) ** shard_levels(splits[19], (2, RANK, INNER), ((0, 2), (2, 16)), -0.2, 0.2)), 0.395136, 1.580544),
        "log_decay": jnp.clip(2.8 * jax.random.uniform(splits[20], (2, STATE, INNER), jnp.float32) ** shard_levels(splits[20], (2, STATE, INNER), ((0, 2), (2, 16)), -0.2, 0.2), 0.0, 2.8),
        "log_decay_first": bell_draw(splits[21], (2, STATE, INNER), (0.00222 * TOKENS ** 0.5), 1.75, ((0, 2), (2, 16)), jnp.float32),
        "log_decay_second": jnp.clip(jnp.exp(math.log(1.580544) - 1.3862944 * jax.random.uniform(splits[22], (2, STATE, INNER), jnp.float32) ** shard_levels(splits[22], (2, STATE, INNER), ((0, 2), (2, 16)), -0.2, 0.2)), 0.395136, 1.580544),
        "channels": draw_channels(jax.random.fold_in(splits[26], 71), 0),
        "channels_first": bell_draw(splits[24], (2, CHANNEL_ROWS, INNER), (0.00555 * TOKENS ** 0.5), 4.0, ((0, 2), (2, 16)), jnp.float32),
        "channels_second": jnp.clip(jnp.exp(math.log(9.897216) - 1.3824993 * jax.random.uniform(splits[25], (2, CHANNEL_ROWS, INNER), jnp.float32) ** shard_levels(splits[25], (2, CHANNEL_ROWS, INNER), ((0, 2), (2, 16)), -0.2, 0.2)), 2.483712, 9.897216),
    }


@jax.custom_vjp
def low(v):
    return lax.optimization_barrier(v.astype(jnp.bfloat16)).astype(jnp.float32)

@jax.custom_vjp
def low_back(v):
    return v

def low_keep(v):
    return (low(v), None)

def low_pass(kept, grad):
    return (grad,)

def back_keep(v):
    return (v, None)

def back_low(kept, grad):
    return (low(grad),)
low.defvjp(low_keep, low_pass)
low_back.defvjp(back_keep, back_low)
HIGH = lax.Precision.HIGHEST
EPS_NORM = 1e-06
BETA_ONE = 0.9
BETA_TWO = 0.95
EPS_ADAM = 1e-08
RATES = (0.15, 0.1, 2.5, 0.12, 0.2, 1.0, 2.5)
DECAYS = (0.1, 0.1, 0.0, 0.1, 0.1, 0.0, 0.0)

def layout(view_count, strides, offsets, slot_count, view_len, patches):
    places = jnp.arange(slot_count, dtype=jnp.int32)
    live_mask = jnp.zeros((slot_count,), jnp.float32)
    labels = jnp.full((slot_count,), -1, jnp.int32)
    clock_time = jnp.zeros((slot_count,), jnp.float32)
    for view_index in range(strides.shape[0]):
        view_start = offsets[view_index]
        inside = (places >= view_start) & (places < view_start + view_len) & (view_index < view_count)
        frame_no = (places - view_start) // patches
        live_mask = jnp.where(inside, 1.0, live_mask)
        labels = jnp.where(inside, view_index, labels)
        clock_time = jnp.where(inside, (frame_no * strides[view_index]).astype(jnp.float32), clock_time)
    return (live_mask, labels, clock_time)

def time_embed(clock_time, model_width):
    half_width = model_width // 2
    frequency = jnp.exp(-math.log(10000.0) * jnp.arange(half_width, dtype=jnp.float32) / half_width)
    angles = clock_time[:, None] * frequency[None, :]
    return jnp.concatenate([jnp.sin(angles), jnp.cos(angles)], 1)

def lag_masks(labels, tap_count):
    mask_rows = []
    for back_step in range(tap_count):
        before = jnp.concatenate([jnp.full((back_step,), -2, jnp.int32), labels[:labels.shape[0] - back_step]])
        mask_rows.append((before == labels).astype(jnp.float32))
    return jnp.stack(mask_rows)

def convolve(inner_rows, tap_rows, bias_row, lag_rows):
    total = bias_row[None, :] + tap_rows[0][None, :] * inner_rows
    for back_step in range(1, tap_rows.shape[0]):
        shifted = jnp.concatenate([jnp.zeros((back_step, inner_rows.shape[1]), inner_rows.dtype), inner_rows[:-back_step]], 0)
        total = total + tap_rows[back_step][None, :] * shifted * lag_rows[back_step][:, None]
    return jax.nn.silu(total)

def recurrence(acted_rows, step_size, b_rows, c_rows, decay_rate, keep_rows):

    def advance(carried, inputs_now):
        acted_now, step_now, b_now, c_now, keep_now = inputs_now
        carried = jnp.exp(step_now[None, :] * decay_rate) * keep_now * carried + (step_now * acted_now)[None, :] * b_now[:, None]
        return (carried, lax.optimization_barrier(jnp.sum(c_now[:, None] * carried, 0)))
    initial = jnp.zeros(decay_rate.shape, decay_rate.dtype)
    _, outputs = lax.scan(advance, initial, (acted_rows, step_size, b_rows, c_rows, keep_rows))
    return outputs

def direction(inner_x, labels, live_mask, proj_weight, step_weight, log_rate, chan_rows):
    lag_rows = lag_masks(labels, CONV)
    acted_rows = convolve(inner_x, chan_rows[:CONV], chan_rows[CONV], lag_rows)
    projected = low_back(jnp.dot(low(acted_rows), proj_weight, precision=HIGH))
    step_in = low(projected[:, :RANK])
    b_rows = projected[:, RANK:RANK + STATE]
    c_rows = projected[:, RANK + STATE:]
    step_pre = low_back(jnp.dot(step_in, step_weight, precision=HIGH))
    step_size = jax.nn.softplus(step_pre + chan_rows[CONV + 1][None, :])
    decay_rate = -jnp.exp(log_rate)
    states = recurrence(acted_rows, step_size, b_rows, c_rows, decay_rate, lag_rows[1])
    step_stats = jnp.stack([lax.optimization_barrier(jnp.sum(live_mask[:, None] * step_size, 0)), lax.optimization_barrier(jnp.sum(live_mask[:, None] * step_size * step_size, 0))]) / VIEW_TOK
    return (states + chan_rows[CONV + 2][None, :] * acted_rows, step_stats)

def one_video(params, token_rows, live_mask, labels, clock_time):
    w_in, w_out, gain, proj_w, step_w, log_rate, chan = [low(weight) for weight in params]
    residual = token_rows + live_mask[:, None] * time_embed(clock_time, D)
    scale_rows = lax.rsqrt(lax.optimization_barrier(jnp.mean(residual * residual, -1, keepdims=True)) + EPS_NORM)
    normed = low(residual * scale_rows * gain[None, :])
    gate_in = low_back(jnp.dot(normed, w_in[:, INNER:], precision=HIGH))
    summed = jnp.zeros((SLOT_TOK, INNER), jnp.float32)
    stats_list = []
    for stream in range(2):
        inner_x = low_back(jnp.dot(normed, w_in[:, :INNER], precision=HIGH))
        labels_now = labels
        live_now = live_mask
        if stream == 1:
            inner_x = jnp.flip(inner_x, 0)
            labels_now = jnp.flip(labels, 0)
            live_now = jnp.flip(live_mask, 0)
        result, stats_now = direction(inner_x, labels_now, live_now, proj_w[stream], step_w[stream], log_rate[stream], chan[stream])
        if stream == 1:
            result = jnp.flip(result, 0)
        summed = summed + low(result)
        stats_list.append(stats_now)
    mixed = low_back(summed)
    gated = low(mixed * jax.nn.silu(gate_in))
    branch = jnp.dot(gated, w_out, precision=HIGH)
    return (residual + live_mask[:, None] * branch, jnp.stack(stats_list))

def adam_step(weight, gradient, first_moment, second, step_rate, decay_rate):
    first_moment = BETA_ONE * first_moment + (1.0 - BETA_ONE) * gradient
    second = BETA_TWO * second + (1.0 - BETA_TWO) * gradient * gradient
    first_hat = first_moment / (1.0 - BETA_ONE ** STEP)
    second_hat = second / (1.0 - BETA_TWO ** STEP)
    weight = weight - step_rate * (first_hat / (jnp.sqrt(second_hat) + EPS_ADAM) + decay_rate * weight)
    return (weight, first_moment, second)

def reference(tokens, cotangent, view_counts, view_strides, view_offsets, in_proj, in_proj_first, in_proj_second, out_proj, out_proj_first, out_proj_second, norm_gain, norm_gain_first, norm_gain_second, state_proj, state_proj_first, state_proj_second, step_proj, step_proj_first, step_proj_second, log_decay, log_decay_first, log_decay_second, channels, channels_first, channels_second):
    plan = partial(layout, slot_count=SLOT_TOK, view_len=VIEW_TOK, patches=PATCHES)
    live_mask, labels, clock_time = jax.vmap(plan)(view_counts, view_strides, view_offsets)
    masters = (in_proj, out_proj, norm_gain, state_proj, step_proj, log_decay, channels)

    def forward(params, token_rows):

        def per_video(inputs_now):
            return jax.checkpoint(one_video)(params, *inputs_now)
        outputs, stats_rows = lax.map(per_video, (token_rows, live_mask, labels, clock_time))
        return (outputs, lax.optimization_barrier(jnp.sum(stats_rows, 0)))
    block_out, pullback, step_stats = jax.vjp(forward, masters, tokens.astype(jnp.float32), has_aux=True)
    grads, token_grad = pullback(cotangent.astype(jnp.float32))
    new_in_proj, new_in_first, new_in_second = adam_step(in_proj, grads[0], in_proj_first, in_proj_second, RATES[0], DECAYS[0])
    new_out_proj, new_out_first, new_out_second = adam_step(out_proj, grads[1], out_proj_first, out_proj_second, RATES[1], DECAYS[1])
    new_gain, new_gain_first, new_gain_second = adam_step(norm_gain, grads[2], norm_gain_first, norm_gain_second, RATES[2], DECAYS[2])
    new_state_proj, new_state_first, new_state_second = adam_step(state_proj, grads[3], state_proj_first, state_proj_second, RATES[3], DECAYS[3])
    new_step_proj, new_step_first, new_step_second = adam_step(step_proj, grads[4], step_proj_first, step_proj_second, RATES[4], DECAYS[4])
    new_log_decay, new_decay_first, new_decay_second = adam_step(log_decay, grads[5], log_decay_first, log_decay_second, RATES[5], DECAYS[5])
    new_channels, new_chan_first, new_chan_second = adam_step(channels, grads[6], channels_first, channels_second, RATES[6], DECAYS[6])
    return (block_out, token_grad, step_stats, new_in_proj, new_in_first, new_in_second, new_out_proj, new_out_first, new_out_second, new_gain, new_gain_first, new_gain_second, new_state_proj, new_state_first, new_state_second, new_step_proj, new_step_first, new_step_second, new_log_decay, new_decay_first, new_decay_second, new_channels, new_chan_first, new_chan_second)
```

```python
import functools
import math

import jax
import jax.numpy as jnp
from jax import lax
from jax.experimental import pallas as pl
from jax.experimental.pallas import tpu as pltpu
from jax.sharding import PartitionSpec as P

PATCHES = 196
STEP = 10
VIEW_TOK = 392
EPS_NORM = 1e-06
BETA_ONE = 0.9
BETA_TWO = 0.95
EPS_ADAM = 1e-08
RATES = (0.15, 0.1, 2.5, 0.12, 0.2, 1.0, 2.5)
DECAYS = (0.1, 0.1, 0.0, 0.1, 0.1, 0.0, 0.0)

F32 = jnp.float32
BF = jnp.bfloat16
LN2 = math.log(2.0)
LOG2E = 1.0 / LN2

SLOTS = 1176
R = 1184
NB = R // 16
NP = NB // 2
HALF = 588
WIN = 608
WBASE = 576
D = 384
E = 768
G6 = E // 128
N = 16
RANK = 24
HALO = 8
XR = HALO + R + HALO
RING = 4
CUT = 1e4
ROW_B, ROW_C, ROW_STEP, ROW_DECAY, ROW_CHAN, ROW_GAIN = 24, 40, 56, 80, 96, 103
NT = (((1,), (1,)), ((), ()))
TN = (((0,), (0,)), ((), ()))
VMEM = pl.BlockSpec(memory_space=pltpu.VMEM)
SMEM = pl.BlockSpec(memory_space=pltpu.SMEM)
ANY = pl.BlockSpec(memory_space=pl.ANY)


def dot(a, b):
    return jnp.dot(a, b, preferred_element_type=F32)


def dot_nt(a, b):
    return lax.dot_general(a, b, NT, preferred_element_type=F32)


def dot_tn(a, b):
    return lax.dot_general(a, b, TN, preferred_element_type=F32)


def sigmoid(v):
    return 0.5 * jnp.tanh(0.5 * v) + 0.5


def rows16(b, n=16):
    return pl.ds(pl.multiple_of(b * 16, 16), n)


def labels_of(meta, r):
    lab = jnp.full(r.shape, -1, jnp.int32)
    late = jnp.zeros(r.shape, jnp.int32)
    for k in range(3):
        start = meta[1 + k]
        inside = (r >= start) & (r < start + VIEW_TOK) & (k < meta[0])
        lab = jnp.where(inside, k, lab)
        late = jnp.where(inside, jnp.where(r >= start + PATCHES, 1, 0), late)
    lab = jnp.where(r < 0, -2, lab)
    lab = jnp.where(r >= SLOTS, -3, lab)
    return lab, late


def residual_tile(meta, tok, etab, base, n):
    r = base + lax.broadcasted_iota(jnp.int32, (n, 128), 0)
    lab, late = labels_of(meta, r)
    live = jnp.where(lab >= 0, 1.0, 0.0)
    out = []
    for c in range(3):
        cols = slice(c * 128, c * 128 + 128)
        emb = jnp.where(lab >= 0, etab[3:4, cols], 0.0)
        for k in range(3):
            emb = jnp.where((lab == k) & (late == 1), etab[k : k + 1, cols], emb)
        out.append(tok[:, cols].astype(F32) + emb)
    return out, live


def row_scale(res):
    total = sum(jnp.sum(v * v, axis=1, keepdims=True) for v in res)
    return lax.rsqrt(total * (1.0 / D) + EPS_NORM)


def fill_labels(meta, lab_ref):
    for base in range(0, XR, 8):
        r = base - HALO + lax.broadcasted_iota(jnp.int32, (8, 128), 0)
        lab_ref[base : base + 8, :] = labels_of(meta, r)[0]


def gain_row(st_ref, wide):
    per = E // wide
    own = D // wide
    i = lax.broadcasted_iota(jnp.int32, (E, D), 0)
    j = lax.broadcasted_iota(jnp.int32, (E, D), 1)
    pick = jnp.where(i == (j // own) * per + j % own, 1.0, 0.0).astype(BF)
    src = jnp.broadcast_to(st_ref[ROW_GAIN : ROW_GAIN + 1, :], (16, E)).astype(BF)
    return dot(src, pick)[0:8]


def fill_broadcast(p_ref, lane, out_ref):
    def body(sb, _):
        base = pl.multiple_of(sb * 128, 128)
        v = p_ref[pl.ds(base, 128), :].T[lane : lane + N]
        for j in range(128):
            out_ref[pl.ds(pl.multiple_of((base + j) * N, N), N), :] = (
                jnp.broadcast_to(v[:, j : j + 1], (N, 128))
            )
        return 0

    lax.fori_loop(0, 10, body, 0)


def conv_tile(x_ref, lab_ref, st_ref, c, base, n, rev):
    cols = slice(c * 128, c * 128 + 128)
    here = lab_ref[pl.ds(base + HALO, n), :]
    lagged = [x_ref[c, pl.ds(base + HALO, n), :]]
    for j in (1, 2, 3):
        at = base + HALO + (j if rev else -j)
        same = lab_ref[pl.ds(at, n), :] == here
        lagged.append(jnp.where(same, x_ref[c, pl.ds(at, n), :], 0.0))
    total = st_ref[ROW_CHAN + 4 : ROW_CHAN + 5, cols]
    for j in range(4):
        total = total + st_ref[ROW_CHAN + j : ROW_CHAN + j + 1, cols] * lagged[j]
    return total, lagged


def fwd_kernel(
    wide, meta, tok, etab, w1, s_ref,
    normed_o, x_o, act_o, al_o, dl_o, p_o, st_o, res_o, stats_o, hs_o,
    lab, dm, u, bb, cbd, hse, hso, gain_s, sem,
):
    stream = meta[4]
    st_o[...] = s_ref[...].astype(F32).T
    fill_labels(meta, lab)
    gain_s[...] = gain_row(st_o, wide)

    def norm_tile(i, _):
        base = pl.multiple_of(i * 32, 32)
        res, _l = residual_tile(meta, tok[pl.ds(base, 32), :], etab, base, 32)
        scale = row_scale(res)
        for c in range(3):
            cols = slice(c * 128, c * 128 + 128)
            normed_o[pl.ds(base, 32), cols] = (res[c] * scale * gain_s[0:1, cols]).astype(BF)
        return 0

    lax.fori_loop(0, R // 32, norm_tile, 0)
    x_o[:, 0:HALO, :] = jnp.zeros((G6, HALO, 128), F32)
    x_o[:, HALO + R : XR, :] = jnp.zeros((G6, HALO, 128), F32)
    for h in range(2):
        for c in range(0, G6, 2):
            y = dot(normed_o[h * 592 : h * 592 + 592, :], w1[:, c * 128 : c * 128 + 256])
            x_o[c, HALO + h * 592 : HALO + h * 592 + 592, :] = y[:, :128]
            x_o[c + 1, HALO + h * 592 : HALO + h * 592 + 592, :] = y[:, 128:]

    def conv(rev):
        def tile(i, _):
            base = pl.multiple_of(i * 32, 32)
            for c in range(G6):
                total, _l = conv_tile(x_o, lab, st_o, c, base, 32, rev)
                act = total * sigmoid(total)
                act_o[c, pl.ds(base, 32), :] = act
                al_o[pl.ds(base, 32), c * 128 : c * 128 + 128] = act.astype(BF)
            return 0

        lax.fori_loop(0, R // 32, tile, 0)

    @pl.when(stream == 0)
    def _():
        conv(False)

    @pl.when(stream == 1)
    def _():
        conv(True)

    p_o[R:, :] = jnp.zeros((1280 - R, 128), F32)
    col = lax.broadcasted_iota(jnp.int32, (128, 256), 1)
    row = lax.broadcasted_iota(jnp.int32, (128, 256), 0)
    spread_c = jnp.where(row == ROW_C + col % N, 1.0, 0.0).astype(BF)
    diag = (
        lax.broadcasted_iota(jnp.int32, (592, 256), 0) % N
        == lax.broadcasted_iota(jnp.int32, (592, 256), 1) // N
    )
    for h in range(2):
        rows = slice(h * 592, h * 592 + 592)
        proj = dot(al_o[rows, :], s_ref[...])
        p_o[rows, :] = proj
        low = proj.astype(BF)
        cbd[rows, :] = jnp.where(diag, dot(low, spread_c), 0.0).astype(BF)
        step_in = low[:, :RANK]
        for c in range(0, G6, 2):
            w = st_o[ROW_STEP : ROW_STEP + RANK, c * 128 : c * 128 + 256].astype(BF)
            y = dot(step_in, w)
            dl_o[c, rows, :] = y[:, :128]
            dl_o[c + 1, rows, :] = y[:, 128:]
    stats_o[...] = jnp.zeros(stats_o.shape, F32)

    def soft(rev):
        def tile(i, _):
            base = pl.multiple_of(i * 32, 32)
            here = lab[pl.ds(base + HALO, 32), :]
            before = lab[pl.ds(base + HALO + (1 if rev else -1), 32), :]
            cut = jnp.where(here == before, 0.0, CUT)
            live = jnp.where(here >= 0, 1.0, 0.0)
            real = jnp.where(here >= -1, 1.0, 0.0)
            for c in range(G6):
                cols = slice(c * 128, c * 128 + 128)
                rows = pl.ds(base, 32)
                v = dl_o[c, rows, :] + st_o[ROW_CHAN + 5 : ROW_CHAN + 6, cols]
                delta = jnp.maximum(v, 0.0) + jnp.log1p(jnp.exp(-jnp.abs(v)))
                dl_o[c, rows, :] = delta
                dm[c, rows, :] = delta + cut
                u[c, rows, :] = delta * act_o[c, rows, :] * real
                t1 = live * delta
                t2 = t1 * delta
                for s in range(4):
                    stats_o[0, :, cols] += t1[8 * s : 8 * s + 8]
                    stats_o[1, :, cols] += t2[8 * s : 8 * s + 8]
            return 0

        lax.fori_loop(0, R // 32, tile, 0)

    @pl.when(stream == 0)
    def _():
        soft(False)

    @pl.when(stream == 1)
    def _():
        soft(True)

    fill_broadcast(p_o, ROW_B, bb)
    hs = (hse, hso)

    def save(k, i):
        slot = i % RING
        return pltpu.make_async_copy(hs[k].at[slot], hs_o.at[k, i], sem.at[k, slot])

    def scan(rev):
        rate = [
            -jnp.exp(st_o[ROW_DECAY : ROW_DECAY + N, c * 128 : c * 128 + 128]) * LOG2E
            for c in range(G6)
        ]

        def block_of(t):
            return NB - 1 - t if rev else t

        def emit(t, k, slot, c):
            rows = rows16(block_of(t))
            y = dot(cbd[rows, :], hs[k][slot, :, c * 128 : c * 128 + 256])
            for h in range(2):
                cols = slice((c + h) * 128, (c + h) * 128 + 128)
                skip = st_o[ROW_CHAN + 6 : ROW_CHAN + 7, cols]
                res_o[rows, cols] = (
                    y[:, h * 128 : h * 128 + 128] + skip * act_o[c + h, rows, :]
                ).astype(BF)

        def block(t, k, slot, state, late):
            b = block_of(t)
            state = list(state)
            for n, j in enumerate(range(15, -1, -1) if rev else range(16)):
                if n % 4 == 0 and late:
                    late.pop(0)()
                q = b * 16 + j
                drive = bb[pl.ds(pl.multiple_of(q * N, N), N), :]
                for c in range(G6):
                    fade = jnp.exp2(dm[c, pl.ds(q, 1), :] * rate[c])
                    state[c] = fade * state[c] + u[c, pl.ds(q, 1), :] * drive
                    hs[k][slot, j * N : j * N + N, c * 128 : c * 128 + 128] = state[c].astype(BF)
            return tuple(state)

        def pair(i, state):
            slot = i % RING

            @pl.when(i >= RING)
            def _():
                save(0, i - RING).wait()
                save(1, i - RING).wait()

            before = jnp.maximum(2 * i - 1, 0)
            late = [
                functools.partial(emit, before, 1, jnp.maximum(i - 1, 0) % RING, c)
                for c in (0, 2, 4)
            ]
            state = block(2 * i, 0, slot, state, late)
            late = [functools.partial(emit, 2 * i, 0, slot, c) for c in (0, 2, 4)]
            state = block(2 * i + 1, 1, slot, state, late)
            save(0, i).start()
            save(1, i).start()
            return state

        hso[0] = jnp.zeros((256, E), BF)
        lax.fori_loop(0, NP, pair, tuple(jnp.zeros((N, 128), F32) for _ in range(G6)))
        for c in (0, 2, 4):
            emit(NB - 1, 1, (NP - 1) % RING, c)
        for i in range(NP - RING, NP):
            save(0, i).wait()
            save(1, i).wait()

    @pl.when(stream == 0)
    def _():
        scan(False)

    @pl.when(stream == 1)
    def _():
        scan(True)


def forward(wide, meta, tok, etab, w1, s):
    S = jax.ShapeDtypeStruct
    return pl.pallas_call(
        functools.partial(fwd_kernel, wide),
        out_shape=[
            S((R, D), BF), S((G6, XR, 128), F32), S((G6, R, 128), F32), S((R, E), BF),
            S((G6, R, 128), F32), S((1280, 128), F32), S((128, E), F32), S((R, E), BF),
            S((2, 8, E), F32), S((2, NP, 256, E), BF),
        ],
        in_specs=[SMEM] + [VMEM] * 4,
        out_specs=[VMEM] * 9 + [ANY],
        scratch_shapes=[
            pltpu.VMEM((XR, 128), jnp.int32),
            pltpu.VMEM((G6, R, 128), F32),
            pltpu.VMEM((G6, R, 128), F32),
            pltpu.VMEM((1280 * N, 128), F32),
            pltpu.VMEM((R, 256), BF),
            pltpu.VMEM((RING, 256, E), BF),
            pltpu.VMEM((RING, 256, E), BF),
            pltpu.VMEM((8, D), F32),
            pltpu.SemaphoreType.DMA((2, RING)),
        ],
        compiler_params=pltpu.CompilerParams(vmem_limit_bytes=60 * 2**20),
        name="forward",
    )(meta, tok, etab, w1, s)


def mid_kernel(
    meta, tok, etab, cot, normed, own, other, w2, wo,
    block_o, mg_o, gpart_o, gw2_o, gwo_o,
    cotw, gated, bgrad, ggrad, blk,
):
    stream = meta[4]
    wbase = pl.multiple_of(stream * WBASE, 32)
    cotw[...] = jnp.zeros(cotw.shape, F32)
    for s, off in ((0, 0), (1, WIN - HALF - 8)):

        @pl.when(stream == s)
        def _():
            cotw[off : off + HALF, :] = cot[...].astype(F32)

    win = pl.ds(wbase, WIN)

    def live_of(base, n):
        r = wbase + base + lax.broadcasted_iota(jnp.int32, (n, 128), 0)
        return jnp.where(labels_of(meta, r)[0] >= 0, 1.0, 0.0)

    def tile(i, _):
        base = pl.multiple_of(i * 32, 32)
        live = live_of(base, 32)
        for c in range(3):
            cols = slice(c * 128, c * 128 + 128)
            bgrad[pl.ds(base, 32), cols] = (live * cotw[pl.ds(base, 32), cols]).astype(BF)
        return 0

    lax.fori_loop(0, WIN // 32, tile, 0)
    for c in range(0, E, 256):
        cols = slice(c, c + 256)
        gate = dot(normed[win, :], w2[:, cols])
        mixed = own[:, cols].astype(F32) + other[:, cols].astype(F32)
        sig = sigmoid(gate)
        silu = gate * sig
        gated[:, cols] = (mixed * silu).astype(BF)
        up = dot_nt(bgrad[...], wo[cols, :])
        mg_o[:, cols] = (up * silu).astype(BF)
        ggrad[:, cols] = (up * mixed * sig * (1.0 + gate * (1.0 - sig))).astype(BF)
    for c in range(0, D, 128):
        cols = slice(c, c + 128)
        branch = dot(gated[...], wo[:, cols])
        blk[:, cols] = branch
        gpart_o[:, cols] = dot_nt(ggrad[...], w2[cols, :])
        gw2_o[cols, :] = dot_tn(normed[win, cols], ggrad[...])
    for c in range(0, E, 256):
        gwo_o[c : c + 256, :] = dot_tn(gated[:, c : c + 256], bgrad[...])

    def out_tile(i, _):
        base = pl.multiple_of(i * 32, 32)
        at = pl.multiple_of(wbase + base, 32)
        res, live = residual_tile(meta, tok[pl.ds(at, 32), :], etab, at, 32)
        for c in range(3):
            cols = slice(c * 128, c * 128 + 128)
            blk[pl.ds(base, 32), cols] = res[c] + live * blk[pl.ds(base, 32), cols]
        return 0

    lax.fori_loop(0, WIN // 32, out_tile, 0)
    for s, off in ((0, 0), (1, WIN - HALF - 8)):

        @pl.when(stream == s)
        def _():
            block_o[...] = blk[off : off + HALF, :]


def middle(meta, tok, etab, cot, normed, own, other, w2, wo):
    S = jax.ShapeDtypeStruct
    return pl.pallas_call(
        mid_kernel,
        out_shape=[
            S((HALF, D), F32), S((WIN, E), BF), S((WIN, D), F32), S((D, E), F32), S((E, D), F32),
        ],
        in_specs=[SMEM] + [VMEM] * 8,
        out_specs=[VMEM] * 5,
        scratch_shapes=[
            pltpu.VMEM((WIN, D), F32), pltpu.VMEM((WIN, E), BF), pltpu.VMEM((WIN, D), BF),
            pltpu.VMEM((WIN, E), BF), pltpu.VMEM((WIN, D), F32),
        ],
        compiler_params=pltpu.CompilerParams(vmem_limit_bytes=60 * 2**20),
        name="middle",
    )(meta, tok, etab, cot, normed, own, other, w2, wo)


def bwd_kernel(
    meta, normed, x, act, al, dl, p, st, mgo, mgx, w1, hs_in,
    npart_o, gw1_o, gs_o,
    lab, dm, dy, dyb, ub, bb, bbd, dbm, dcm, dd, zs, dacc, pgs, hse, hso, g0, g1, z0, z1, dc, sel, sums, sem,
):
    stream = meta[4]
    fill_labels(meta, lab)

    def lay(i, _):
        base = pl.multiple_of(i * 32, 32)
        for c in range(G6):
            cols = slice(c * 128, c * 128 + 128)
            lowrow = mgo[pl.ds(pl.multiple_of(jnp.minimum(base, WIN - 32), 32), 32), cols].astype(F32)
            hirow = mgx[pl.ds(pl.multiple_of(jnp.maximum(base - WBASE, 0), 32), 32), cols].astype(F32)
            v = jnp.where(base < WIN, lowrow, 0.0) + jnp.where(base >= WBASE, hirow, 0.0)
            dy[c, pl.ds(base, 32), :] = v
            dyb[pl.ds(base, 32), cols] = v.astype(BF)
        return 0

    lax.fori_loop(0, R // 32, lay, 0)
    sums[...] = jnp.zeros(sums.shape, F32)

    def prep(rev):
        def tile(i, _):
            base = pl.multiple_of(i * 32, 32)
            rows = pl.ds(base, 32)
            here = lab[pl.ds(base + HALO, 32), :]
            before = lab[pl.ds(base + HALO + (1 if rev else -1), 32), :]
            cut = jnp.where(here == before, 0.0, CUT)
            real = jnp.where(here >= -1, 1.0, 0.0)
            for c in range(G6):
                cols = slice(c * 128, c * 128 + 128)
                dm[c, rows, :] = dl[c, rows, :] + cut
                a = act[c, rows, :]
                ub[rows, cols] = (dl[c, rows, :] * a * real).astype(BF)
                t = dy[c, rows, :] * a
                sums[0, :, cols] += t[0:8] + t[8:16] + t[16:24] + t[24:32]
            return 0

        lax.fori_loop(0, R // 32, tile, 0)

    @pl.when(stream == 0)
    def _():
        prep(False)

    @pl.when(stream == 1)
    def _():
        prep(True)

    col = lax.broadcasted_iota(jnp.int32, (128, 256), 1)
    row = lax.broadcasted_iota(jnp.int32, (128, 256), 0)
    spread_b = jnp.where(row == ROW_B + col % N, 1.0, 0.0).astype(BF)
    diag = (
        lax.broadcasted_iota(jnp.int32, (592, 256), 0) % N
        == lax.broadcasted_iota(jnp.int32, (592, 256), 1) // N
    )
    for h in range(2):
        rows = slice(h * 592, h * 592 + 592)
        bbd[rows, :] = jnp.where(diag, dot(p[rows, :].astype(BF), spread_b), 0.0).astype(BF)
    fill_broadcast(p, ROW_C, bb)
    i = lax.broadcasted_iota(jnp.int32, (32, 256), 0)
    j = lax.broadcasted_iota(jnp.int32, (32, 256), 1)
    sel[...] = jnp.where(i == jnp.where(i < N, j // N, N + j % N), 1.0, 0.0).astype(BF)
    dacc[...] = jnp.zeros(dacc.shape, F32)
    hs, gs, zz = (hse, hso), (g0, g1), (z0, z1)

    def load(k, i):
        slot = i % RING
        return pltpu.make_async_copy(hs_in.at[k, i], hs[k].at[slot], sem.at[k, slot])

    def scan(rev):
        rate = [
            -jnp.exp(st[ROW_DECAY : ROW_DECAY + N, c * 128 : c * 128 + 128]) * LOG2E
            for c in range(G6)
        ]
        block_diag = (
            lax.broadcasted_iota(jnp.int32, (N, 256), 0)
            == lax.broadcasted_iota(jnp.int32, (N, 256), 1) // N
        )

        def block_of(t):
            return NB - 1 - t if rev else t

        def drive_dot(t, k, c):
            rows = rows16(block_of(t))
            y = dot(bbd[rows, :], gs[k][:, c * 128 : c * 128 + 256])
            dd[c, rows, :] = y[:, :128]
            dd[c + 1, rows, :] = y[:, 128:]

        def step_dot(t, k, c, first):
            rows = rows16(block_of(t))
            y = dot(sel[...], zz[k][:, c * 128 : c * 128 + 256])
            zs[c, rows, :] = y[:N, :128]
            zs[c + 1, rows, :] = y[:N, 128:]
            dacc[c] += jnp.where(first, 0.0, y[N:, :128])
            dacc[c + 1] += jnp.where(first, 0.0, y[N:, 128:])

        def b_dot(t, k):
            rows = rows16(block_of(t))
            dbm[rows, :] = jnp.where(block_diag, dot_nt(ub[rows, :], gs[k][...]), 0.0).astype(BF)

        def c_dot(t, k, slot):
            rows = rows16(block_of(t))
            dcm[rows, :] = jnp.where(block_diag, dot_nt(dyb[rows, :], hs[k][slot]), 0.0).astype(BF)

        def block(t, k, slot, pslot, carry, late):
            b = block_of(t)
            carry = list(carry)
            late = list(late)
            for n, j in enumerate(range(16) if rev else range(15, -1, -1)):
                if n % 2 == 0 and late:
                    late.pop(0)()
                q = b * 16 + j
                cb = bb[pl.ds(pl.multiple_of(q * N, N), N), :]
                jp = j + 1 if rev else j - 1
                if 0 <= jp < 16:
                    old_ref, old_slot = hs[k], slot
                else:
                    jp = 0 if rev else 15
                    old_ref, old_slot = hs[1 - k], pslot
                for c in range(G6):
                    cols = slice(c * 128, c * 128 + 128)
                    w = dm[c, pl.ds(q, 1), :] * rate[c]
                    fade = jnp.exp2(w)
                    g = cb * dy[c, pl.ds(q, 1), :] + carry[c]
                    carry[c] = fade * g
                    old = old_ref[old_slot, jp * N : jp * N + N, cols]
                    gs[k][j * N : j * N + N, cols] = g.astype(BF)
                    zz[k][j * N : j * N + N, cols] = (w * carry[c]).astype(BF) * old
            return tuple(carry)

        def pair(ii, carry):
            i = NP - 1 - ii
            slot = i % RING
            pslot = jnp.maximum(i - 1, 0) % RING

            @pl.when(i >= 1)
            def _():
                load(0, i - 1).wait()
                load(1, i - 1).wait()

            @pl.when(i >= 3)
            def _():
                load(0, i - 3).start()
                load(1, i - 3).start()

            one = 1 + (i >> 20)
            for k in (1, 0):
                t = 2 * i + k
                after = jnp.minimum(t + 1, NB - 1)
                first = t + 1 > NB - 1
                late = [functools.partial(drive_dot, after, 1 - k, c) for c in (0, 2, 4)]
                late += [functools.partial(step_dot, after, 1 - k, c, first) for c in (0, 2, 4)]
                late += [functools.partial(b_dot, after, 1 - k), functools.partial(c_dot, t, k, slot)]
                ps = slot if k == 1 else pslot
                carry = lax.fori_loop(
                    0, one, lambda _, cc, t=t, k=k, ps=ps, late=late: block(t, k, slot, ps, cc, late), carry
                )
            return carry

        for i in range(NP - 1, NP - 4, -1):
            load(0, i).start()
            load(1, i).start()
        load(0, NP - 1).wait()
        load(1, NP - 1).wait()
        g0[...] = jnp.zeros((256, E), BF)
        z0[...] = jnp.zeros((256, E), BF)
        lax.fori_loop(0, NP, pair, tuple(jnp.zeros((N, 128), F32) for _ in range(G6)))
        for c in (0, 2, 4):
            drive_dot(0, 0, c)
            step_dot(0, 0, c, False)
        b_dot(0, 0)

    @pl.when(stream == 0)
    def _():
        scan(False)

    @pl.when(stream == 1)
    def _():
        scan(True)

    def step_tile(i, _):
        base = pl.multiple_of(i * 32, 32)
        rows = pl.ds(base, 32)
        for c in range(G6):
            cols = slice(c * 128, c * 128 + 128)
            delta, a, d = dl[c, rows, :], act[c, rows, :], dd[c, rows, :]
            near = 1.0 - delta * (0.5 - delta * (1.0 / 6.0 - delta * (1.0 / 24.0)))
            ratio = jnp.where(delta < 0.03, near, (1.0 - jnp.exp(-delta)) / delta)
            pre = ratio * (zs[c, rows, :] * LN2 + a * d * delta)
            ub[rows, cols] = pre.astype(BF)
            dm[c, rows, :] = delta * d + st[ROW_CHAN + 6 : ROW_CHAN + 7, cols] * dy[c, rows, :]
            sums[1, :, cols] += pre[0:8] + pre[8:16] + pre[16:24] + pre[24:32]
        return 0

    lax.fori_loop(0, R // 32, step_tile, 0)
    w_step = st[ROW_STEP : ROW_STEP + RANK, :].astype(BF)
    w_b = jnp.concatenate([st[ROW_B : ROW_B + N, :]] * N, 0).astype(BF)
    w_c = jnp.concatenate([st[ROW_C : ROW_C + N, :]] * N, 0).astype(BF)
    w_s = st[0:RANK, :].astype(BF)
    for h in range(2):
        rows = slice(h * 592, h * 592 + 592)
        sg = dot_nt(ub[rows, :], w_step).astype(BF)
        pgs[rows, :] = jnp.concatenate([sg, jnp.zeros((592, 128 - RANK), BF)], 1)
        for c in range(0, G6, 2):
            cols = slice(c * 128, c * 128 + 256)
            y = dot(sg, w_s[:, cols]) + dot(dbm[rows, :], w_b[:, cols]) + dot(dcm[rows, :], w_c[:, cols])
            dm[c, rows, :] += y[:, :128]
            dm[c + 1, rows, :] += y[:, 128:]
    dc[:, 0:HALO, :] = jnp.zeros((G6, HALO, 128), F32)
    dc[:, HALO + R : XR, :] = jnp.zeros((G6, HALO, 128), F32)

    def conv(rev):
        def first(i, _):
            base = pl.multiple_of(i * 32, 32)
            for c in range(G6):
                cols = slice(c * 128, c * 128 + 128)
                total, lagged = conv_tile(x, lab, st, c, base, 32, rev)
                sig = sigmoid(total)
                v = dm[c, pl.ds(base, 32), :] * sig * (1.0 + total * (1.0 - sig))
                dc[c, pl.ds(base + HALO, 32), :] = v
                sums[2, :, cols] += v[0:8] + v[8:16] + v[16:24] + v[24:32]
                for j in range(4):
                    t = v * lagged[j]
                    sums[3 + j, :, cols] += t[0:8] + t[8:16] + t[16:24] + t[24:32]
            return 0

        def second(i, _):
            base = pl.multiple_of(i * 32, 32)
            here = lab[pl.ds(base + HALO, 32), :]
            for c in range(G6):
                cols = slice(c * 128, c * 128 + 128)
                v = dc[c, pl.ds(base + HALO, 32), :] * st[ROW_CHAN : ROW_CHAN + 1, cols]
                for j in (1, 2, 3):
                    at = base + HALO + (-j if rev else j)
                    same = lab[pl.ds(at, 32), :] == here
                    later = jnp.where(same, dc[c, pl.ds(at, 32), :], 0.0)
                    v = v + later * st[ROW_CHAN + j : ROW_CHAN + j + 1, cols]
                dyb[pl.ds(base, 32), cols] = v.astype(BF)
            return 0

        lax.fori_loop(0, R // 32, first, 0)
        lax.fori_loop(0, R // 32, second, 0)

    @pl.when(stream == 0)
    def _():
        conv(False)

    @pl.when(stream == 1)
    def _():
        conv(True)

    for h in range(2):
        rows = slice(h * 592, h * 592 + 592)
        npart_o[rows, :] = dot_nt(dyb[rows, :], w1[...])
    for c in range(0, D, 128):
        gw1_o[c : c + 128, :] = dot_tn(normed[:, c : c + 128], dyb[...])
    top = dot_tn(pgs[...], al[...])
    gb = dot_tn(dbm[...], al[...])
    gc = dot_tn(dcm[...], al[...])
    gb = sum(gb[k * N : k * N + N] for k in range(N))
    gc = sum(gc[k * N : k * N + N] for k in range(N))
    low = p[0:R, :].astype(BF)
    gstep = dot_tn(low, ub[...])[0:RANK]
    gdecay = jnp.concatenate([dacc[c] for c in range(G6)], 1) * LN2

    def total(k):
        return jnp.sum(sums[k], axis=0, keepdims=True)

    chan = [total(3 + k) for k in range(4)] + [total(2), total(1), total(0)]
    chan = jnp.concatenate(chan + [jnp.zeros((1, E), F32)], 0)
    gt = jnp.concatenate(
        [top[0:RANK], gb, gc, gstep, gdecay, chan, jnp.zeros((128 - 104, E), F32)], 0
    )
    gs_o[...] = gt.T


def backward(meta, normed, x, act, al, dl, p, st, mgo, mgx, w1, hs):
    S = jax.ShapeDtypeStruct
    big = pltpu.VMEM((G6, R, 128), F32)
    return pl.pallas_call(
        bwd_kernel,
        out_shape=[S((R, D), F32), S((D, E), F32), S((E, 128), F32)],
        in_specs=[SMEM] + [VMEM] * 10 + [ANY],
        out_specs=[VMEM] * 3,
        scratch_shapes=[
            pltpu.VMEM((XR, 128), jnp.int32), big, big,
            pltpu.VMEM((R, E), BF), pltpu.VMEM((R, E), BF),
            pltpu.VMEM((1280 * N, 128), F32),
            pltpu.VMEM((R, 256), BF), pltpu.VMEM((R, 256), BF), pltpu.VMEM((R, 256), BF),
            big, big, pltpu.VMEM((G6, N, 128), F32), pltpu.VMEM((R, 128), BF),
            pltpu.VMEM((RING, 256, E), BF), pltpu.VMEM((RING, 256, E), BF),
            pltpu.VMEM((256, E), BF), pltpu.VMEM((256, E), BF),
            pltpu.VMEM((256, E), BF), pltpu.VMEM((256, E), BF),
            pltpu.VMEM((G6, XR, 128), F32), pltpu.VMEM((32, 256), BF),
            pltpu.VMEM((7, 8, E), F32),
            pltpu.SemaphoreType.DMA((2, RING)),
        ],
        compiler_params=pltpu.CompilerParams(vmem_limit_bytes=63 * 2**20),
        name="backward",
    )(meta, normed, x, act, al, dl, p, st, mgo, mgx, w1, hs)


def end_kernel(wide, meta, tok, etab, cot, npart, other, gpart, st, tg_o, gg_o, cotw, out, gain_s, acc):
    stream = meta[4]
    wbase = pl.multiple_of(stream * WBASE, 32)
    gain_s[...] = gain_row(st, wide)
    acc[...] = jnp.zeros(acc.shape, F32)
    cotw[...] = jnp.zeros(cotw.shape, F32)
    for s, off in ((0, 0), (1, WIN - HALF - 8)):

        @pl.when(stream == s)
        def _():
            cotw[off : off + HALF, :] = cot[...].astype(F32)

    lo = stream * HALF

    def tile(i, _):
        base = pl.multiple_of(i * 32, 32)
        at = pl.multiple_of(wbase + base, 32)
        res, _l = residual_tile(meta, tok[pl.ds(at, 32), :], etab, at, 32)
        scale = row_scale(res)
        r = at + lax.broadcasted_iota(jnp.int32, (32, 128), 0)
        mine = (r >= lo) & (r < lo + HALF)
        ng, un = [], []
        for c in range(3):
            cols = slice(c * 128, c * 128 + 128)
            v = npart[pl.ds(at, 32), cols] + other[pl.ds(base, 32), cols].astype(F32) + gpart[pl.ds(base, 32), cols]
            unit = res[c] * scale
            t = jnp.where(mine, v * unit, 0.0)
            acc[:, cols] += t[0:8] + t[8:16] + t[16:24] + t[24:32]
            ng.append(v * gain_s[0:1, cols])
            un.append(unit)
        mean = sum(jnp.sum(a * b, axis=1, keepdims=True) for a, b in zip(ng, un)) * (1.0 / D)
        for c in range(3):
            cols = slice(c * 128, c * 128 + 128)
            out[pl.ds(base, 32), cols] = cotw[pl.ds(base, 32), cols] + scale * (ng[c] - un[c] * mean)
        return 0

    lax.fori_loop(0, WIN // 32, tile, 0)
    gg_o[...] = acc[...]
    for s, off in ((0, 0), (1, WIN - HALF - 8)):

        @pl.when(stream == s)
        def _():
            tg_o[...] = out[off : off + HALF, :]


def ending(wide, meta, tok, etab, cot, npart, other, gpart, st):
    S = jax.ShapeDtypeStruct
    return pl.pallas_call(
        functools.partial(end_kernel, wide),
        out_shape=[S((HALF, D), F32), S((8, D), F32)],
        in_specs=[SMEM] + [VMEM] * 7,
        out_specs=[VMEM] * 2,
        scratch_shapes=[
            pltpu.VMEM((WIN, D), F32), pltpu.VMEM((WIN, D), F32), pltpu.VMEM((8, D), F32), pltpu.VMEM((8, D), F32),
        ],
        compiler_params=pltpu.CompilerParams(vmem_limit_bytes=60 * 2**20),
        name="ending",
    )(meta, tok, etab, cot, npart, other, gpart, st)


def adam_step(weight, gradient, first_moment, second, step_rate, decay_rate):
    first_moment = BETA_ONE * first_moment + (1.0 - BETA_ONE) * gradient
    second = BETA_TWO * second + (1.0 - BETA_TWO) * gradient * gradient
    first_hat = first_moment / (1.0 - BETA_ONE**STEP)
    second_hat = second / (1.0 - BETA_TWO**STEP)
    weight = weight - step_rate * (
        first_hat / (jnp.sqrt(second_hat) + EPS_ADAM) + decay_rate * weight
    )
    return (weight, first_moment, second)


def sum_at_owner(array, axis):
    n = lax.axis_size(axis)
    blocks = array.reshape(n, array.shape[0] // n, *array.shape[1:])
    arrived = lax.all_to_all(blocks, axis, split_axis=0, concat_axis=0, tiled=True)
    return arrived.astype(F32).sum(axis=0)


def swap(array):
    return lax.ppermute(array, "dir", [(0, 1), (1, 0)])


def local(
    tokens, cotangent, view_counts, view_strides, view_offsets,
    in_proj, in_first, in_second, out_proj, out_first, out_second,
    norm_gain, gain_first, gain_second, state_proj, state_first, state_second,
    step_proj, step_first, step_second, log_decay, decay_first, decay_second,
    channels, chan_first, chan_second,
):
    stream = lax.axis_index("dir")
    wide = lax.axis_size("wide")
    rows = state_proj.shape[1]
    own_gain = norm_gain.shape[0]
    gain_col = jnp.concatenate([norm_gain, jnp.zeros((rows - own_gain,), F32)])[:, None]
    small = jnp.concatenate(
        [
            state_proj[0], step_proj[0].T, log_decay[0].T, channels[0].T, gain_col,
            jnp.zeros((rows, 128 - ROW_GAIN - 1), F32),
        ],
        1,
    ).astype(BF)
    w_in = lax.all_gather(in_proj.astype(BF), "wide", axis=0, tiled=True)
    w_out = lax.all_gather(out_proj.astype(BF), "wide", axis=0, tiled=True)
    s = lax.all_gather(small, "wide", axis=0, tiled=True)
    w1, w2 = w_in[:, :E], w_in[:, E:]

    meta = jnp.concatenate(
        [view_counts, view_offsets[0], stream[None].astype(jnp.int32), jnp.zeros((3,), jnp.int32)]
    )
    half = D // 2
    freq = jnp.exp(-math.log(10000.0) * jnp.arange(half, dtype=F32) / half)
    angles = view_strides[0].astype(F32)[:, None] * freq[None, :]
    etab = jnp.concatenate([jnp.sin(angles), jnp.cos(angles)], 1)
    rest = jnp.concatenate([jnp.zeros((1, half), F32), jnp.ones((1, half), F32)], 1)
    etab = jnp.concatenate([etab, rest, jnp.zeros((4, D), F32)], 0)
    tok = jnp.pad(tokens[0], ((0, R - SLOTS), (0, 0)))
    cot = cotangent[0]

    normed, x, act, al, dl, p, st, res, stats, hs = forward(wide, meta, tok, etab, w1, s)
    mine = lax.dynamic_slice_in_dim(res, stream * WBASE, WIN, 0)
    other = swap(lax.dynamic_slice_in_dim(res, (1 - stream) * WBASE, WIN, 0))
    block, mg, gpart, gw2, gwo = middle(meta, tok, etab, cot, normed, mine, other, w2, w_out)
    mgx = swap(mg)
    mg0 = jnp.where(stream == 0, mg, mgx)
    mg1 = jnp.where(stream == 0, mgx, mg)
    npart, gw1, gs = backward(meta, normed, x, act, al, dl, p, st, mg0, mg1, w1, hs)
    other = swap(lax.dynamic_slice_in_dim(npart, (1 - stream) * WBASE, WIN, 0).astype(BF))
    token_grad, gg = ending(wide, meta, tok, etab, cot, npart, other, gpart, st)

    gin = jnp.concatenate([gw1, gw2], 1)
    gin, gwo, gg = (
        lax.psum(gin.astype(BF), "dir"),
        lax.psum(gwo.astype(BF), "dir"),
        lax.psum(gg.sum(0).astype(BF), "dir"),
    )
    shard_in = sum_at_owner(gin, "wide")
    shard_out = sum_at_owner(gwo, "wide")
    shard_gain = sum_at_owner(gg, "wide")
    shard_small = sum_at_owner(gs.astype(BF), "wide")
    small_t = shard_small.T
    stats = stats.sum(1) / VIEW_TOK
    stats = sum_at_owner(stats.T, "wide").T

    outs = []
    for w, g, f, s2, k in (
        (in_proj, shard_in, in_first, in_second, 0),
        (out_proj, shard_out, out_first, out_second, 1),
        (norm_gain, shard_gain, gain_first, gain_second, 2),
        (state_proj, shard_small[None, :, : ROW_STEP], state_first, state_second, 3),
        (step_proj, small_t[None, ROW_STEP:ROW_DECAY], step_first, step_second, 4),
        (log_decay, small_t[None, ROW_DECAY:ROW_CHAN], decay_first, decay_second, 5),
        (channels, small_t[None, ROW_CHAN:ROW_GAIN], chan_first, chan_second, 6),
    ):
        outs += adam_step(w, g, f, s2, RATES[k], DECAYS[k])
    return (block[None], token_grad[None], stats[None], *outs)


def solution(mesh):
    row, col = P("wide", None), P("dir", None, "wide")
    mat = P("dir", "wide", None)
    weights = [row] * 6 + [P("wide")] * 3 + [mat] * 3 + [col] * 9
    return jax.shard_map(
        local,
        mesh=mesh,
        in_specs=(
            P("wide", None, None), P("wide", "dir", None), P("wide"), row, row, *weights,
        ),
        out_specs=(P("wide", "dir", None), P("wide", "dir", None), col, *weights),
        check_vma=False,
    )
```

```python
import functools
import math

import jax
import jax.numpy as jnp
from jax import lax
from jax.experimental import pallas as pl
from jax.experimental.pallas import tpu as pltpu
from jax.sharding import PartitionSpec as P

PATCHES = 196
STEP = 10
VIEW_TOK = 392
EPS_NORM = 1e-06
BETA_ONE = 0.9
BETA_TWO = 0.95
EPS_ADAM = 1e-08
RATES = (0.15, 0.1, 2.5, 0.12, 0.2, 1.0, 2.5)
DECAYS = (0.1, 0.1, 0.0, 0.1, 0.1, 0.0, 0.0)

F32 = jnp.float32
BF = jnp.bfloat16
LN2 = math.log(2.0)
LOG2E = 1.0 / LN2

SLOTS = 1176
R = 1184
NB = R // 16
NP = NB // 2
HALF = 588
WIN = 608
WBASE = 576
D = 384
E = 768
G6 = E // 128
N = 16
RANK = 24
HALO = 8
XR = HALO + R + HALO
RING = 4
CUT = 1e4
SENDS = WIN // 32
MESH = pl.DeviceIdType.MESH
ROW_B, ROW_C, ROW_STEP, ROW_DECAY, ROW_CHAN, ROW_GAIN, ROW_STATS = 24, 40, 56, 80, 96, 103, 104
NT = (((1,), (1,)), ((), ()))
TN = (((0,), (0,)), ((), ()))
VMEM = pl.BlockSpec(memory_space=pltpu.VMEM)
SMEM = pl.BlockSpec(memory_space=pltpu.SMEM)
ANY = pl.BlockSpec(memory_space=pl.ANY)


def dot(a, b):
    return jnp.dot(a, b, preferred_element_type=F32)


def dot_nt(a, b):
    return lax.dot_general(a, b, NT, preferred_element_type=F32)


def dot_tn(a, b):
    return lax.dot_general(a, b, TN, preferred_element_type=F32)


def sigmoid(v):
    return 0.5 * jnp.tanh(0.5 * v) + 0.5


def rows16(b, n=16):
    return pl.ds(pl.multiple_of(b * 16, 16), n)


def labels_of(meta, r):
    lab = jnp.full(r.shape, -1, jnp.int32)
    late = jnp.zeros(r.shape, jnp.int32)
    for k in range(3):
        start = meta[1 + k]
        inside = (r >= start) & (r < start + VIEW_TOK) & (k < meta[0])
        lab = jnp.where(inside, k, lab)
        late = jnp.where(inside, jnp.where(r >= start + PATCHES, 1, 0), late)
    lab = jnp.where(r < 0, -2, lab)
    lab = jnp.where(r >= SLOTS, -3, lab)
    return lab, late


def residual_tile(meta, tok, etab, base, n):
    r = base + lax.broadcasted_iota(jnp.int32, (n, 128), 0)
    lab, late = labels_of(meta, r)
    live = jnp.where(lab >= 0, 1.0, 0.0)
    out = []
    for c in range(3):
        cols = slice(c * 128, c * 128 + 128)
        emb = jnp.where(lab >= 0, etab[3:4, cols], 0.0)
        for k in range(3):
            emb = jnp.where((lab == k) & (late == 1), etab[k : k + 1, cols], emb)
        out.append(tok[c, pl.ds(base, n), :] + emb)
    return out, live


def lay_tokens(tok, tokf):
    for c in range(3):
        tokf[c, 0:SLOTS, :] = tok[:, c * 128 : c * 128 + 128].astype(F32)
        tokf[c, SLOTS:R, :] = jnp.zeros((R - SLOTS, 128), F32)


def row_scale(res):
    total = sum(jnp.sum(v * v, axis=1, keepdims=True) for v in res)
    return lax.rsqrt(total * (1.0 / D) + EPS_NORM)


def fill_labels(meta, lab_ref):
    for base in range(0, XR, 8):
        r = base - HALO + lax.broadcasted_iota(jnp.int32, (8, 128), 0)
        lab_ref[base : base + 8, :] = labels_of(meta, r)[0]


def gain_row(st_ref, wide):
    per = E // wide
    own = D // wide
    i = lax.broadcasted_iota(jnp.int32, (E, D), 0)
    j = lax.broadcasted_iota(jnp.int32, (E, D), 1)
    pick = jnp.where(i == (j // own) * per + j % own, 1.0, 0.0).astype(BF)
    src = jnp.broadcast_to(st_ref[ROW_GAIN : ROW_GAIN + 1, :], (16, E)).astype(BF)
    return dot(src, pick)[0:8]


def fill_broadcast(p_ref, lane, out_ref):
    def spread(base, n):
        v = p_ref[pl.ds(base, 128), :].T[lane : lane + N]
        for j in range(n):
            out_ref[pl.ds(pl.multiple_of((base + j) * N, N), N), :] = (
                jnp.broadcast_to(v[:, j : j + 1], (N, 128))
            )

    def body(sb, _):
        spread(pl.multiple_of(sb * 128, 128), 128)
        return 0

    lax.fori_loop(0, R // 128, body, 0)
    spread(R // 128 * 128, R % 128)


def conv_tile(x_ref, lab_ref, st_ref, c, base, n, rev):
    cols = slice(c * 128, c * 128 + 128)
    here = lab_ref[pl.ds(base + HALO, n), :]
    lagged = [x_ref[c, pl.ds(base + HALO, n), :]]
    for j in (1, 2, 3):
        at = base + HALO + (j if rev else -j)
        same = lab_ref[pl.ds(at, n), :] == here
        lagged.append(jnp.where(same, x_ref[c, pl.ds(at, n), :], 0.0))
    total = st_ref[ROW_CHAN + 4 : ROW_CHAN + 5, cols]
    for j in range(4):
        total = total + st_ref[ROW_CHAN + j : ROW_CHAN + j + 1, cols] * lagged[j]
    return total, lagged


def views(count, offset, stream):
    return [count[0], offset[0, 0], offset[0, 1], offset[0, 2], stream]


def fill_embedding(stride, etab):
    lane = lax.broadcasted_iota(jnp.int32, (8, D), 1)
    row = lax.broadcasted_iota(jnp.int32, (8, D), 0)
    half = D // 2
    j = jnp.where(lane < half, lane, lane - half).astype(F32)
    freq = jnp.exp(-math.log(10000.0) * j / half)
    clock = jnp.zeros((8, D), F32)
    for k in range(3):
        clock = jnp.where(row == k, stride[0, k].astype(F32), clock)
    angle = clock * freq
    etab[...] = jnp.where(lane < half, jnp.sin(angle), jnp.cos(angle))


def fwd_kernel(
    wide, count, offset, stride, tok, w1, s_ref,
    normed_h, x_h, act_h, dl_h, p_h, st_h, res_h, other_h, stats_o, hs_o,
    normed_o, x_o, act_o, dl_o, p_o, st_o, res_o, other_o, al_o,
    lab, dm, u, bb, cbd, hse, hso, gain_s, tokf, etab, sem, out_sem, send, recv,
):
    stream, place = lax.axis_index("dir"), lax.axis_index("wide")
    bar = pltpu.get_barrier_semaphore()
    pl.semaphore_signal(bar, inc=1, device_id=(1 - stream, place), device_id_type=MESH)
    meta = views(count, offset, stream)
    fill_embedding(stride, etab)
    lay_tokens(tok, tokf)
    st_o[...] = s_ref[...].astype(F32).T
    fill_labels(meta, lab)
    gain_s[...] = gain_row(st_o, wide)
    saves = [
        pltpu.make_async_copy(v, h, out_sem.at[k])
        for k, (v, h) in enumerate(
            zip(
                (normed_o, x_o, act_o, dl_o, p_o, st_o, res_o, other_o),
                (normed_h, x_h, act_h, dl_h, p_h, st_h, res_h, other_h),
            )
        )
    ]

    def norm_tile(i, _):
        base = pl.multiple_of(i * 32, 32)
        res, _l = residual_tile(meta, tokf, etab, base, 32)
        scale = row_scale(res)
        for c in range(3):
            cols = slice(c * 128, c * 128 + 128)
            normed_o[pl.ds(base, 32), cols] = (res[c] * scale * gain_s[0:1, cols]).astype(BF)
        return 0

    lax.fori_loop(0, R // 32, norm_tile, 0)
    x_o[:, 0:HALO, :] = jnp.zeros((G6, HALO, 128), F32)
    x_o[:, HALO + R : XR, :] = jnp.zeros((G6, HALO, 128), F32)
    for h in range(2):
        for c in range(0, G6, 2):
            y = dot(normed_o[h * 592 : h * 592 + 592, :], w1[:, c * 128 : c * 128 + 256])
            x_o[c, HALO + h * 592 : HALO + h * 592 + 592, :] = y[:, :128]
            x_o[c + 1, HALO + h * 592 : HALO + h * 592 + 592, :] = y[:, 128:]

    def conv(rev):
        def tile(i, _):
            base = pl.multiple_of(i * 32, 32)
            for c in range(G6):
                total, _l = conv_tile(x_o, lab, st_o, c, base, 32, rev)
                act = total * sigmoid(total)
                act_o[c, pl.ds(base, 32), :] = act
                al_o[pl.ds(base, 32), c * 128 : c * 128 + 128] = act.astype(BF)
            return 0

        lax.fori_loop(0, R // 32, tile, 0)

    @pl.when(stream == 0)
    def _():
        conv(False)

    @pl.when(stream == 1)
    def _():
        conv(True)

    p_o[R:, :] = jnp.zeros((1280 - R, 128), F32)
    col = lax.broadcasted_iota(jnp.int32, (128, 256), 1)
    row = lax.broadcasted_iota(jnp.int32, (128, 256), 0)
    spread_c = jnp.where(row == ROW_C + col % N, 1.0, 0.0).astype(BF)
    diag = (
        lax.broadcasted_iota(jnp.int32, (592, 256), 0) % N
        == lax.broadcasted_iota(jnp.int32, (592, 256), 1) // N
    )
    for h in range(2):
        rows = slice(h * 592, h * 592 + 592)
        proj = dot(al_o[rows, :], s_ref[...])
        p_o[rows, :] = proj
        low = proj.astype(BF)
        cbd[rows, :] = jnp.where(diag, dot(low, spread_c), 0.0).astype(BF)
        step_in = low[:, :RANK]
        for c in range(0, G6, 2):
            w = st_o[ROW_STEP : ROW_STEP + RANK, c * 128 : c * 128 + 256].astype(BF)
            y = dot(step_in, w)
            dl_o[c, rows, :] = y[:, :128]
            dl_o[c + 1, rows, :] = y[:, 128:]
    stats_o[...] = jnp.zeros(stats_o.shape, F32)

    def soft(rev):
        def tile(i, _):
            base = pl.multiple_of(i * 32, 32)
            here = lab[pl.ds(base + HALO, 32), :]
            before = lab[pl.ds(base + HALO + (1 if rev else -1), 32), :]
            cut = jnp.where(here == before, 0.0, CUT)
            live = jnp.where(here >= 0, 1.0, 0.0)
            real = jnp.where(here >= -1, 1.0, 0.0)
            for c in range(G6):
                cols = slice(c * 128, c * 128 + 128)
                rows = pl.ds(base, 32)
                v = dl_o[c, rows, :] + st_o[ROW_CHAN + 5 : ROW_CHAN + 6, cols]
                delta = jnp.maximum(v, 0.0) + jnp.log1p(jnp.exp(-jnp.abs(v)))
                dl_o[c, rows, :] = delta
                dm[c, rows, :] = delta + cut
                u[c, rows, :] = delta * act_o[c, rows, :] * real
                t1 = live * delta
                t2 = t1 * delta
                for s in range(4):
                    stats_o[0, :, cols] += t1[8 * s : 8 * s + 8]
                    stats_o[1, :, cols] += t2[8 * s : 8 * s + 8]
            return 0

        lax.fori_loop(0, R // 32, tile, 0)

    @pl.when(stream == 0)
    def _():
        soft(False)

    @pl.when(stream == 1)
    def _():
        soft(True)

    for c in saves[:6]:
        c.start()
    fill_broadcast(p_o, ROW_B, bb)
    hs = (hse, hso)

    def save(k, i):
        slot = i % RING
        return pltpu.make_async_copy(hs[k].at[slot], hs_o.at[k, i], sem.at[k, slot])

    def give(i, rev):
        row = pl.multiple_of((NP - 1 - i if rev else i) * 32, 32)
        at = pl.multiple_of(row if rev else row - WBASE, 32)
        k = i - (NP - SENDS)
        return pltpu.make_async_remote_copy(
            src_ref=res_o.at[pl.ds(row, 32), :], dst_ref=other_o.at[pl.ds(at, 32), :],
            send_sem=send.at[k], recv_sem=recv.at[k], device_id=(1 - stream, place), device_id_type=MESH,
        )

    def scan(rev):
        rate = [
            -jnp.exp(st_o[ROW_DECAY : ROW_DECAY + N, c * 128 : c * 128 + 128]) * LOG2E
            for c in range(G6)
        ]

        def block_of(t):
            return NB - 1 - t if rev else t

        def emit(t, k, slot, c):
            rows = rows16(block_of(t))
            y = dot(cbd[rows, :], hs[k][slot, :, c * 128 : c * 128 + 256])
            for h in range(2):
                cols = slice((c + h) * 128, (c + h) * 128 + 128)
                skip = st_o[ROW_CHAN + 6 : ROW_CHAN + 7, cols]
                res_o[rows, cols] = (
                    y[:, h * 128 : h * 128 + 128] + skip * act_o[c + h, rows, :]
                ).astype(BF)

        def block(t, k, slot, state, late):
            b = block_of(t)
            state = list(state)
            for n, j in enumerate(range(15, -1, -1) if rev else range(16)):
                if n % 4 == 0 and late:
                    late.pop(0)()
                q = b * 16 + j
                drive = bb[pl.ds(pl.multiple_of(q * N, N), N), :]
                for c in range(G6):
                    fade = jnp.exp2(dm[c, pl.ds(q, 1), :] * rate[c])
                    state[c] = fade * state[c] + u[c, pl.ds(q, 1), :] * drive
                    hs[k][slot, j * N : j * N + N, c * 128 : c * 128 + 128] = state[c].astype(BF)
            return tuple(state)

        def pair(i, state):
            slot = i % RING

            @pl.when(i >= RING)
            def _():
                save(0, i - RING).wait()
                save(1, i - RING).wait()

            before = jnp.maximum(2 * i - 1, 0)
            late = [
                functools.partial(emit, before, 1, jnp.maximum(i - 1, 0) % RING, c)
                for c in (0, 2, 4)
            ]
            state = block(2 * i, 0, slot, state, late)
            late = [functools.partial(emit, 2 * i, 0, slot, c) for c in (0, 2, 4)]
            state = block(2 * i + 1, 1, slot, state, late)
            save(0, i).start()
            save(1, i).start()

            @pl.when(i > NP - SENDS)
            def _():
                give(i - 1, rev).start()

            return state

        hso[0] = jnp.zeros((256, E), BF)
        lax.fori_loop(0, NP, pair, tuple(jnp.zeros((N, 128), F32) for _ in range(G6)))
        for c in (0, 2, 4):
            emit(NB - 1, 1, (NP - 1) % RING, c)
        give(NP - 1, rev).start()
        for i in range(NP - RING, NP):
            save(0, i).wait()
            save(1, i).wait()

        def settle(i, _):
            give(i, rev).wait()
            return 0

        lax.fori_loop(NP - SENDS, NP, settle, 0)

    pl.semaphore_wait(bar, 1)

    @pl.when(stream == 0)
    def _():
        scan(False)

    @pl.when(stream == 1)
    def _():
        scan(True)

    for c in saves[6:]:
        c.start()
    for c in saves:
        c.wait()


def forward(wide, count, offset, stride, tok, w1, s):
    S = jax.ShapeDtypeStruct
    kept = [
        ((R, D), BF), ((G6, XR, 128), F32), ((G6, R, 128), F32), ((G6, R, 128), F32),
        ((1280, 128), F32), ((128, E), F32), ((R, E), BF), ((WIN, E), BF),
    ]
    return pl.pallas_call(
        functools.partial(fwd_kernel, wide),
        out_shape=[S(*k) for k in kept] + [S((2, 8, E), F32), S((2, NP, 256, E), BF)],
        in_specs=[SMEM] * 3 + [VMEM] * 3,
        out_specs=[ANY] * 8 + [VMEM, ANY],
        scratch_shapes=[pltpu.VMEM(*k) for k in kept]
        + [
            pltpu.VMEM((R, E), BF),
            pltpu.VMEM((XR, 128), jnp.int32),
            pltpu.VMEM((G6, R, 128), F32),
            pltpu.VMEM((G6, R, 128), F32),
            pltpu.VMEM((R * N, 128), F32),
            pltpu.VMEM((R, 256), BF),
            pltpu.VMEM((RING, 256, E), BF),
            pltpu.VMEM((RING, 256, E), BF),
            pltpu.VMEM((8, D), F32),
            pltpu.VMEM((3, R, 128), F32),
            pltpu.VMEM((8, D), F32),
            pltpu.SemaphoreType.DMA((2, RING)),
            pltpu.SemaphoreType.DMA((8,)),
            pltpu.SemaphoreType.DMA((SENDS,)),
            pltpu.SemaphoreType.DMA((SENDS,)),
        ],
        compiler_params=pltpu.CompilerParams(
            vmem_limit_bytes=60 * 2**20, collective_id=3, has_side_effects=True
        ),
        cost_estimate=pl.CostEstimate(flops=int(5e10), bytes_accessed=1 << 20, transcendentals=0),
        name="forward",
    )(count, offset, stride, tok, w1, s)


def middle(meta, wide, tokf, etab, cot, normed, own, other, w2, wo, cotw, gated, bgrad, ggrad, blk, mg, gpart, stage, g2, block_o, sent, shared):
    stream = meta[4]
    wbase = pl.multiple_of(stream * WBASE, 32)
    lay_cotangent(stream, cot, cotw)
    win = pl.ds(wbase, WIN)

    def tile(i, _):
        base = pl.multiple_of(i * 32, 32)
        r = wbase + base + lax.broadcasted_iota(jnp.int32, (32, 128), 0)
        live = jnp.where(labels_of(meta, r)[0] >= 0, 1.0, 0.0)
        for c in range(3):
            v = live * cotw[c, pl.ds(base, 32), :]
            ref, col = (bgrad[0], c * 128) if c < 2 else (bgrad[1], 0)
            ref[pl.ds(base, 32), col : col + 128] = v.astype(BF)
        return 0

    lax.fori_loop(0, WIN // 32, tile, 0)

    def branch_grad():
        return jnp.concatenate([bgrad[0][0:WIN, :], bgrad[1][0:WIN, 0:128]], 1)

    for c in range(0, E, 256):
        cols = slice(c, c + 256)
        gate = dot(normed[win, :], w2[:, cols])
        mixed = own[:, cols].astype(F32) + other[:, cols].astype(F32)
        sig = sigmoid(gate)
        silu = gate * sig
        gated[0:WIN, cols] = (mixed * silu).astype(BF)
        up = dot_nt(branch_grad(), wo[cols, :])
        mg[:, cols] = (up * silu).astype(BF)
        ggrad[0:WIN, cols] = (up * mixed * sig * (1.0 + gate * (1.0 - sig))).astype(BF)
        sent(c // 256).start()
    drow, erow = D // wide, E // wide
    rows = 2 * drow
    pitch = -(-rows // 8) * 8
    for c in range(0, D, 128):
        g = dot_tn(normed[win, c : c + 128], ggrad[0:WIN, :])
        lay_rows(g, c, drow, lambda k, r, v: put(stage, pitch, k, r, 0, v))
    for c in range(0, E, 256):
        g = dot_tn(gated[0:WIN, c : c + 256], branch_grad())
        half = erow // 2
        lay_rows(g, c, half, lambda k, r, v: put(stage, pitch, k // 2, drow + r, (k % 2) * D, v))
    for k in range(wide):
        for c in range(G6):
            at = (k * G6 + c) * pitch
            g2[k, :, c * 128 : c * 128 + 128] = stage[at : at + rows, :].astype(BF)
    shared()
    for c in range(0, D, 128):
        cols = slice(c, c + 128)
        blk[c // 128, 0:WIN, :] = dot(gated[0:WIN, :], wo[:, cols])
        gpart[:, cols] = dot_nt(ggrad[0:WIN, :], w2[cols, :])

    def out_tile(i, _):
        base = pl.multiple_of(i * 32, 32)
        at = pl.multiple_of(wbase + base, 32)
        res, live = residual_tile(meta, tokf, etab, at, 32)
        for c in range(3):
            blk[c, pl.ds(base, 32), :] = res[c] + live * blk[c, pl.ds(base, 32), :]
        return 0

    lax.fori_loop(0, WIN // 32, out_tile, 0)
    take_half(stream, blk, block_o)


WINDOWS = ((0, 0), (1, WIN - HALF - 8))


def lay_cotangent(stream, cot, cotw):
    cotw[:, 0:WIN, :] = jnp.zeros((3, WIN, 128), F32)
    for s, off in WINDOWS:

        @pl.when(stream == s)
        def _():
            for c in range(3):
                cotw[c, off : off + HALF, :] = cot[:, c * 128 : c * 128 + 128].astype(F32)


def take_half(stream, src, out):
    for s, off in WINDOWS:

        @pl.when(stream == s)
        def _():
            for c in range(3):
                out[:, c * 128 : c * 128 + 128] = src[c, off : off + HALF, :]


def put(ref, pitch, k, r, col, v):
    for c in range(0, v.shape[1], 128):
        at = (k * G6 + (col + c) // 128) * pitch + r
        ref[at : at + v.shape[0], :] = v[:, c : c + 128]


def lay_rows(v, start, size, store):
    at = 0
    while at < v.shape[0]:
        k, r = divmod(start + at, size)
        n = min(size - r, v.shape[0] - at)
        store(k, r, v[at : at + n])
        at += n


def unpack(pack, w2, wo, wide):
    drow, half = D // wide, E // wide // 2
    per = max(1, 16 // math.gcd(16, drow))
    for k in range(0, wide, per):
        v = [pack[k + i].astype(F32) for i in range(per)]
        w2[k * drow : (k + per) * drow, :] = jnp.concatenate([t[0:drow] for t in v], 0).astype(BF)
        pieces = []
        for t in v:
            pieces += [t[drow : drow + half, 0:D], t[drow : drow + half, D : 2 * D]]
        wo[2 * k * half : 2 * (k + per) * half, :] = jnp.concatenate(pieces, 0).astype(BF)


def bwd_kernel(
    wide, count, offset, stride, tok, cot, normed, own, other, pack, stats, w1, st,
    x_h, act_h, dl_h, p_h, hs_in,
    block_o, tg_o, gw1_o, gs_o, gg_o, g2_o, g2x_o,
    x, act, dl, p, w2, wo, gpart, mg, mgx, g2s, g2r, nrecv,
    lab, dm, dy, dyb, ub, bb, bbd, dbm, dcm, dd, zs, dacc, hse, hso, g0, g1, z0, z1, sel, sums,
    etab, gain_s, acc, sem, in_sem, mgsend, mgrecv, g2send, g2recv, swsend, swrecv,
):
    stream, place = lax.axis_index("dir"), lax.axis_index("wide")
    loads = [
        pltpu.make_async_copy(h, v, in_sem.at[k])
        for k, (h, v) in enumerate(zip((x_h, act_h, dl_h, p_h), (x, act, dl, p)))
    ]
    for c in loads:
        c.start()
    greet(stream, place, wide)
    meta = views(count, offset, stream)
    wbase = pl.multiple_of(stream * WBASE, 32)
    partner = dict(device_id=(1 - stream, place), device_id_type=MESH)
    fill_embedding(stride, etab)
    fill_labels(meta, lab)
    tokf, cotw, blk = zs.at[0:3], zs.at[3:6], dd.at[0:3]
    lay_tokens(tok, tokf)
    unpack(pack, w2, wo, wide)

    def sent(k):
        cols = slice(k * 256, k * 256 + 256)
        return pltpu.make_async_remote_copy(
            src_ref=mg.at[:, cols], dst_ref=mgx.at[:, cols], send_sem=mgsend.at[k], recv_sem=mgrecv.at[k], **partner
        )

    g2 = [
        pltpu.make_async_remote_copy(
            src_ref=g2s.at[place ^ k], dst_ref=g2r.at[k], send_sem=g2send.at[k], recv_sem=g2recv.at[k],
            device_id=(stream, place ^ k), device_id_type=MESH,
        )
        for k in range(1, wide)
    ]

    def shared():
        for c in g2:
            c.start()

    middle(
        meta, wide, tokf, etab, cot, normed, own, other, w2, wo, cotw, ub, (dbm, dcm), dyb, blk, mg, gpart, bb, g2s,
        block_o, sent, shared,
    )
    for k in range(3):
        sent(k).wait()
    for c in loads:
        c.wait()

    for s, lowref, highref in ((0, mg, mgx), (1, mgx, mg)):

        @pl.when(stream == s)
        def _():
            def lay(i, _):
                base = pl.multiple_of(i * 32, 32)
                lowat = pl.multiple_of(jnp.minimum(base, WIN - 32), 32)
                highat = pl.multiple_of(jnp.maximum(base - WBASE, 0), 32)
                for c in range(G6):
                    cols = slice(c * 128, c * 128 + 128)
                    lowrow = lowref[pl.ds(lowat, 32), cols].astype(F32)
                    highrow = highref[pl.ds(highat, 32), cols].astype(F32)
                    v = jnp.where(base < WIN, lowrow, 0.0) + jnp.where(base >= WBASE, highrow, 0.0)
                    dy[c, pl.ds(base, 32), :] = v
                    dyb[pl.ds(base, 32), cols] = v.astype(BF)
                return 0

            lax.fori_loop(0, R // 32, lay, 0)

    sums[...] = jnp.zeros(sums.shape, F32)

    def prep(rev):
        def tile(i, _):
            base = pl.multiple_of(i * 32, 32)
            rows = pl.ds(base, 32)
            here = lab[pl.ds(base + HALO, 32), :]
            before = lab[pl.ds(base + HALO + (1 if rev else -1), 32), :]
            cut = jnp.where(here == before, 0.0, CUT)
            real = jnp.where(here >= -1, 1.0, 0.0)
            for c in range(G6):
                cols = slice(c * 128, c * 128 + 128)
                dm[c, rows, :] = dl[c, rows, :] + cut
                a = act[c, rows, :]
                ub[rows, cols] = (dl[c, rows, :] * a * real).astype(BF)
                t = dy[c, rows, :] * a
                sums[0, :, cols] += t[0:8] + t[8:16] + t[16:24] + t[24:32]
            return 0

        lax.fori_loop(0, R // 32, tile, 0)

    @pl.when(stream == 0)
    def _():
        prep(False)

    @pl.when(stream == 1)
    def _():
        prep(True)

    col = lax.broadcasted_iota(jnp.int32, (128, 256), 1)
    row = lax.broadcasted_iota(jnp.int32, (128, 256), 0)
    spread_b = jnp.where(row == ROW_B + col % N, 1.0, 0.0).astype(BF)
    diag = (
        lax.broadcasted_iota(jnp.int32, (592, 256), 0) % N
        == lax.broadcasted_iota(jnp.int32, (592, 256), 1) // N
    )
    for h in range(2):
        rows = slice(h * 592, h * 592 + 592)
        bbd[rows, :] = jnp.where(diag, dot(p[rows, :].astype(BF), spread_b), 0.0).astype(BF)
    fill_broadcast(p, ROW_C, bb)
    i = lax.broadcasted_iota(jnp.int32, (32, 256), 0)
    j = lax.broadcasted_iota(jnp.int32, (32, 256), 1)
    sel[...] = jnp.where(i == jnp.where(i < N, j // N, N + j % N), 1.0, 0.0).astype(BF)
    dacc[...] = jnp.zeros(dacc.shape, F32)
    hs, gs, zz = (hse, hso), (g0, g1), (z0, z1)

    def load(k, i):
        slot = i % RING
        return pltpu.make_async_copy(hs_in.at[k, i], hs[k].at[slot], sem.at[k, slot])

    def scan(rev):
        rate = [
            -jnp.exp(st[ROW_DECAY : ROW_DECAY + N, c * 128 : c * 128 + 128]) * LOG2E
            for c in range(G6)
        ]
        block_diag = (
            lax.broadcasted_iota(jnp.int32, (N, 256), 0)
            == lax.broadcasted_iota(jnp.int32, (N, 256), 1) // N
        )

        def block_of(t):
            return NB - 1 - t if rev else t

        def drive_dot(t, k, c):
            rows = rows16(block_of(t))
            y = dot(bbd[rows, :], gs[k][:, c * 128 : c * 128 + 256])
            dd[c, rows, :] = y[:, :128]
            dd[c + 1, rows, :] = y[:, 128:]

        def step_dot(t, k, c, first):
            rows = rows16(block_of(t))
            y = dot(sel[...], zz[k][:, c * 128 : c * 128 + 256])
            zs[c, rows, :] = y[:N, :128]
            zs[c + 1, rows, :] = y[:N, 128:]
            dacc[c] += jnp.where(first, 0.0, y[N:, :128])
            dacc[c + 1] += jnp.where(first, 0.0, y[N:, 128:])

        def b_dot(t, k):
            rows = rows16(block_of(t))
            dbm[rows, :] = jnp.where(block_diag, dot_nt(ub[rows, :], gs[k][...]), 0.0).astype(BF)

        def c_dot(t, k, slot):
            rows = rows16(block_of(t))
            dcm[rows, :] = jnp.where(block_diag, dot_nt(dyb[rows, :], hs[k][slot]), 0.0).astype(BF)

        def block(t, k, slot, pslot, carry, late):
            b = block_of(t)
            carry = list(carry)
            late = list(late)
            for n, j in enumerate(range(16) if rev else range(15, -1, -1)):
                if n % 2 == 0 and late:
                    late.pop(0)()
                q = b * 16 + j
                cb = bb[pl.ds(pl.multiple_of(q * N, N), N), :]
                jp = j + 1 if rev else j - 1
                if 0 <= jp < 16:
                    old_ref, old_slot = hs[k], slot
                else:
                    jp = 0 if rev else 15
                    old_ref, old_slot = hs[1 - k], pslot
                for c in range(G6):
                    cols = slice(c * 128, c * 128 + 128)
                    w = dm[c, pl.ds(q, 1), :] * rate[c]
                    fade = jnp.exp2(w)
                    g = cb * dy[c, pl.ds(q, 1), :] + carry[c]
                    carry[c] = fade * g
                    old = old_ref[old_slot, jp * N : jp * N + N, cols]
                    gs[k][j * N : j * N + N, cols] = g.astype(BF)
                    zz[k][j * N : j * N + N, cols] = (w * carry[c]).astype(BF) * old
            return tuple(carry)

        def pair(ii, carry):
            i = NP - 1 - ii
            slot = i % RING
            pslot = jnp.maximum(i - 1, 0) % RING

            @pl.when(i >= 1)
            def _():
                load(0, i - 1).wait()
                load(1, i - 1).wait()

            @pl.when(i >= 3)
            def _():
                load(0, i - 3).start()
                load(1, i - 3).start()

            one = 1 + i // 1048576
            for k in (1, 0):
                t = 2 * i + k
                after = jnp.minimum(t + 1, NB - 1)
                first = t + 1 > NB - 1
                late = [functools.partial(drive_dot, after, 1 - k, c) for c in (0, 2, 4)]
                late += [functools.partial(step_dot, after, 1 - k, c, first) for c in (0, 2, 4)]
                late += [functools.partial(b_dot, after, 1 - k), functools.partial(c_dot, t, k, slot)]
                ps = slot if k == 1 else pslot
                carry = lax.fori_loop(
                    0, one, lambda _, cc, t=t, k=k, ps=ps, late=late: block(t, k, slot, ps, cc, late), carry
                )
            return carry

        for i in range(NP - 1, NP - 4, -1):
            load(0, i).start()
            load(1, i).start()
        load(0, NP - 1).wait()
        load(1, NP - 1).wait()
        g0[...] = jnp.zeros((256, E), BF)
        z0[...] = jnp.zeros((256, E), BF)
        lax.fori_loop(0, NP, pair, tuple(jnp.zeros((N, 128), F32) for _ in range(G6)))
        for c in (0, 2, 4):
            drive_dot(0, 0, c)
            step_dot(0, 0, c, False)
        b_dot(0, 0)

    @pl.when(stream == 0)
    def _():
        scan(False)

    @pl.when(stream == 1)
    def _():
        scan(True)

    def step_tile(i, _):
        base = pl.multiple_of(i * 32, 32)
        rows = pl.ds(base, 32)
        for c in range(G6):
            cols = slice(c * 128, c * 128 + 128)
            delta, a, d = dl[c, rows, :], act[c, rows, :], dd[c, rows, :]
            near = 1.0 - delta * (0.5 - delta * (1.0 / 6.0 - delta * (1.0 / 24.0)))
            ratio = jnp.where(delta < 0.03, near, (1.0 - jnp.exp(-delta)) / delta)
            pre = ratio * (zs[c, rows, :] * LN2 + a * d * delta)
            ub[rows, cols] = pre.astype(BF)
            dm[c, rows, :] = delta * d + st[ROW_CHAN + 6 : ROW_CHAN + 7, cols] * dy[c, rows, :]
            sums[1, :, cols] += pre[0:8] + pre[8:16] + pre[16:24] + pre[24:32]
        return 0

    lax.fori_loop(0, R // 32, step_tile, 0)
    pgs = bbd.at[:, 0:128]
    w_step = st[ROW_STEP : ROW_STEP + RANK, :].astype(BF)
    w_b = jnp.concatenate([st[ROW_B : ROW_B + N, :]] * N, 0).astype(BF)
    w_c = jnp.concatenate([st[ROW_C : ROW_C + N, :]] * N, 0).astype(BF)
    w_s = st[0:RANK, :].astype(BF)
    for h in range(2):
        rows = slice(h * 592, h * 592 + 592)
        sg = dot_nt(ub[rows, :], w_step).astype(BF)
        pgs[rows, :] = jnp.concatenate([sg, jnp.zeros((592, 128 - RANK), BF)], 1)
        for c in range(0, G6, 2):
            cols = slice(c * 128, c * 128 + 256)
            y = dot(sg, w_s[:, cols]) + dot(dbm[rows, :], w_b[:, cols]) + dot(dcm[rows, :], w_c[:, cols])
            dm[c, rows, :] += y[:, :128]
            dm[c + 1, rows, :] += y[:, 128:]
    dc = dd
    dc[:, 0:HALO, :] = jnp.zeros((G6, HALO, 128), F32)
    dc[:, HALO + R : XR, :] = jnp.zeros((G6, HALO, 128), F32)

    def conv(rev):
        def first(i, _):
            base = pl.multiple_of(i * 32, 32)
            for c in range(G6):
                cols = slice(c * 128, c * 128 + 128)
                total, lagged = conv_tile(x, lab, st, c, base, 32, rev)
                sig = sigmoid(total)
                v = dm[c, pl.ds(base, 32), :] * sig * (1.0 + total * (1.0 - sig))
                dc[c, pl.ds(base + HALO, 32), :] = v
                sums[2, :, cols] += v[0:8] + v[8:16] + v[16:24] + v[24:32]
                for j in range(4):
                    t = v * lagged[j]
                    sums[3 + j, :, cols] += t[0:8] + t[8:16] + t[16:24] + t[24:32]
            return 0

        def second(i, _):
            base = pl.multiple_of(i * 32, 32)
            here = lab[pl.ds(base + HALO, 32), :]
            for c in range(G6):
                cols = slice(c * 128, c * 128 + 128)
                v = dc[c, pl.ds(base + HALO, 32), :] * st[ROW_CHAN : ROW_CHAN + 1, cols]
                for j in (1, 2, 3):
                    at = base + HALO + (-j if rev else j)
                    same = lab[pl.ds(at, 32), :] == here
                    later = jnp.where(same, dc[c, pl.ds(at, 32), :], 0.0)
                    v = v + later * st[ROW_CHAN + j : ROW_CHAN + j + 1, cols]
                dyb[pl.ds(base, 32), cols] = v.astype(BF)
            return 0

        lax.fori_loop(0, R // 32, first, 0)
        lax.fori_loop(0, R // 32, second, 0)

    @pl.when(stream == 0)
    def _():
        conv(False)

    @pl.when(stream == 1)
    def _():
        conv(True)

    theirs = pl.ds(pl.multiple_of((1 - stream) * WBASE, 32), WIN)
    nsend = mg.at[:, 0:D]
    nsend[...] = dot_nt(dyb[theirs, :], w1[...]).astype(BF)
    nswap = pltpu.make_async_remote_copy(
        src_ref=nsend, dst_ref=nrecv, send_sem=swsend.at[0], recv_sem=swrecv.at[0], **partner
    )
    nswap.start()
    for c in g2:
        c.wait()
    for r in range(0, g2_o.shape[0], 24):
        rows = slice(r, min(r + 24, g2_o.shape[0]))
        total = g2s[place, :, :].astype(F32)[rows]
        for k in range(1, wide):
            total = total + g2r[k].astype(F32)[rows]
        g2_o[rows, :] = total
    g2swap = pltpu.make_async_remote_copy(
        src_ref=g2_o, dst_ref=g2x_o, send_sem=swsend.at[1], recv_sem=swrecv.at[1], **partner
    )
    g2swap.start()
    gpart[...] += dot_nt(dyb[pl.ds(wbase, WIN), :], w1[...])
    for c in range(0, D, 128):
        gw1_o[c : c + 128, :] = dot_tn(normed[:, c : c + 128], dyb[...])
    low = p[0:R, :].astype(BF)
    gstep = dot_tn(low, ub[...])[0:RANK]

    def activation(i, _):
        rows = pl.ds(pl.multiple_of(i * 32, 32), 32)
        for c in range(G6):
            ub[rows, c * 128 : c * 128 + 128] = act[c, rows, :].astype(BF)
        return 0

    lax.fori_loop(0, R // 32, activation, 0)
    top = dot_tn(pgs[...], ub[...])
    gb = dot_tn(dbm[...], ub[...])
    gc = dot_tn(dcm[...], ub[...])
    gb = sum(gb[k * N : k * N + N] for k in range(N))
    gc = sum(gc[k * N : k * N + N] for k in range(N))
    gdecay = jnp.concatenate([dacc[c] for c in range(G6)], 1) * LN2

    def total(k):
        return jnp.sum(sums[k], axis=0, keepdims=True)

    chan = [total(3 + k) for k in range(4)] + [total(2), total(1), total(0)]
    fine = [jnp.sum(stats[k], axis=0, keepdims=True) * (1.0 / VIEW_TOK) for k in range(2)]
    coarse = [v.astype(BF).astype(F32) for v in fine]
    fine = [a - b for a, b in zip(fine, coarse)]
    chan = jnp.concatenate(chan + [jnp.zeros((1, E), F32)] + coarse + fine, 0)
    gt = jnp.concatenate(
        [top[0:RANK], gb, gc, gstep, gdecay, chan, jnp.zeros((128 - 108, E), F32)], 0
    )
    gs_o[...] = gt.T


    nswap.wait()
    ending(meta, wide, tok, etab, cot, nrecv, gpart, st, zs.at[0:3], zs.at[3:6], dd.at[0:3], gain_s, acc, tg_o, gg_o)
    g2swap.wait()


def ending(meta, wide, tok, etab, cot, other, gpart, st, tokf, cotw, out, gain_s, acc, tg_o, gg_o):
    stream = meta[4]
    wbase = pl.multiple_of(stream * WBASE, 32)
    lay_tokens(tok, tokf)
    lay_cotangent(stream, cot, cotw)
    gain_s[...] = gain_row(st, wide)
    acc[...] = jnp.zeros(acc.shape, F32)
    lo = stream * HALF

    def tile(i, _):
        base = pl.multiple_of(i * 32, 32)
        at = pl.multiple_of(wbase + base, 32)
        rows = pl.ds(base, 32)
        res, _l = residual_tile(meta, tokf, etab, at, 32)
        scale = row_scale(res)
        r = at + lax.broadcasted_iota(jnp.int32, (32, 128), 0)
        mine = (r >= lo) & (r < lo + HALF)
        ng, un = [], []
        for c in range(3):
            cols = slice(c * 128, c * 128 + 128)
            v = gpart[rows, cols] + other[rows, cols].astype(F32)
            unit = res[c] * scale
            t = jnp.where(mine, v * unit, 0.0)
            acc[:, cols] += t[0:8] + t[8:16] + t[16:24] + t[24:32]
            ng.append(v * gain_s[0:1, cols])
            un.append(unit)
        mean = sum(jnp.sum(a * b, axis=1, keepdims=True) for a, b in zip(ng, un)) * (1.0 / D)
        for c in range(3):
            out[c, rows, :] = cotw[c, rows, :] + scale * (ng[c] - un[c] * mean)
        return 0

    lax.fori_loop(0, WIN // 32, tile, 0)
    gg_o[...] = acc[...]
    take_half(stream, out, tg_o)


def backward(wide, count, offset, stride, tok, cot, normed, own, other, pack, stats, w1, st, x, act, dl, p, hs):
    S = jax.ShapeDtypeStruct
    V = pltpu.VMEM
    big = V((G6, R, 128), F32)
    own_rows = pack.shape[1]
    return pl.pallas_call(
        functools.partial(bwd_kernel, wide),
        out_shape=[
            S((HALF, D), F32), S((HALF, D), F32), S((D, E), F32), S((E, 128), F32), S((8, D), F32),
            S((own_rows, E), F32), S((own_rows, E), F32),
        ],
        in_specs=[SMEM] * 3 + [VMEM] * 9 + [ANY] * 5,
        out_specs=[VMEM] * 7,
        scratch_shapes=[
            V((G6, XR, 128), F32), big, big, V((1280, 128), F32),
            V((D, E), BF), V((E, D), BF), V((WIN, D), F32), V((WIN, E), BF), V((WIN, E), BF),
            V((wide, own_rows, E), BF), V((wide, own_rows, E), BF), V((WIN, D), BF),
            V((XR, 128), jnp.int32), big, big, V((R, E), BF), V((R, E), BF), V((R * N, 128), F32),
            V((R, 256), BF), V((R, 256), BF), V((R, 256), BF), V((G6, XR, 128), F32), big, V((G6, N, 128), F32),
            V((RING, 256, E), BF), V((RING, 256, E), BF),
            V((256, E), BF), V((256, E), BF), V((256, E), BF), V((256, E), BF), V((32, 256), BF), V((7, 8, E), F32),
            V((8, D), F32), V((8, D), F32), V((8, D), F32),
            pltpu.SemaphoreType.DMA((2, RING)), pltpu.SemaphoreType.DMA((4,)),
            pltpu.SemaphoreType.DMA((3,)), pltpu.SemaphoreType.DMA((3,)),
            pltpu.SemaphoreType.DMA((wide,)), pltpu.SemaphoreType.DMA((wide,)),
            pltpu.SemaphoreType.DMA((2,)), pltpu.SemaphoreType.DMA((2,)),
        ],
        compiler_params=pltpu.CompilerParams(
            vmem_limit_bytes=63 * 2**20, collective_id=4, has_side_effects=True
        ),
        cost_estimate=pl.CostEstimate(flops=int(9e10), bytes_accessed=1 << 20, transcendentals=0),
        name="backward",
    )(count, offset, stride, tok, cot, normed, own, other, pack, stats, w1, st, x, act, dl, p, hs)


PACK = 128
ROWS_S = 48
ROWS_W = 24


def greet(d, w, wide):
    bar = pltpu.get_barrier_semaphore()
    for k in range(1, wide):
        pl.semaphore_signal(bar, inc=1, device_id=(d, w ^ k), device_id_type=MESH)
    pl.semaphore_signal(bar, inc=1, device_id=(1 - d, w), device_id_type=MESH)
    pl.semaphore_wait(bar, wide)


def gather_kernel(
    wide, inp, state, step, decay, chan, gain, w1_o, s_o, stage, mine, got, send, recv, psend, precv
):
    d, w = lax.axis_index("dir"), lax.axis_index("wide")
    stage[...] = jnp.zeros(stage.shape, F32)
    stage[ROW_STEP:ROW_DECAY, 0:ROWS_S] = step[0]
    stage[ROW_DECAY:ROW_CHAN, 0:ROWS_S] = decay[0]
    stage[ROW_CHAN:ROW_GAIN, 0:ROWS_S] = chan[0]
    stage[ROW_GAIN : ROW_GAIN + 1, 0:ROWS_W] = gain[...]
    small = stage[...].T[0:ROWS_S]
    stage[0:ROWS_S, 0:ROW_STEP] = state[0]
    col = lax.broadcasted_iota(jnp.int32, (ROWS_S, 128), 1)
    parts = [jnp.where(col < ROW_STEP, stage[0:ROWS_S, :], small)]
    for c in range(3):
        low, high = inp[:, c * 128 : c * 128 + 128], inp[:, D + c * 128 : D + c * 128 + 128]
        parts.append(jnp.where(d == 0, low, high))
    parts.append(jnp.zeros((PACK - ROWS_S - 3 * ROWS_W, 128), F32))
    mine[...] = jnp.concatenate(parts, 0).astype(BF)
    got[w] = mine[...]
    greet(d, w, wide)
    copies = []
    for k in range(1, wide):
        copies.append(
            pltpu.make_async_remote_copy(
                src_ref=mine, dst_ref=got.at[w], send_sem=send.at[k], recv_sem=recv.at[k],
                device_id=(d, w ^ k), device_id_type=MESH,
            )
        )
        copies[-1].start()
    for c in copies:
        c.wait_recv()
    for k in range(0, wide, 2):
        s_o[k * ROWS_S : (k + 2) * ROWS_S, :] = jnp.concatenate([got[k, 0:ROWS_S], got[k + 1, 0:ROWS_S]], 0)
        v = [got[k + i, ROWS_S:PACK, :].astype(F32) for i in range(2)]
        for c in range(3):
            piece = [t[c * ROWS_W : (c + 1) * ROWS_W] for t in v]
            piece = jnp.concatenate(piece, 0).astype(BF)
            for s in range(2):

                @pl.when(d == s)
                def _():
                    at = s * D + c * 128
                    w1_o[k * ROWS_W : (k + 2) * ROWS_W, at : at + 128] = piece

    cols = pl.ds(pl.multiple_of(d * D, 128), D)
    half = pltpu.make_async_remote_copy(
        src_ref=w1_o.at[:, cols], dst_ref=w1_o.at[:, cols], send_sem=psend, recv_sem=precv,
        device_id=(1 - d, w), device_id_type=MESH,
    )
    half.start()
    for c in copies:
        c.wait_send()
    half.wait()


def gather(wide, inp, state, step, decay, chan, gain):
    S = jax.ShapeDtypeStruct
    return pl.pallas_call(
        functools.partial(gather_kernel, wide),
        out_shape=[S((D, E), BF), S((E, 128), BF)],
        in_specs=[VMEM] * 6,
        out_specs=[VMEM] * 2,
        scratch_shapes=[
            pltpu.VMEM((128, 128), F32), pltpu.VMEM((PACK, 128), BF), pltpu.VMEM((wide, PACK, 128), BF),
            pltpu.SemaphoreType.DMA((wide,)), pltpu.SemaphoreType.DMA((wide,)),
            pltpu.SemaphoreType.DMA, pltpu.SemaphoreType.DMA,
        ],
        compiler_params=pltpu.CompilerParams(collective_id=1, has_side_effects=True),
        name="gather",
    )(inp, state, step, decay, chan, gain)


def reduce_kernel(
    wide, gw1, gs, gg, own_o, other_o,
    pout, pin, out, got, gcol, send, recv, psend, precv, fsend, frecv,
):
    d, w = lax.axis_index("dir"), lax.axis_index("wide")
    greet(d, w, wide)
    for s in range(2):

        @pl.when(d == s)
        def _():
            pout[...] = gw1[:, (1 - s) * D : (2 - s) * D].astype(BF)

    pre = pltpu.make_async_remote_copy(
        src_ref=pout, dst_ref=pin, send_sem=psend, recv_sem=precv,
        device_id=(1 - d, w), device_id_type=MESH,
    )
    pre.start()
    gcol[...] = gg[...].T
    pre.wait()
    copies = []
    lane = lax.broadcasted_iota(jnp.int32, (ROWS_S, 128), 1)
    for k in range(wide):
        rows = slice(k * ROWS_W, (k + 1) * ROWS_W)
        g = jnp.sum(gcol[rows, :], axis=1, keepdims=True)
        g = jnp.concatenate([g, jnp.zeros((ROWS_S - ROWS_W, 1), F32)], 0)
        small = jnp.where(lane == ROW_GAIN, g, gs[k * ROWS_S : (k + 1) * ROWS_S, :])
        parts = [small]
        at = k * ROWS_W % 16
        base = k * ROWS_W - at
        arrived = pin[base : base + 32, :].astype(F32)[at : at + ROWS_W]
        for c in range(3):
            low, high = gw1[rows, c * 128 : c * 128 + 128], gw1[rows, D + c * 128 : D + c * 128 + 128]
            parts.append(jnp.where(d == 0, low, high) + arrived[:, c * 128 : c * 128 + 128])
        parts.append(jnp.zeros((PACK - ROWS_S - 3 * ROWS_W, 128), F32))
        out[k] = jnp.concatenate(parts, 0).astype(BF)
    for k in range(1, wide):
        copies.append(
            pltpu.make_async_remote_copy(
                src_ref=out.at[w ^ k], dst_ref=got.at[k], send_sem=send.at[k], recv_sem=recv.at[k],
                device_id=(d, w ^ k), device_id_type=MESH,
            )
        )
        copies[-1].start()
    for c in copies:
        c.wait()
    total = out[w].astype(F32)
    for k in range(1, wide):
        total = total + got[k].astype(F32)
    own_o[...] = total
    last = pltpu.make_async_remote_copy(
        src_ref=own_o, dst_ref=other_o, send_sem=fsend, recv_sem=frecv,
        device_id=(1 - d, w), device_id_type=MESH,
    )
    last.start()
    last.wait()


def reduce(wide, gw1, gs, gg):
    S = jax.ShapeDtypeStruct
    return pl.pallas_call(
        functools.partial(reduce_kernel, wide),
        out_shape=[S((PACK, 128), F32), S((PACK, 128), F32)],
        in_specs=[VMEM] * 3,
        out_specs=[VMEM] * 2,
        scratch_shapes=[
            pltpu.VMEM((D, D), BF), pltpu.VMEM((D, D), BF), pltpu.VMEM((wide, PACK, 128), BF),
            pltpu.VMEM((wide, PACK, 128), BF), pltpu.VMEM((D, 8), F32),
            pltpu.SemaphoreType.DMA((wide,)), pltpu.SemaphoreType.DMA((wide,)),
        ]
        + [pltpu.SemaphoreType.DMA] * 4,
        compiler_params=pltpu.CompilerParams(collective_id=2, has_side_effects=True),
        name="reduce",
    )(gw1, gs, gg)


def gather_plain(inp, state, step, decay, chan, gain):
    rows = state.shape[1]
    column = jnp.concatenate([gain, jnp.zeros((rows - gain.shape[0],), F32)])[:, None]
    small = [state[0], step[0].T, decay[0].T, chan[0].T, column, jnp.zeros((rows, 127 - ROW_GAIN), F32)]
    small = jnp.concatenate(small, 1).astype(BF)
    return (
        lax.all_gather(inp[:, :E].astype(BF), "wide", axis=0, tiled=True),
        lax.all_gather(small, "wide", axis=0, tiled=True),
    )


def reduce_plain(gw1, gs, gg):
    def total(v):
        return lax.psum_scatter(v, "wide", scatter_dimension=0, tiled=True)

    return total(lax.psum(gw1, "dir")), total(gs), total(lax.psum(gg.sum(0), "dir"))


def adam_step(weight, gradient, first_moment, second, step_rate, decay_rate):
    first_moment = BETA_ONE * first_moment + (1.0 - BETA_ONE) * gradient
    second = BETA_TWO * second + (1.0 - BETA_TWO) * gradient * gradient
    first_hat = first_moment / (1.0 - BETA_ONE**STEP)
    second_hat = second / (1.0 - BETA_TWO**STEP)
    weight = weight - step_rate * (
        first_hat / (jnp.sqrt(second_hat) + EPS_ADAM) + decay_rate * weight
    )
    return (weight, first_moment, second)


def update_kernel(got, twin, g2, g2x, *refs):
    stream = lax.axis_index("dir")
    masters, outs = refs[:21], refs[21:]

    def step(k, gradient, at=(slice(None),), out=None):
        new = adam_step(
            masters[3 * k][at], gradient, masters[3 * k + 1][at], masters[3 * k + 2][at], RATES[k], DECAYS[k]
        )
        for i in range(3):
            outs[1 + 3 * k + i][at] = new[i]

    mine, theirs = got[...], twin[...]
    low, high = jnp.where(stream == 0, mine, theirs), jnp.where(stream == 0, theirs, mine)
    for h, v in enumerate((low, high)):
        for c in range(3):
            at = ROWS_S + c * ROWS_W
            col = h * D + c * 128
            step(0, v[at : at + ROWS_W], (slice(None), slice(col, col + 128)))
    shared = g2[...] + g2x[...]
    step(0, shared[0:ROWS_W], (slice(None), slice(E, 2 * E)))
    step(1, shared[ROWS_W:, 0:D], (slice(0, ROWS_W), slice(None)))
    step(1, shared[ROWS_W:, D:], (slice(ROWS_W, 2 * ROWS_W), slice(None)))
    t = mine.T
    gain = t[ROW_GAIN : ROW_GAIN + 1, 0:ROWS_W] + theirs.T[ROW_GAIN : ROW_GAIN + 1, 0:ROWS_W]
    step(2, gain)
    step(3, mine[0:ROWS_S, 0:ROW_STEP], (0,))
    step(4, t[ROW_STEP:ROW_DECAY, 0:ROWS_S], (0,))
    step(5, t[ROW_DECAY:ROW_CHAN, 0:ROWS_S], (0,))
    for k in range(7):
        step(6, t[ROW_CHAN + k : ROW_CHAN + k + 1, 0:ROWS_S], (k,))
    outs[0][0] = t[ROW_STATS : ROW_STATS + 2, 0:ROWS_S] + t[ROW_STATS + 2 : ROW_STATS + 4, 0:ROWS_S]


def update(got, twin, g2, g2x, masters):
    S = jax.ShapeDtypeStruct
    masters = list(masters)
    masters[6:9] = [v[None] for v in masters[6:9]]
    masters[18:21] = [jnp.transpose(v, (1, 0, 2)) for v in masters[18:21]]
    outs = pl.pallas_call(
        update_kernel,
        out_shape=[S((1, 2, ROWS_S), F32)] + [S(v.shape, F32) for v in masters],
        in_specs=[VMEM] * 25,
        out_specs=[VMEM] * 22,
        name="update",
    )(got, twin, g2, g2x, *masters)
    stats, outs = outs[0], list(outs[1:])
    outs[6:9] = [v[0] for v in outs[6:9]]
    outs[18:21] = [jnp.transpose(v, (1, 0, 2)) for v in outs[18:21]]
    return stats, outs


def update_plain(gw1, gs, gg, g2, masters):
    drow = masters[0].shape[0]
    g1, small, gain = reduce_plain(gw1, gs, gg)
    t = small.T
    grads = (
        jnp.concatenate([g1, g2[:drow]], 1),
        jnp.concatenate([g2[drow:, :D], g2[drow:, D:]], 0),
        gain,
        small[None, :, :ROW_STEP],
        t[None, ROW_STEP:ROW_DECAY],
        t[None, ROW_DECAY:ROW_CHAN],
        t[None, ROW_CHAN:ROW_GAIN],
    )
    outs = []
    for k, g in enumerate(grads):
        w, f, s2 = masters[3 * k : 3 * k + 3]
        outs += adam_step(w, g, f, s2, RATES[k], DECAYS[k])
    return (t[ROW_STATS : ROW_STATS + 2] + t[ROW_STATS + 2 : ROW_STATS + 4])[None], outs


def local(tokens, cotangent, view_counts, view_strides, view_offsets, *masters):
    stream = lax.axis_index("dir")
    wide = lax.axis_size("wide")
    in_proj, out_proj, norm_gain = masters[0], masters[3], masters[6]
    drow, erow = in_proj.shape[0], out_proj.shape[0]
    mine = E // wide == ROWS_S and D // wide == ROWS_W
    out_pair = jnp.concatenate([out_proj[: erow // 2], out_proj[erow // 2 :]], 1)
    pack = jnp.concatenate([in_proj[:, E:], out_pair], 0).astype(BF)
    pack = lax.all_gather(pack, "wide", axis=0)
    weights = (in_proj, masters[9], masters[12], masters[15], masters[18])
    if mine:
        w1, s = gather(wide, *weights, norm_gain[None])
    else:
        w1, s = gather_plain(*weights, norm_gain)
    about = (view_counts, view_offsets, view_strides)
    tok, cot = tokens[0], cotangent[0]
    normed, x, act, dl, p, st, res, other, stats, hs = forward(wide, *about, tok, w1, s)
    own = lax.dynamic_slice_in_dim(res, stream * WBASE, WIN, 0)
    block, token_grad, gw1, gs, gg, g2, g2x = backward(
        wide, *about, tok, cot, normed, own, other, pack, stats, w1, st, x, act, dl, p, hs
    )
    if mine:
        stats, outs = update(*reduce(wide, gw1, gs, gg), g2, g2x, masters)
    else:
        stats, outs = update_plain(gw1, gs, gg, g2 + g2x, masters)
    return (block[None], token_grad[None], stats, *outs)


def solution(mesh):
    row, col = P("wide", None), P("dir", None, "wide")
    mat = P("dir", "wide", None)
    weights = [row] * 6 + [P("wide")] * 3 + [mat] * 3 + [col] * 9
    return jax.shard_map(
        local,
        mesh=mesh,
        in_specs=(
            P("wide", None, None), P("wide", "dir", None), P("wide"), row, row, *weights,
        ),
        out_specs=(P("wide", "dir", None), P("wide", "dir", None), col, *weights),
        check_vma=False,
    )
```

```python
import functools
import math

import jax
import jax.numpy as jnp
from jax import lax
from jax.experimental import pallas as pl
from jax.experimental.pallas import tpu as pltpu
from jax.sharding import PartitionSpec as P

PATCHES = 196
STEP = 10
VIEW_TOK = 392
EPS_NORM = 1e-06
BETA_ONE = 0.9
BETA_TWO = 0.95
EPS_ADAM = 1e-08
RATES = (0.15, 0.1, 2.5, 0.12, 0.2, 1.0, 2.5)
DECAYS = (0.1, 0.1, 0.0, 0.1, 0.1, 0.0, 0.0)

F32 = jnp.float32
BF = jnp.bfloat16
LN2 = math.log(2.0)
LOG2E = 1.0 / LN2

SLOTS = 1176
R = 1184
NB = R // 16
NP = NB // 2
HALF = 588
WIN = 608
WBASE = 576
D = 384
E = 768
G6 = E // 128
N = 16
RANK = 24
HALO = 8
XR = HALO + R + HALO
RING = 4
CUT = 1e4
SENDS = WIN // 32
MESH = pl.DeviceIdType.MESH
ROW_B, ROW_C, ROW_STEP, ROW_DECAY, ROW_CHAN, ROW_GAIN, ROW_STATS = 24, 40, 56, 80, 96, 103, 104
NT = (((1,), (1,)), ((), ()))
TN = (((0,), (0,)), ((), ()))
VMEM = pl.BlockSpec(memory_space=pltpu.VMEM)
SMEM = pl.BlockSpec(memory_space=pltpu.SMEM)
ANY = pl.BlockSpec(memory_space=pl.ANY)


def dot(a, b):
    return jnp.dot(a, b, preferred_element_type=F32)


def dot_nt(a, b):
    return lax.dot_general(a, b, NT, preferred_element_type=F32)


def dot_tn(a, b):
    return lax.dot_general(a, b, TN, preferred_element_type=F32)


def sigmoid(v):
    return 0.5 * jnp.tanh(0.5 * v) + 0.5


def rows16(b, n=16):
    return pl.ds(pl.multiple_of(b * 16, 16), n)


def labels_of(meta, r):
    lab = jnp.full(r.shape, -1, jnp.int32)
    late = jnp.zeros(r.shape, jnp.int32)
    for k in range(3):
        start = meta[1 + k]
        inside = (r >= start) & (r < start + VIEW_TOK) & (k < meta[0])
        lab = jnp.where(inside, k, lab)
        late = jnp.where(inside, jnp.where(r >= start + PATCHES, 1, 0), late)
    lab = jnp.where(r < 0, -2, lab)
    lab = jnp.where(r >= SLOTS, -3, lab)
    return lab, late


def residual_tile(meta, tok, etab, base, n):
    r = base + lax.broadcasted_iota(jnp.int32, (n, 128), 0)
    lab, late = labels_of(meta, r)
    live = jnp.where(lab >= 0, 1.0, 0.0)
    out = []
    for c in range(3):
        cols = slice(c * 128, c * 128 + 128)
        emb = jnp.where(lab >= 0, etab[3:4, cols], 0.0)
        for k in range(3):
            emb = jnp.where((lab == k) & (late == 1), etab[k : k + 1, cols], emb)
        out.append(tok[c, pl.ds(base, n), :] + emb)
    return out, live


def lay_tokens(tok, tokf):
    for c in range(3):
        tokf[c, 0:SLOTS, :] = tok[:, c * 128 : c * 128 + 128].astype(F32)
        tokf[c, SLOTS:R, :] = jnp.zeros((R - SLOTS, 128), F32)


def row_scale(res):
    total = sum(jnp.sum(v * v, axis=1, keepdims=True) for v in res)
    return lax.rsqrt(total * (1.0 / D) + EPS_NORM)


def fill_labels(meta, lab_ref):
    for base in range(0, XR, 8):
        r = base - HALO + lax.broadcasted_iota(jnp.int32, (8, 128), 0)
        lab_ref[base : base + 8, :] = labels_of(meta, r)[0]


def gain_row(st_ref, wide):
    per = E // wide
    own = D // wide
    i = lax.broadcasted_iota(jnp.int32, (E, D), 0)
    j = lax.broadcasted_iota(jnp.int32, (E, D), 1)
    pick = jnp.where(i == (j // own) * per + j % own, 1.0, 0.0).astype(BF)
    src = jnp.broadcast_to(st_ref[ROW_GAIN : ROW_GAIN + 1, :], (16, E)).astype(BF)
    return dot(src, pick)[0:8]


def spread_tile(p_ref, lane, out_ref, base):
    v = p_ref[pl.ds(base, 32), :].T[lane : lane + N]
    for j in range(32):
        out_ref[pl.ds(pl.multiple_of((base + j) * N, N), N), :] = jnp.broadcast_to(v[:, j : j + 1], (N, 128))


def pairs(count, body):
    def two(i, _):
        body(2 * i)
        body(2 * i + 1)
        return 0

    lax.fori_loop(0, count // 2, two, 0)
    if count % 2:
        body(count - 1)


def conv_tile(x_ref, lab_ref, st_ref, c, base, n, rev):
    cols = slice(c * 128, c * 128 + 128)
    here = lab_ref[pl.ds(base + HALO, n), :]
    lagged = [x_ref[c, pl.ds(base + HALO, n), :]]
    for j in (1, 2, 3):
        at = base + HALO + (j if rev else -j)
        same = lab_ref[pl.ds(at, n), :] == here
        lagged.append(jnp.where(same, x_ref[c, pl.ds(at, n), :], 0.0))
    total = st_ref[ROW_CHAN + 4 : ROW_CHAN + 5, cols]
    for j in range(4):
        total = total + st_ref[ROW_CHAN + j : ROW_CHAN + j + 1, cols] * lagged[j]
    return total, lagged


def views(count, offset, stream):
    return [count[0], offset[0, 0], offset[0, 1], offset[0, 2], stream]


def fill_embedding(stride, etab):
    lane = lax.broadcasted_iota(jnp.int32, (8, D), 1)
    row = lax.broadcasted_iota(jnp.int32, (8, D), 0)
    half = D // 2
    j = jnp.where(lane < half, lane, lane - half).astype(F32)
    freq = jnp.exp(-math.log(10000.0) * j / half)
    clock = jnp.zeros((8, D), F32)
    for k in range(3):
        clock = jnp.where(row == k, stride[0, k].astype(F32), clock)
    angle = clock * freq
    etab[...] = jnp.where(lane < half, jnp.sin(angle), jnp.cos(angle))


def fwd_kernel(wide, mine, *refs):
    refs = list(refs)
    count, offset, stride, tok = refs[:4]
    given, refs = refs[4 : 4 + (7 if mine else 2)], refs[4 + (7 if mine else 2) :]
    (
        normed_h, x_h, act_h, dl_h, p_h, st_h, res_h, other_h, w1_h, *pack_h, stats_o, hs_o,
    ) = refs[: 12 if mine else 11]
    (
        normed_o, x_o, act_o, dl_o, p_o, st_o, res_o, other_o, w1, al_o, s_ref,
        lab, dm, u, bb, cbd, hse, hso, gain_s, tokf, etab, sem, out_sem, send, recv, *links,
    ) = refs[12 if mine else 11 :]
    stream, place = lax.axis_index("dir"), lax.axis_index("wide")
    meta = views(count, offset, stream)
    if mine:
        stage, first, got, second, pack, gsend, grecv, psend, precv, hsem = links
        fill_shares(stream, given, stage, first, second)
        got[place] = first[...]
        pack[place] = second[...]
        greet(stream, place, wide)
        early, later = [], []
        for k in range(1, wide):
            where = dict(device_id=(stream, place ^ k), device_id_type=MESH)
            early.append(
                pltpu.make_async_remote_copy(
                    src_ref=first, dst_ref=got.at[place], send_sem=gsend.at[k], recv_sem=grecv.at[k], **where
                )
            )
            later.append(
                pltpu.make_async_remote_copy(
                    src_ref=second, dst_ref=pack.at[place], send_sem=psend.at[k], recv_sem=precv.at[k], **where
                )
            )
            early[-1].start()
    else:
        bar = pltpu.get_barrier_semaphore()
        pl.semaphore_signal(bar, inc=1, device_id=(1 - stream, place), device_id_type=MESH)
        pl.semaphore_wait(bar, 1)
        w1[...] = given[0][...]
        s_ref[...] = given[1][...]
    fill_embedding(stride, etab)
    lay_tokens(tok, tokf)
    fill_labels(meta, lab)

    def unit_tile(i):
        base = i * 32 if isinstance(i, int) else pl.multiple_of(i * 32, 32)
        res, _l = residual_tile(meta, tokf, etab, base, 32)
        scale = row_scale(res)
        for c in range(3):
            tokf[c, pl.ds(base, 32), :] = res[c] * scale

    pairs(R // 32, unit_tile)
    if mine:
        for c in early:
            c.wait_recv()
        take_shares(stream, wide, got, w1, s_ref)
        cols = pl.ds(pl.multiple_of(stream * D, 128), D)
        half = pltpu.make_async_remote_copy(
            src_ref=w1.at[:, cols], dst_ref=w1.at[:, cols], send_sem=hsem.at[0], recv_sem=hsem.at[1],
            device_id=(1 - stream, place), device_id_type=MESH,
        )
        half.start()
        for c in early:
            c.wait_send()
        for c in later:
            c.start()
    st_o[...] = s_ref[...].astype(F32).T
    gain_s[...] = gain_row(st_o, wide)
    saves = [
        pltpu.make_async_copy(v, h, out_sem.at[k])
        for k, (v, h) in enumerate(
            zip(
                (normed_o, x_o, act_o, dl_o, p_o, st_o, w1, res_o, other_o),
                (normed_h, x_h, act_h, dl_h, p_h, st_h, w1_h, res_h, other_h),
            )
        )
    ]

    def norm_tile(i, _):
        base = pl.multiple_of(i * 32, 32)
        for c in range(3):
            cols = slice(c * 128, c * 128 + 128)
            normed_o[pl.ds(base, 32), cols] = (tokf[c, pl.ds(base, 32), :] * gain_s[0:1, cols]).astype(BF)
        return 0

    lax.fori_loop(0, R // 32, norm_tile, 0)
    if mine:
        half.wait()
    x_o[:, 0:HALO, :] = jnp.zeros((G6, HALO, 128), F32)
    x_o[:, HALO + R : XR, :] = jnp.zeros((G6, HALO, 128), F32)
    for h in range(2):
        for c in range(0, G6, 2):
            y = dot(normed_o[h * 592 : h * 592 + 592, :], w1[:, c * 128 : c * 128 + 256])
            x_o[c, HALO + h * 592 : HALO + h * 592 + 592, :] = y[:, :128]
            x_o[c + 1, HALO + h * 592 : HALO + h * 592 + 592, :] = y[:, 128:]

    def conv(rev):
        def tile(i, _):
            base = pl.multiple_of(i * 32, 32)
            for c in range(G6):
                total, _l = conv_tile(x_o, lab, st_o, c, base, 32, rev)
                act = total * sigmoid(total)
                act_o[c, pl.ds(base, 32), :] = act
                al_o[pl.ds(base, 32), c * 128 : c * 128 + 128] = act.astype(BF)
            return 0

        lax.fori_loop(0, R // 32, tile, 0)

    @pl.when(stream == 0)
    def _():
        conv(False)

    @pl.when(stream == 1)
    def _():
        conv(True)

    p_o[R:, :] = jnp.zeros((1280 - R, 128), F32)
    col = lax.broadcasted_iota(jnp.int32, (128, 256), 1)
    row = lax.broadcasted_iota(jnp.int32, (128, 256), 0)
    spread_c = jnp.where(row == ROW_C + col % N, 1.0, 0.0).astype(BF)
    diag = (
        lax.broadcasted_iota(jnp.int32, (592, 256), 0) % N
        == lax.broadcasted_iota(jnp.int32, (592, 256), 1) // N
    )
    for h in range(2):
        rows = slice(h * 592, h * 592 + 592)
        proj = dot(al_o[rows, :], s_ref[...])
        p_o[rows, :] = proj
        low = proj.astype(BF)
        cbd[rows, :] = jnp.where(diag, dot(low, spread_c), 0.0).astype(BF)
        step_in = low[:, :RANK]
        for c in range(0, G6, 2):
            w = st_o[ROW_STEP : ROW_STEP + RANK, c * 128 : c * 128 + 256].astype(BF)
            y = dot(step_in, w)
            dl_o[c, rows, :] = y[:, :128]
            dl_o[c + 1, rows, :] = y[:, 128:]
    stats_o[...] = jnp.zeros(stats_o.shape, F32)

    def soft(rev):
        def tile(i, _):
            base = pl.multiple_of(i * 32, 32)
            here = lab[pl.ds(base + HALO, 32), :]
            before = lab[pl.ds(base + HALO + (1 if rev else -1), 32), :]
            cut = jnp.where(here == before, 0.0, CUT)
            live = jnp.where(here >= 0, 1.0, 0.0)
            real = jnp.where(here >= -1, 1.0, 0.0)
            spread_tile(p_o, ROW_B, bb, base)
            for c in range(G6):
                cols = slice(c * 128, c * 128 + 128)
                rows = pl.ds(base, 32)
                v = dl_o[c, rows, :] + st_o[ROW_CHAN + 5 : ROW_CHAN + 6, cols]
                delta = jnp.maximum(v, 0.0) + jnp.log1p(jnp.exp(-jnp.abs(v)))
                dl_o[c, rows, :] = delta
                dm[c, rows, :] = delta + cut
                u[c, rows, :] = delta * act_o[c, rows, :] * real
                t1 = live * delta
                t2 = t1 * delta
                for s in range(4):
                    stats_o[0, :, cols] += t1[8 * s : 8 * s + 8]
                    stats_o[1, :, cols] += t2[8 * s : 8 * s + 8]
            return 0

        lax.fori_loop(0, R // 32, tile, 0)

    @pl.when(stream == 0)
    def _():
        soft(False)

    @pl.when(stream == 1)
    def _():
        soft(True)

    for c in saves[:7]:
        c.start()
    hs = (hse, hso)

    def save(k, i):
        slot = i % RING
        return pltpu.make_async_copy(hs[k].at[slot], hs_o.at[k, i], sem.at[k, slot])

    def give(i, rev):
        row = pl.multiple_of((NP - 1 - i if rev else i) * 32, 32)
        at = pl.multiple_of(row if rev else row - WBASE, 32)
        k = i - (NP - SENDS)
        return pltpu.make_async_remote_copy(
            src_ref=res_o.at[pl.ds(row, 32), :], dst_ref=other_o.at[pl.ds(at, 32), :],
            send_sem=send.at[k], recv_sem=recv.at[k], device_id=(1 - stream, place), device_id_type=MESH,
        )

    def scan(rev):
        rate = [
            -jnp.exp(st_o[ROW_DECAY : ROW_DECAY + N, c * 128 : c * 128 + 128]) * LOG2E
            for c in range(G6)
        ]

        def block_of(t):
            return NB - 1 - t if rev else t

        def emit(t, k, slot, c):
            rows = rows16(block_of(t))
            y = dot(cbd[rows, :], hs[k][slot, :, c * 128 : c * 128 + 256])
            for h in range(2):
                cols = slice((c + h) * 128, (c + h) * 128 + 128)
                skip = st_o[ROW_CHAN + 6 : ROW_CHAN + 7, cols]
                res_o[rows, cols] = (
                    y[:, h * 128 : h * 128 + 128] + skip * act_o[c + h, rows, :]
                ).astype(BF)

        def block(t, k, slot, state, late):
            b = block_of(t)
            state = list(state)
            for n, j in enumerate(range(15, -1, -1) if rev else range(16)):
                if n % 4 == 0 and late:
                    late.pop(0)()
                q = b * 16 + j
                drive = bb[pl.ds(pl.multiple_of(q * N, N), N), :]
                for c in range(G6):
                    fade = jnp.exp2(dm[c, pl.ds(q, 1), :] * rate[c])
                    state[c] = fade * state[c] + u[c, pl.ds(q, 1), :] * drive
                    hs[k][slot, j * N : j * N + N, c * 128 : c * 128 + 128] = state[c].astype(BF)
            return tuple(state)

        def pair(i, state):
            slot = i % RING

            @pl.when(i >= RING)
            def _():
                save(0, i - RING).wait()
                save(1, i - RING).wait()

            before = jnp.maximum(2 * i - 1, 0)
            late = [
                functools.partial(emit, before, 1, jnp.maximum(i - 1, 0) % RING, c)
                for c in (0, 2, 4)
            ]
            one = 1 + i // 1048576
            state = lax.fori_loop(0, one, lambda _, v, late=late: block(2 * i, 0, slot, v, list(late)), state)
            late = [functools.partial(emit, 2 * i, 0, slot, c) for c in (0, 2, 4)]
            state = lax.fori_loop(0, one, lambda _, v, late=late: block(2 * i + 1, 1, slot, v, list(late)), state)
            save(0, i).start()
            save(1, i).start()

            @pl.when(i > NP - SENDS)
            def _():
                give(i - 1, rev).start()

            return state

        hso[0] = jnp.zeros((256, E), BF)
        lax.fori_loop(0, NP, pair, tuple(jnp.zeros((N, 128), F32) for _ in range(G6)))
        for c in (0, 2, 4):
            emit(NB - 1, 1, (NP - 1) % RING, c)
        give(NP - 1, rev).start()
        for i in range(NP - RING, NP):
            save(0, i).wait()
            save(1, i).wait()

        def settle(i, _):
            give(i, rev).wait()
            return 0

        lax.fori_loop(NP - SENDS, NP, settle, 0)

    @pl.when(stream == 0)
    def _():
        scan(False)

    @pl.when(stream == 1)
    def _():
        scan(True)

    for c in saves[7:]:
        c.start()
    if mine:
        for c in later:
            c.wait()
        packed = pltpu.make_async_copy(pack, pack_h[0], out_sem.at[9])
        packed.start()
        packed.wait()
    for c in saves:
        c.wait()


def forward(wide, mine, count, offset, stride, tok, *given):
    S = jax.ShapeDtypeStruct
    V = pltpu.VMEM
    kept = [
        ((R, D), BF), ((G6, XR, 128), F32), ((G6, R, 128), F32), ((G6, R, 128), F32), ((1280, 128), F32),
        ((128, E), F32), ((R, E), BF), ((WIN, E), BF), ((D, E), BF),
    ]
    pack = [((wide, 2 * D // wide, E), BF)] if mine else []
    dma = pltpu.SemaphoreType.DMA
    links = [
        V((128, 128), F32), V((PACK, 128), BF), V((wide, PACK, 128), BF), V(pack[0][0][1:], BF), V(*pack[0]),
        dma((wide,)), dma((wide,)), dma((wide,)), dma((wide,)), dma((2,)),
    ] if mine else []
    return pl.pallas_call(
        functools.partial(fwd_kernel, wide, mine),
        out_shape=[S(*k) for k in kept + pack] + [S((2, 8, E), F32), S((2, NP, 256, E), BF)],
        in_specs=[SMEM] * 3 + [VMEM] * (1 + len(given)),
        out_specs=[ANY] * len(kept + pack) + [VMEM, ANY],
        scratch_shapes=[V(*k) for k in kept]
        + [
            V((R, E), BF), V((E, 128), BF), V((XR, 128), jnp.int32), V((G6, R, 128), F32), V((G6, R, 128), F32),
            V((R * N, 128), F32), V((R, 256), BF), V((RING, 256, E), BF), V((RING, 256, E), BF), V((8, D), F32),
            V((3, R, 128), F32), V((8, D), F32),
            dma((2, RING)), dma((10,)), dma((SENDS,)), dma((SENDS,)),
        ]
        + links,
        compiler_params=pltpu.CompilerParams(
            vmem_limit_bytes=60 * 2**20, collective_id=3, has_side_effects=True
        ),
        cost_estimate=pl.CostEstimate(flops=int(5e10), bytes_accessed=1 << 20, transcendentals=0),
        name="forward",
    )(count, offset, stride, tok, *given)


def middle(meta, wide, tokf, etab, cot, normed, own, other, w2, wo, cotw, gated, bgrad, ggrad, blk, mg, gpart, stage, sent, shared):
    stream = meta[4]
    wbase = pl.multiple_of(stream * WBASE, 32)
    lay_cotangent(stream, cot, cotw)
    win = pl.ds(wbase, WIN)

    def tile(i, _):
        base = pl.multiple_of(i * 32, 32)
        r = wbase + base + lax.broadcasted_iota(jnp.int32, (32, 128), 0)
        live = jnp.where(labels_of(meta, r)[0] >= 0, 1.0, 0.0)
        for c in range(3):
            v = live * cotw[c, pl.ds(base, 32), :]
            ref, col = (bgrad[0], c * 128) if c < 2 else (bgrad[1], 0)
            ref[pl.ds(base, 32), col : col + 128] = v.astype(BF)
        return 0

    lax.fori_loop(0, WIN // 32, tile, 0)

    def branch_grad():
        return jnp.concatenate([bgrad[0][0:WIN, :], bgrad[1][0:WIN, 0:128]], 1)

    for c in range(0, E, 256):
        cols = slice(c, c + 256)
        gate = dot(normed[win, :], w2[:, cols])
        mixed = own(cols) + other(cols)
        sig = sigmoid(gate)
        silu = gate * sig
        gated[0:WIN, cols] = (mixed * silu).astype(BF)
        up = dot_nt(branch_grad(), wo[cols, :])
        mg[:, cols] = (up * silu).astype(BF)
        ggrad[0:WIN, cols] = (up * mixed * sig * (1.0 + gate * (1.0 - sig))).astype(BF)
        sent(c // 256).start()
    drow, erow = D // wide, E // wide
    rows = 2 * drow
    pitch = -(-rows // 8) * 8
    for c in range(0, D, 128):
        g = dot_tn(normed[win, c : c + 128], ggrad[0:WIN, :])
        lay_rows(g, c, drow, lambda k, r, v: put(stage, pitch, k, r, 0, v))
    for c in range(0, E, 256):
        g = dot_tn(gated[0:WIN, c : c + 256], branch_grad())
        half = erow // 2
        lay_rows(g, c, half, lambda k, r, v: put(stage, pitch, k // 2, drow + r, (k % 2) * D, v))
    shared(rows, pitch)
    for c in range(0, D, 128):
        cols = slice(c, c + 128)
        blk[c // 128, 0:WIN, :] = dot(gated[0:WIN, :], wo[:, cols])
        gpart[:, cols] = dot_nt(ggrad[0:WIN, :], w2[cols, :])

    def out_tile(i, _):
        base = pl.multiple_of(i * 32, 32)
        at = pl.multiple_of(wbase + base, 32)
        res, live = residual_tile(meta, tokf, etab, at, 32)
        for c in range(3):
            blk[c, pl.ds(base, 32), :] = res[c] + live * blk[c, pl.ds(base, 32), :]
        return 0

    lax.fori_loop(0, WIN // 32, out_tile, 0)


WINDOWS = ((0, 0), (1, WIN - HALF - 8))


def lay_cotangent(stream, cot, cotw):
    cotw[:, 0:WIN, :] = jnp.zeros((3, WIN, 128), F32)
    for s, off in WINDOWS:

        @pl.when(stream == s)
        def _():
            for c in range(3):
                cotw[c, off : off + HALF, :] = cot[:, c * 128 : c * 128 + 128].astype(F32)


def take_half(stream, src, out, sem):
    def copy(off, c):
        return pltpu.make_async_copy(
            src.at[c, off : off + HALF, :], out.at[:, 0, c * 128 : c * 128 + 128], sem.at[c]
        )

    for s, off in WINDOWS:

        @pl.when(stream == s)
        def _():
            for c in range(3):
                copy(off, c).start()

    def wait():
        for c in range(3):
            copy(0, c).wait()

    return wait


def put(ref, pitch, k, r, col, v):
    for c in range(0, v.shape[1], 128):
        at = (k * G6 + (col + c) // 128) * pitch + r
        ref[at : at + v.shape[0], :] = v[:, c : c + 128]


def lay_rows(v, start, size, store):
    at = 0
    while at < v.shape[0]:
        k, r = divmod(start + at, size)
        n = min(size - r, v.shape[0] - at)
        store(k, r, v[at : at + n])
        at += n


def unpack(pack, w2, wo, wide):
    drow, half = D // wide, E // wide // 2
    per = max(1, 16 // math.gcd(16, drow))
    for k in range(0, wide, per):
        v = [pack[k + i].astype(F32) for i in range(per)]
        w2[k * drow : (k + per) * drow, :] = jnp.concatenate([t[0:drow] for t in v], 0).astype(BF)
        pieces = []
        for t in v:
            pieces += [t[drow : drow + half, 0:D], t[drow : drow + half, D : 2 * D]]
        wo[2 * k * half : 2 * (k + per) * half, :] = jnp.concatenate(pieces, 0).astype(BF)


def bwd_kernel(wide, mine, *refs):
    refs = list(refs)
    count, offset, stride, tok, cot, normed, pack, stats, w1, st, res_h, other_h, x_h, act_h, dl_h, p_h, hs_in = refs[:17]
    if mine:
        block_h, tg_h, own_o, twin_o, g2_o, g2x_o = refs[17:23]
    else:
        block_h, tg_h, gw1, gsm, gg_o, g2_o = refs[17:23]
    (
        x, act, dl, p, w2, wo, gpart, mg, mgx, nrecv,
        lab, dm, dy, dyb, ub, bb, bbd, dbm, dcm, dd, zs, dacc, hse, hso, g0, g1, z0, z1, pb0, pb1, pc0, pc1, sel, sums,
        etab, gain_s, acc, sem, in_sem, out_sem, mgsend, mgrecv, swsend, swrecv, win_sem, *links,
    ) = refs[23:]
    if mine:
        g2s, g2r, gw1, gsm, pout, pin, out, got, gout, gin, g2send, g2recv, rsend, rrecv, osend, orecv = links
    stream, place = lax.axis_index("dir"), lax.axis_index("wide")
    wbase = pl.multiple_of(stream * WBASE, 32)
    loads = [
        pltpu.make_async_copy(h, v, in_sem.at[k])
        for k, (h, v) in enumerate(zip((x_h, act_h, dl_h, p_h), (x, act, dl, p)))
    ]
    windows = []
    for i, (h, v, at) in enumerate(((res_h, hse, wbase), (other_h, hso, 0))):
        for k in range(0, WIN, 256):
            n = min(256, WIN - k)
            rows = pl.ds(pl.multiple_of(at + k, 32), n)
            windows.append(
                pltpu.make_async_copy(h.at[rows, :], v.at[k // 256, 0:n, :], win_sem.at[i, k // 256])
            )
    for c in windows + loads:
        c.start()

    def window(ref, cols):
        rows = [ref[k // 256, 0 : min(256, WIN - k), cols] for k in range(0, WIN, 256)]
        return jnp.concatenate(rows, 0).astype(F32)

    if mine:
        greet(stream, place, wide)
    else:
        bar = pltpu.get_barrier_semaphore()
        pl.semaphore_signal(bar, inc=1, device_id=(1 - stream, place), device_id_type=MESH)
        pl.semaphore_wait(bar, 1)
    meta = views(count, offset, stream)
    partner = dict(device_id=(1 - stream, place), device_id_type=MESH)
    fill_embedding(stride, etab)
    fill_labels(meta, lab)
    tokf, cotw, blk = zs.at[0:3], zs.at[3:6], dd.at[0:3]
    lay_tokens(tok, tokf)
    unpack(pack, w2, wo, wide)

    def sent(k):
        cols = slice(k * 256, k * 256 + 256)
        return pltpu.make_async_remote_copy(
            src_ref=mg.at[:, cols], dst_ref=mgx.at[:, cols], send_sem=mgsend.at[k], recv_sem=mgrecv.at[k], **partner
        )

    g2 = []
    if mine:
        for k in range(1, wide):
            g2.append(
                pltpu.make_async_remote_copy(
                    src_ref=g2s.at[place ^ k], dst_ref=g2r.at[k], send_sem=g2send.at[k], recv_sem=g2recv.at[k],
                    device_id=(stream, place ^ k), device_id_type=MESH,
                )
            )

    def shared(rows, pitch):
        for k in range(wide):
            for c in range(G6):
                at = (k * G6 + c) * pitch
                cols = slice(c * 128, c * 128 + 128)
                if mine:
                    g2s[k, :, cols] = bb[at : at + rows, :].astype(BF)
                else:
                    g2_o[k, :, cols] = bb[at : at + rows, :]
        for c in g2:
            c.start()

    for c in windows:
        c.wait()
    middle(
        meta, wide, tokf, etab, cot, normed, lambda cols: window(hse, cols), lambda cols: window(hso, cols),
        w2, wo, cotw, ub, (dbm, dcm), dyb, blk, mg, gpart, bb, sent, shared,
    )
    block_out = take_half(stream, blk, block_h, out_sem.at[0])
    for c in loads:
        c.wait()

    def prep(rev):
        def tile(i, _):
            base = pl.multiple_of(i * 32, 32)
            rows = pl.ds(base, 32)
            here = lab[pl.ds(base + HALO, 32), :]
            before = lab[pl.ds(base + HALO + (1 if rev else -1), 32), :]
            cut = jnp.where(here == before, 0.0, CUT)
            spread_tile(p, ROW_C, bb, base)
            for c in range(G6):
                dm[c, rows, :] = dl[c, rows, :] + cut
            return 0

        lax.fori_loop(0, R // 32, tile, 0)

    @pl.when(stream == 0)
    def _():
        prep(False)

    @pl.when(stream == 1)
    def _():
        prep(True)

    col = lax.broadcasted_iota(jnp.int32, (128, 256), 1)
    row = lax.broadcasted_iota(jnp.int32, (128, 256), 0)
    spread_b = jnp.where(row == ROW_B + col % N, 1.0, 0.0).astype(BF)
    diag = (
        lax.broadcasted_iota(jnp.int32, (592, 256), 0) % N
        == lax.broadcasted_iota(jnp.int32, (592, 256), 1) // N
    )
    for h in range(2):
        rows = slice(h * 592, h * 592 + 592)
        bbd[rows, :] = jnp.where(diag, dot(p[rows, :].astype(BF), spread_b), 0.0).astype(BF)
    for k in range(3):
        sent(k).wait()
    block_out()
    sums[...] = jnp.zeros(sums.shape, F32)

    for s, lowref, highref in ((0, mg, mgx), (1, mgx, mg)):

        @pl.when(stream == s)
        def _():
            def lay(i, _):
                base = pl.multiple_of(i * 32, 32)
                lowat = pl.multiple_of(jnp.minimum(base, WIN - 32), 32)
                highat = pl.multiple_of(jnp.maximum(base - WBASE, 0), 32)
                for c in range(G6):
                    cols = slice(c * 128, c * 128 + 128)
                    lowrow = lowref[pl.ds(lowat, 32), cols].astype(F32)
                    highrow = highref[pl.ds(highat, 32), cols].astype(F32)
                    v = jnp.where(base < WIN, lowrow, 0.0) + jnp.where(base >= WBASE, highrow, 0.0)
                    dy[c, pl.ds(base, 32), :] = v
                    t = v * act[c, pl.ds(base, 32), :]
                    sums[0, :, cols] += t[0:8] + t[8:16] + t[16:24] + t[24:32]
                return 0

            lax.fori_loop(0, R // 32, lay, 0)

    i = lax.broadcasted_iota(jnp.int32, (32, 256), 0)
    j = lax.broadcasted_iota(jnp.int32, (32, 256), 1)
    sel[...] = jnp.where(i == jnp.where(i < N, j // N, N + j % N), 1.0, 0.0).astype(BF)
    dacc[...] = jnp.zeros(dacc.shape, F32)
    hs, gs, zz, pb, pc = (hse, hso), (g0, g1), (z0, z1), (pb0, pb1), (pc0, pc1)

    def load(k, i):
        slot = i % RING
        return pltpu.make_async_copy(hs_in.at[k, i], hs[k].at[slot], sem.at[k, slot])

    def scan(rev):
        rate = [
            -jnp.exp(st[ROW_DECAY : ROW_DECAY + N, c * 128 : c * 128 + 128]) * LOG2E
            for c in range(G6)
        ]
        block_diag = (
            lax.broadcasted_iota(jnp.int32, (N, 256), 0)
            == lax.broadcasted_iota(jnp.int32, (N, 256), 1) // N
        )

        def block_of(t):
            return NB - 1 - t if rev else t

        def drive_dot(t, k, c):
            rows = rows16(block_of(t))
            y = dot(bbd[rows, :], gs[k][:, c * 128 : c * 128 + 256])
            dd[c, rows, :] = y[:, :128]
            dd[c + 1, rows, :] = y[:, 128:]

        def step_dot(t, k, c, first):
            rows = rows16(block_of(t))
            y = dot(sel[...], zz[k][:, c * 128 : c * 128 + 256])
            zs[c, rows, :] = y[:N, :128]
            zs[c + 1, rows, :] = y[:N, 128:]
            dacc[c] += jnp.where(first, 0.0, y[N:, :128])
            dacc[c + 1] += jnp.where(first, 0.0, y[N:, 128:])

        ones = jnp.ones((N, 128), BF)

        def b_dot(t, k):
            rows = rows16(block_of(t))
            dbm[rows, :] = jnp.where(block_diag, dot_nt(ones, pb[k][...]), 0.0).astype(BF)

        def c_dot(t, k):
            rows = rows16(block_of(t))
            dcm[rows, :] = jnp.where(block_diag, dot_nt(ones, pc[k][...]), 0.0).astype(BF)

        def block(t, k, slot, pslot, carry, late):
            b = block_of(t)
            carry = list(carry)
            late = list(late)
            start = 0 if rev else 15
            now = [hs[k][slot, start * N : start * N + N, c * 128 : c * 128 + 128] for c in range(G6)]
            for n, j in enumerate(range(16) if rev else range(15, -1, -1)):
                if n % 2 == 0 and late:
                    late.pop(0)()
                q = b * 16 + j
                cb = bb[pl.ds(pl.multiple_of(q * N, N), N), :]
                jp = j + 1 if rev else j - 1
                if 0 <= jp < 16:
                    old_ref, old_slot = hs[k], slot
                else:
                    jp = 0 if rev else 15
                    old_ref, old_slot = hs[1 - k], pslot
                sum_b = sum_c = None
                for c in range(G6):
                    cols = slice(c * 128, c * 128 + 128)
                    w = dm[c, pl.ds(q, 1), :] * rate[c]
                    fade = jnp.exp2(w)
                    up = dy[c, pl.ds(q, 1), :]
                    g = cb * up + carry[c]
                    carry[c] = fade * g
                    old = old_ref[old_slot, jp * N : jp * N + N, cols]
                    low = g.astype(BF)
                    gs[k][j * N : j * N + N, cols] = low
                    zz[k][j * N : j * N + N, cols] = (w * carry[c]).astype(BF) * old
                    drive = dl[c, pl.ds(q, 1), :] * act[c, pl.ds(q, 1), :]
                    tb = low * jnp.broadcast_to(drive, (N, 128)).astype(BF)
                    tc = now[c] * jnp.broadcast_to(up, (N, 128)).astype(BF)
                    sum_b = tb if sum_b is None else sum_b + tb
                    sum_c = tc if sum_c is None else sum_c + tc
                    now[c] = old
                pb[k][j * N : j * N + N, :] = sum_b
                pc[k][j * N : j * N + N, :] = sum_c
            return tuple(carry)

        def pair(ii, carry):
            i = NP - 1 - ii
            slot = i % RING
            pslot = jnp.maximum(i - 1, 0) % RING

            @pl.when(i >= 1)
            def _():
                load(0, i - 1).wait()
                load(1, i - 1).wait()

            @pl.when(i >= 3)
            def _():
                load(0, i - 3).start()
                load(1, i - 3).start()

            one = 1 + i // 1048576
            for k in (1, 0):
                t = 2 * i + k
                after = jnp.minimum(t + 1, NB - 1)
                first = t + 1 > NB - 1
                late = [functools.partial(b_dot, after, 1 - k), functools.partial(c_dot, after, 1 - k)]
                late += [functools.partial(drive_dot, after, 1 - k, c) for c in (0, 2, 4)]
                late += [functools.partial(step_dot, after, 1 - k, c, first) for c in (0, 2, 4)]
                ps = slot if k == 1 else pslot
                carry = lax.fori_loop(
                    0, one, lambda _, cc, t=t, k=k, ps=ps, late=late: block(t, k, slot, ps, cc, late), carry
                )
            return carry

        for i in range(NP - 1, NP - 4, -1):
            load(0, i).start()
            load(1, i).start()
        load(0, NP - 1).wait()
        load(1, NP - 1).wait()
        for ref in (g0, z0, pb0, pc0):
            ref[...] = jnp.zeros(ref.shape, BF)
        lax.fori_loop(0, NP, pair, tuple(jnp.zeros((N, 128), F32) for _ in range(G6)))
        for c in (0, 2, 4):
            drive_dot(0, 0, c)
            step_dot(0, 0, c, False)
        b_dot(0, 0)
        c_dot(0, 0)

    @pl.when(stream == 0)
    def _():
        scan(False)

    @pl.when(stream == 1)
    def _():
        scan(True)

    def step_tile(i, _):
        base = pl.multiple_of(i * 32, 32)
        rows = pl.ds(base, 32)
        for c in range(G6):
            cols = slice(c * 128, c * 128 + 128)
            delta, a, d = dl[c, rows, :], act[c, rows, :], dd[c, rows, :]
            near = 1.0 - delta * (0.5 - delta * (1.0 / 6.0 - delta * (1.0 / 24.0)))
            ratio = jnp.where(delta < 0.03, near, (1.0 - jnp.exp(-delta)) / delta)
            pre = ratio * (zs[c, rows, :] * LN2 + a * d * delta)
            ub[rows, cols] = pre.astype(BF)
            dm[c, rows, :] = delta * d + st[ROW_CHAN + 6 : ROW_CHAN + 7, cols] * dy[c, rows, :]
            sums[1, :, cols] += pre[0:8] + pre[8:16] + pre[16:24] + pre[24:32]
        return 0

    lax.fori_loop(0, R // 32, step_tile, 0)
    pgs = bbd.at[:, 0:128]
    w_step = st[ROW_STEP : ROW_STEP + RANK, :].astype(BF)
    w_b = jnp.concatenate([st[ROW_B : ROW_B + N, :]] * N, 0).astype(BF)
    w_c = jnp.concatenate([st[ROW_C : ROW_C + N, :]] * N, 0).astype(BF)
    w_s = st[0:RANK, :].astype(BF)
    for h in range(2):
        rows = slice(h * 592, h * 592 + 592)
        sg = dot_nt(ub[rows, :], w_step).astype(BF)
        pgs[rows, :] = jnp.concatenate([sg, jnp.zeros((592, 128 - RANK), BF)], 1)
        for c in range(0, G6, 2):
            cols = slice(c * 128, c * 128 + 256)
            y = dot(sg, w_s[:, cols]) + dot(dbm[rows, :], w_b[:, cols]) + dot(dcm[rows, :], w_c[:, cols])
            dm[c, rows, :] += y[:, :128]
            dm[c + 1, rows, :] += y[:, 128:]
    dc = dd
    dc[:, 0:HALO, :] = jnp.zeros((G6, HALO, 128), F32)
    dc[:, HALO + R : XR, :] = jnp.zeros((G6, HALO, 128), F32)

    def conv(rev):
        def first(i, _):
            base = pl.multiple_of(i * 32, 32)
            for c in range(G6):
                cols = slice(c * 128, c * 128 + 128)
                total, lagged = conv_tile(x, lab, st, c, base, 32, rev)
                sig = sigmoid(total)
                v = dm[c, pl.ds(base, 32), :] * sig * (1.0 + total * (1.0 - sig))
                dc[c, pl.ds(base + HALO, 32), :] = v
                sums[2, :, cols] += v[0:8] + v[8:16] + v[16:24] + v[24:32]
                for j in range(4):
                    t = v * lagged[j]
                    sums[3 + j, :, cols] += t[0:8] + t[8:16] + t[16:24] + t[24:32]
            return 0

        def second(i, _):
            base = pl.multiple_of(i * 32, 32)
            here = lab[pl.ds(base + HALO, 32), :]
            for c in range(G6):
                cols = slice(c * 128, c * 128 + 128)
                v = dc[c, pl.ds(base + HALO, 32), :] * st[ROW_CHAN : ROW_CHAN + 1, cols]
                for j in (1, 2, 3):
                    at = base + HALO + (-j if rev else j)
                    same = lab[pl.ds(at, 32), :] == here
                    later = jnp.where(same, dc[c, pl.ds(at, 32), :], 0.0)
                    v = v + later * st[ROW_CHAN + j : ROW_CHAN + j + 1, cols]
                dyb[pl.ds(base, 32), cols] = v.astype(BF)
            return 0

        lax.fori_loop(0, R // 32, first, 0)
        lax.fori_loop(0, R // 32, second, 0)

    @pl.when(stream == 0)
    def _():
        conv(False)

    @pl.when(stream == 1)
    def _():
        conv(True)

    theirs = pl.ds(pl.multiple_of((1 - stream) * WBASE, 32), WIN)
    nsend = mg.at[:, 0:D]
    nsend[...] = dot_nt(dyb[theirs, :], w1[...]).astype(BF)
    nswap = pltpu.make_async_remote_copy(
        src_ref=nsend, dst_ref=nrecv, send_sem=swsend.at[0], recv_sem=swrecv.at[0], **partner
    )
    nswap.start()
    for c in range(0, D, 128):
        gw1[c : c + 128, :] = dot_tn(normed[:, c : c + 128], dyb[...])
    if mine:
        for s in range(2):

            @pl.when(stream == s)
            def _():
                pout[...] = gw1[:, (1 - s) * D : (2 - s) * D].astype(BF)

        pre = pltpu.make_async_remote_copy(
            src_ref=pout, dst_ref=pin, send_sem=swsend.at[1], recv_sem=swrecv.at[1], **partner
        )
        pre.start()
    low = p[0:R, :].astype(BF)
    gstep = dot_tn(low, ub[...])[0:RANK]

    def activation(i, _):
        rows = pl.ds(pl.multiple_of(i * 32, 32), 32)
        for c in range(G6):
            ub[rows, c * 128 : c * 128 + 128] = act[c, rows, :].astype(BF)
        return 0

    lax.fori_loop(0, R // 32, activation, 0)
    top = dot_tn(pgs[...], ub[...])
    gb = dot_tn(dbm[...], ub[...])
    gc = dot_tn(dcm[...], ub[...])
    gb = sum(gb[k * N : k * N + N] for k in range(N))
    gc = sum(gc[k * N : k * N + N] for k in range(N))
    gdecay = jnp.concatenate([dacc[c] for c in range(G6)], 1) * LN2

    def total(k):
        return jnp.sum(sums[k], axis=0, keepdims=True)

    chan = [total(3 + k) for k in range(4)] + [total(2), total(1), total(0)]
    fine = [jnp.sum(stats[k], axis=0, keepdims=True) * (1.0 / VIEW_TOK) for k in range(2)]
    coarse = [v.astype(BF).astype(F32) for v in fine]
    fine = [a - b for a, b in zip(fine, coarse)]
    chan = jnp.concatenate(chan + [jnp.zeros((1, E), F32)] + coarse + fine, 0)
    gt = jnp.concatenate(
        [top[0:RANK], gb, gc, gstep, gdecay, chan, jnp.zeros((128 - 108, E), F32)], 0
    )
    gsm[...] = gt.T
    if mine:
        pre.wait()
        fill_owners(stream, wide, gsm, gw1, pin, out)
        shares = [
            pltpu.make_async_remote_copy(
                src_ref=out.at[place ^ k], dst_ref=got.at[k], send_sem=rsend.at[k], recv_sem=rrecv.at[k],
                device_id=(stream, place ^ k), device_id_type=MESH,
            )
            for k in range(1, wide)
        ]
        for c in shares:
            c.start()
    gpart[...] += dot_nt(dyb[pl.ds(wbase, WIN), :], w1[...])
    nswap.wait()
    ending(meta, wide, tok, etab, cot, nrecv, gpart, st, zs.at[0:3], zs.at[3:6], dd.at[0:3], gain_s, acc)
    token_out = take_half(stream, dd.at[0:3], tg_h, out_sem.at[1])
    if not mine:
        gg_o[...] = acc[...]
        token_out()
        return
    gain = jnp.sum(acc[...], axis=0, keepdims=True)
    each = D // wide
    for k in range(wide):
        piece = jnp.broadcast_to(gain[:, k * each : (k + 1) * each], (16, each))
        gout[k] = jnp.concatenate([piece, jnp.zeros((16, 128 - each), F32)], 1).astype(BF)
    gains = [
        pltpu.make_async_remote_copy(
            src_ref=gout.at[place ^ k], dst_ref=gin.at[k], send_sem=osend.at[k], recv_sem=orecv.at[k],
            device_id=(stream, place ^ k), device_id_type=MESH,
        )
        for k in range(1, wide)
    ]
    for c in gains:
        c.start()
    for c in g2:
        c.wait()
    for r in range(0, g2_o.shape[0], 24):
        rows = slice(r, r + 24)
        total = g2s[place].astype(F32)[rows]
        for k in range(1, wide):
            total = total + g2r[k].astype(F32)[rows]
        g2_o[rows, :] = total
    g2swap = pltpu.make_async_remote_copy(
        src_ref=g2_o, dst_ref=g2x_o, send_sem=swsend.at[2], recv_sem=swrecv.at[2], **partner
    )
    g2swap.start()
    for c in shares:
        c.wait()
    total = out[place].astype(F32)
    for k in range(1, wide):
        total = total + got[k].astype(F32)
    own_o[...] = total
    for c in gains:
        c.wait()
    total = gout[place].astype(F32)
    for k in range(1, wide):
        total = total + gin[k].astype(F32)
    own_o[PACK - 8 : PACK, :] = total[0:8]
    last = pltpu.make_async_remote_copy(
        src_ref=own_o, dst_ref=twin_o, send_sem=swsend.at[3], recv_sem=swrecv.at[3], **partner
    )
    last.start()
    token_out()
    g2swap.wait()
    last.wait()


def ending(meta, wide, tok, etab, cot, other, gpart, st, tokf, cotw, out, gain_s, acc):
    stream = meta[4]
    wbase = pl.multiple_of(stream * WBASE, 32)
    lay_tokens(tok, tokf)
    lay_cotangent(stream, cot, cotw)
    gain_s[...] = gain_row(st, wide)
    acc[...] = jnp.zeros(acc.shape, F32)
    lo = stream * HALF

    def tile(i):
        base = i * 32 if isinstance(i, int) else pl.multiple_of(i * 32, 32)
        at = pl.multiple_of(wbase + base, 32)
        rows = pl.ds(base, 32)
        res, _l = residual_tile(meta, tokf, etab, at, 32)
        scale = row_scale(res)
        r = at + lax.broadcasted_iota(jnp.int32, (32, 128), 0)
        mine = (r >= lo) & (r < lo + HALF)
        ng, un = [], []
        for c in range(3):
            cols = slice(c * 128, c * 128 + 128)
            v = gpart[rows, cols] + other[rows, cols].astype(F32)
            unit = res[c] * scale
            t = jnp.where(mine, v * unit, 0.0)
            acc[:, cols] += t[0:8] + t[8:16] + t[16:24] + t[24:32]
            ng.append(v * gain_s[0:1, cols])
            un.append(unit)
        mean = sum(jnp.sum(a * b, axis=1, keepdims=True) for a, b in zip(ng, un)) * (1.0 / D)
        for c in range(3):
            out[c, rows, :] = cotw[c, rows, :] + scale * (ng[c] - un[c] * mean)

    pairs(WIN // 32, tile)


def backward(wide, mine, *args):
    S = jax.ShapeDtypeStruct
    V = pltpu.VMEM
    dma = pltpu.SemaphoreType.DMA
    big = V((G6, R, 128), F32)
    rows = 2 * D // wide
    half = S((HALF, 1, D), F32)
    if mine:
        outs = [S((PACK, 128), F32), S((PACK, 128), F32), S((rows, E), F32), S((rows, E), F32)]
        links = [
            V((wide, rows, E), BF), V((wide, rows, E), BF), V((D, E), F32), V((E, 128), F32), V((D, D), BF), V((D, D), BF),
            V((wide, PACK, 128), BF), V((wide, PACK, 128), BF), V((wide, 16, 128), BF), V((wide, 16, 128), BF),
        ] + [dma((wide,))] * 6
    else:
        outs = [S((D, E), F32), S((E, 128), F32), S((8, D), F32), S((wide, rows, E), F32)]
        links = []
    return pl.pallas_call(
        functools.partial(bwd_kernel, wide, mine),
        out_shape=[half, half] + outs,
        in_specs=[SMEM] * 3 + [VMEM] * 7 + [ANY] * 7,
        out_specs=[ANY] * 2 + [VMEM] * 4,
        scratch_shapes=[
            V((G6, XR, 128), F32), big, big, V((1280, 128), F32),
            V((D, E), BF), V((E, D), BF), V((WIN, D), F32), V((WIN, E), BF), V((WIN, E), BF), V((WIN, D), BF),
            V((XR, 128), jnp.int32), big, big, V((R, E), BF), V((R, E), BF), V((R * N, 128), F32),
            V((R, 256), BF), V((R, 256), BF), V((R, 256), BF), V((G6, XR, 128), F32), big, V((G6, N, 128), F32),
            V((RING, 256, E), BF), V((RING, 256, E), BF),
            V((256, E), BF), V((256, E), BF), V((256, E), BF), V((256, E), BF),
            V((256, 128), BF), V((256, 128), BF), V((256, 128), BF), V((256, 128), BF), V((32, 256), BF), V((7, 8, E), F32),
            V((8, D), F32), V((8, D), F32), V((8, D), F32),
            dma((2, RING)), dma((4,)), dma((2, 3)), dma((3,)), dma((3,)), dma((4,)), dma((4,)), dma((2, 3)),
        ]
        + links,
        compiler_params=pltpu.CompilerParams(
            vmem_limit_bytes=63 * 2**20, collective_id=4, has_side_effects=True
        ),
        cost_estimate=pl.CostEstimate(flops=int(9e10), bytes_accessed=1 << 20, transcendentals=0),
        name="backward",
    )(*args)


PACK = 128
ROWS_S = 48
ROWS_W = 24


def greet(d, w, wide):
    bar = pltpu.get_barrier_semaphore()
    for k in range(1, wide):
        pl.semaphore_signal(bar, inc=1, device_id=(d, w ^ k), device_id_type=MESH)
    pl.semaphore_signal(bar, inc=1, device_id=(1 - d, w), device_id_type=MESH)
    pl.semaphore_wait(bar, wide)


def fill_shares(d, given, stage, first, second):
    inp, out, state, step, decay, chan, gain = given
    stage[...] = jnp.zeros(stage.shape, F32)
    stage[ROW_STEP:ROW_DECAY, 0:ROWS_S] = step[0]
    stage[ROW_DECAY:ROW_CHAN, 0:ROWS_S] = decay[0]
    for k in range(7):
        stage[ROW_CHAN + k : ROW_CHAN + k + 1, 0:ROWS_S] = chan[k]
    stage[ROW_GAIN : ROW_GAIN + 1, 0:ROWS_W] = gain[...]
    small = stage[...].T[0:ROWS_S]
    stage[0:ROWS_S, 0:ROW_STEP] = state[0]
    col = lax.broadcasted_iota(jnp.int32, (ROWS_S, 128), 1)
    parts = [jnp.where(col < ROW_STEP, stage[0:ROWS_S, :], small)]
    for c in range(3):
        low, high = inp[:, c * 128 : c * 128 + 128], inp[:, D + c * 128 : D + c * 128 + 128]
        parts.append(jnp.where(d == 0, low, high))
    parts.append(jnp.zeros((PACK - ROWS_S - 3 * ROWS_W, 128), F32))
    first[...] = jnp.concatenate(parts, 0).astype(BF)
    pair = jnp.concatenate([out[0:ROWS_W, :], out[ROWS_W : 2 * ROWS_W, :]], 1)
    second[...] = jnp.concatenate([inp[:, E:], pair], 0).astype(BF)


def take_shares(d, wide, got, w1, s_ref):
    for k in range(0, wide, 2):
        s_ref[k * ROWS_S : (k + 2) * ROWS_S, :] = jnp.concatenate([got[k, 0:ROWS_S], got[k + 1, 0:ROWS_S]], 0)
        v = [got[k + i, ROWS_S:PACK, :].astype(F32) for i in range(2)]
        for c in range(3):
            piece = [t[c * ROWS_W : (c + 1) * ROWS_W] for t in v]
            piece = jnp.concatenate(piece, 0).astype(BF)
            for s in range(2):

                @pl.when(d == s)
                def _():
                    at = s * D + c * 128
                    w1[k * ROWS_W : (k + 2) * ROWS_W, at : at + 128] = piece


def fill_owners(d, wide, gs, gw1, pin, out):
    for k in range(wide):
        rows = slice(k * ROWS_W, (k + 1) * ROWS_W)
        parts = [gs[k * ROWS_S : (k + 1) * ROWS_S, :]]
        at = k * ROWS_W % 16
        base = k * ROWS_W - at
        arrived = pin[base : base + 32, :].astype(F32)[at : at + ROWS_W]
        for c in range(3):
            low, high = gw1[rows, c * 128 : c * 128 + 128], gw1[rows, D + c * 128 : D + c * 128 + 128]
            parts.append(jnp.where(d == 0, low, high) + arrived[:, c * 128 : c * 128 + 128])
        parts.append(jnp.zeros((PACK - ROWS_S - 3 * ROWS_W, 128), F32))
        out[k] = jnp.concatenate(parts, 0).astype(BF)


def gather_plain(inp, state, step, decay, chan, gain):
    rows = state.shape[1]
    column = jnp.concatenate([gain, jnp.zeros((rows - gain.shape[0],), F32)])[:, None]
    small = [state[0], step[0].T, decay[0].T, chan[0].T, column, jnp.zeros((rows, 127 - ROW_GAIN), F32)]
    small = jnp.concatenate(small, 1).astype(BF)
    return (
        lax.all_gather(inp[:, :E].astype(BF), "wide", axis=0, tiled=True),
        lax.all_gather(small, "wide", axis=0, tiled=True),
    )


def reduce_plain(gw1, gs, gg):
    def total(v):
        return lax.psum_scatter(v, "wide", scatter_dimension=0, tiled=True)

    return total(lax.psum(gw1, "dir")), total(gs), total(lax.psum(gg.sum(0), "dir"))


def adam_step(weight, gradient, first_moment, second, step_rate, decay_rate):
    first_moment = BETA_ONE * first_moment + (1.0 - BETA_ONE) * gradient
    second = BETA_TWO * second + (1.0 - BETA_TWO) * gradient * gradient
    first_hat = first_moment / (1.0 - BETA_ONE**STEP)
    second_hat = second / (1.0 - BETA_TWO**STEP)
    weight = weight - step_rate * (
        first_hat / (jnp.sqrt(second_hat) + EPS_ADAM) + decay_rate * weight
    )
    return (weight, first_moment, second)


def update_kernel(got, twin, g2, g2x, *refs):
    stream = lax.axis_index("dir")
    masters, outs = refs[:21], refs[21:]

    def step(k, gradient, at=(slice(None),), out=None):
        new = adam_step(
            masters[3 * k][at], gradient, masters[3 * k + 1][at], masters[3 * k + 2][at], RATES[k], DECAYS[k]
        )
        for i in range(3):
            outs[1 + 3 * k + i][at] = new[i]

    mine, theirs = got[...], twin[...]
    low, high = jnp.where(stream == 0, mine, theirs), jnp.where(stream == 0, theirs, mine)
    for h, v in enumerate((low, high)):
        for c in range(3):
            at = ROWS_S + c * ROWS_W
            col = h * D + c * 128
            step(0, v[at : at + ROWS_W], (slice(None), slice(col, col + 128)))
    shared = g2[...] + g2x[...]
    step(0, shared[0:ROWS_W], (slice(None), slice(E, 2 * E)))
    step(1, shared[ROWS_W:, 0:D], (slice(0, ROWS_W), slice(None)))
    step(1, shared[ROWS_W:, D:], (slice(ROWS_W, 2 * ROWS_W), slice(None)))
    t = mine.T
    step(2, mine[PACK - 8 : PACK - 7, 0:ROWS_W] + theirs[PACK - 8 : PACK - 7, 0:ROWS_W])
    step(3, mine[0:ROWS_S, 0:ROW_STEP], (0,))
    step(4, t[ROW_STEP:ROW_DECAY, 0:ROWS_S], (0,))
    step(5, t[ROW_DECAY:ROW_CHAN, 0:ROWS_S], (0,))
    for k in range(7):
        step(6, t[ROW_CHAN + k : ROW_CHAN + k + 1, 0:ROWS_S], (k,))
    outs[0][0] = t[ROW_STATS : ROW_STATS + 2, 0:ROWS_S] + t[ROW_STATS + 2 : ROW_STATS + 4, 0:ROWS_S]


def update(got, twin, g2, g2x, masters):
    S = jax.ShapeDtypeStruct
    masters = list(masters)
    masters[6:9] = [v[None] for v in masters[6:9]]
    masters[18:21] = [jnp.transpose(v, (1, 0, 2)) for v in masters[18:21]]
    outs = pl.pallas_call(
        update_kernel,
        out_shape=[S((1, 2, ROWS_S), F32)] + [S(v.shape, F32) for v in masters],
        in_specs=[VMEM] * 25,
        out_specs=[VMEM] * 22,
        name="update",
    )(got, twin, g2, g2x, *masters)
    stats, outs = outs[0], list(outs[1:])
    outs[6:9] = [v[0] for v in outs[6:9]]
    outs[18:21] = [jnp.transpose(v, (1, 0, 2)) for v in outs[18:21]]
    return stats, outs


def update_plain(gw1, gs, gg, g2, masters):
    drow = masters[0].shape[0]
    g1, small, gain = reduce_plain(gw1, gs, gg)
    t = small.T
    grads = (
        jnp.concatenate([g1, g2[:drow]], 1),
        jnp.concatenate([g2[drow:, :D], g2[drow:, D:]], 0),
        gain,
        small[None, :, :ROW_STEP],
        t[None, ROW_STEP:ROW_DECAY],
        t[None, ROW_DECAY:ROW_CHAN],
        t[None, ROW_CHAN:ROW_GAIN],
    )
    outs = []
    for k, g in enumerate(grads):
        w, f, s2 = masters[3 * k : 3 * k + 3]
        outs += adam_step(w, g, f, s2, RATES[k], DECAYS[k])
    return (t[ROW_STATS : ROW_STATS + 2] + t[ROW_STATS + 2 : ROW_STATS + 4])[None], outs


def local(tokens, cotangent, view_counts, view_strides, view_offsets, *masters):
    wide = lax.axis_size("wide")
    in_proj, out_proj, gain = masters[0], masters[3], masters[6]
    erow = out_proj.shape[0]
    mine = E // wide == ROWS_S and D // wide == ROWS_W
    about = (view_counts, view_offsets, view_strides)
    tok, cot = tokens[0], cotangent[0]
    small = masters[9], masters[12], masters[15]
    if mine:
        chan = jnp.transpose(masters[18], (1, 0, 2))
        *kept, pack, stats, hs = forward(wide, mine, *about, tok, in_proj, out_proj, *small, chan, gain[None])
    else:
        pair = jnp.concatenate([out_proj[: erow // 2], out_proj[erow // 2 :]], 1)
        pack = lax.all_gather(jnp.concatenate([in_proj[:, E:], pair], 0).astype(BF), "wide", axis=0)
        given = gather_plain(in_proj, *small, masters[18], gain)
        *kept, stats, hs = forward(wide, mine, *about, tok, *given)
    normed, x, act, dl, p, st, res, other, w1 = kept
    block, token_grad, *sums = backward(
        wide, mine, *about, tok, cot, normed, pack, stats, w1, st, res, other, x, act, dl, p, hs
    )
    if mine:
        stats, outs = update(*sums, masters)
    else:
        gw1, gs, gg, g2 = sums
        g2 = lax.psum(lax.psum_scatter(g2, "wide", scatter_dimension=0, tiled=True)[0], "dir")
        stats, outs = update_plain(gw1, gs, gg, g2, masters)
    return (jnp.transpose(block, (1, 0, 2)), jnp.transpose(token_grad, (1, 0, 2)), stats, *outs)


def solution(mesh):
    row, col = P("wide", None), P("dir", None, "wide")
    mat = P("dir", "wide", None)
    weights = [row] * 6 + [P("wide")] * 3 + [mat] * 3 + [col] * 9
    return jax.shard_map(
        local,
        mesh=mesh,
        in_specs=(
            P("wide", None, None), P("wide", "dir", None), P("wide"), row, row, *weights,
        ),
        out_specs=(P("wide", "dir", None), P("wide", "dir", None), col, *weights),
        check_vma=False,
    )
```

```python
import functools
import math

import jax
import jax.numpy as jnp
from jax import lax
from jax.experimental import pallas as pl
from jax.experimental.pallas import tpu as pltpu
from jax.sharding import PartitionSpec as P

PATCHES = 196
STEP = 10
VIEW_TOK = 392
EPS_NORM = 1e-06
BETA_ONE = 0.9
BETA_TWO = 0.95
EPS_ADAM = 1e-08
RATES = (0.15, 0.1, 2.5, 0.12, 0.2, 1.0, 2.5)
DECAYS = (0.1, 0.1, 0.0, 0.1, 0.1, 0.0, 0.0)

F32 = jnp.float32
BF = jnp.bfloat16
LN2 = math.log(2.0)
LOG2E = 1.0 / LN2

SLOTS = 1176
R = 1184
NB = R // 16
NP = NB // 2
HALF = 588
WIN = 608
WBASE = 576
D = 384
E = 768
G6 = E // 128
N = 16
RANK = 24
HALO = 8
XR = HALO + R + HALO
RING = 4
CUT = 1e4
SENDS = WIN // 32
MESH = pl.DeviceIdType.MESH
ROW_B, ROW_C, ROW_STEP, ROW_DECAY, ROW_CHAN, ROW_GAIN, ROW_STATS = 24, 40, 56, 80, 96, 103, 104
NT = (((1,), (1,)), ((), ()))
TN = (((0,), (0,)), ((), ()))
VMEM = pl.BlockSpec(memory_space=pltpu.VMEM)
SMEM = pl.BlockSpec(memory_space=pltpu.SMEM)
ANY = pl.BlockSpec(memory_space=pl.ANY)


def dot(a, b):
    return jnp.dot(a, b, preferred_element_type=F32)


def dot_nt(a, b):
    return lax.dot_general(a, b, NT, preferred_element_type=F32)


def dot_tn(a, b):
    return lax.dot_general(a, b, TN, preferred_element_type=F32)


def sigmoid(v):
    return 0.5 * jnp.tanh(0.5 * v) + 0.5


def rows16(b, n=16):
    return pl.ds(pl.multiple_of(b * 16, 16), n)


def labels_of(meta, r):
    lab = jnp.full(r.shape, -1, jnp.int32)
    late = jnp.zeros(r.shape, jnp.int32)
    for k in range(3):
        start = meta[1 + k]
        inside = (r >= start) & (r < start + VIEW_TOK) & (k < meta[0])
        lab = jnp.where(inside, k, lab)
        late = jnp.where(inside, jnp.where(r >= start + PATCHES, 1, 0), late)
    lab = jnp.where(r < 0, -2, lab)
    lab = jnp.where(r >= SLOTS, -3, lab)
    return lab, late


def residual_tile(meta, tok, etab, base, n):
    r = base + lax.broadcasted_iota(jnp.int32, (n, 128), 0)
    lab, late = labels_of(meta, r)
    live = jnp.where(lab >= 0, 1.0, 0.0)
    out = []
    for c in range(3):
        cols = slice(c * 128, c * 128 + 128)
        emb = jnp.where(lab >= 0, etab[3:4, cols], 0.0)
        for k in range(3):
            emb = jnp.where((lab == k) & (late == 1), etab[k : k + 1, cols], emb)
        out.append(tok[c, pl.ds(base, n), :] + emb)
    return out, live


def lay_tokens(tok, tokf):
    for c in range(3):
        tokf[c, 0:SLOTS, :] = tok[:, c * 128 : c * 128 + 128].astype(F32)
        tokf[c, SLOTS:R, :] = jnp.zeros((R - SLOTS, 128), F32)


def row_scale(res):
    total = sum(jnp.sum(v * v, axis=1, keepdims=True) for v in res)
    return lax.rsqrt(total * (1.0 / D) + EPS_NORM)


def fill_labels(meta, lab_ref):
    for base in range(0, XR, 8):
        r = base - HALO + lax.broadcasted_iota(jnp.int32, (8, 128), 0)
        lab_ref[base : base + 8, :] = labels_of(meta, r)[0]


def gain_row(st_ref, wide):
    per = E // wide
    own = D // wide
    i = lax.broadcasted_iota(jnp.int32, (E, D), 0)
    j = lax.broadcasted_iota(jnp.int32, (E, D), 1)
    pick = jnp.where(i == (j // own) * per + j % own, 1.0, 0.0).astype(BF)
    src = jnp.broadcast_to(st_ref[ROW_GAIN : ROW_GAIN + 1, :], (16, E)).astype(BF)
    return dot(src, pick)[0:8]


def turn(p_ref, lane, out_ref):
    for sb in range(-(-R // 128)):
        v = p_ref[sb * 128 : sb * 128 + 128, :].T[lane : lane + N]
        for k in range(8):
            if sb * 8 + k < NB:
                out_ref[sb * 8 + k] = v if k == 0 else pltpu.roll(v, 128 - 16 * k, 1)


def spread_tile(turned, b, out_ref):
    v = turned[b]
    for j in range(16):
        out_ref[pl.ds(pl.multiple_of((b * 16 + j) * N, N), N), :] = jnp.broadcast_to(v[:, j : j + 1], (N, 128))


def pairs(count, body):
    def two(i, _):
        body(2 * i)
        body(2 * i + 1)
        return 0

    lax.fori_loop(0, count // 2, two, 0)
    if count % 2:
        body(count - 1)


def conv_tile(x_ref, lab_ref, chan, c, base, n, rev):
    cols = slice(c * 128, c * 128 + 128)
    here = lab_ref[pl.ds(base + HALO, n), :]
    lagged = [x_ref[c, pl.ds(base + HALO, n), :]]
    for j in (1, 2, 3):
        at = base + HALO + (j if rev else -j)
        same = lab_ref[pl.ds(at, n), :] == here
        lagged.append(jnp.where(same, x_ref[c, pl.ds(at, n), :], 0.0))
    total = chan[4:5, cols]
    for j in range(4):
        total = total + chan[j : j + 1, cols] * lagged[j]
    return total, lagged


def views(count, offset, stream):
    return [count[0], offset[0, 0], offset[0, 1], offset[0, 2], stream]


def fill_embedding(stride, etab):
    lane = lax.broadcasted_iota(jnp.int32, (8, D), 1)
    row = lax.broadcasted_iota(jnp.int32, (8, D), 0)
    half = D // 2
    j = jnp.where(lane < half, lane, lane - half).astype(F32)
    freq = jnp.exp(-math.log(10000.0) * j / half)
    clock = jnp.zeros((8, D), F32)
    for k in range(3):
        clock = jnp.where(row == k, stride[0, k].astype(F32), clock)
    angle = clock * freq
    etab[...] = jnp.where(lane < half, jnp.sin(angle), jnp.cos(angle))


def fwd_kernel(wide, mine, *refs):
    refs = list(refs)
    count, offset, stride, tok = refs[:4]
    given, refs = refs[4 : 4 + (7 if mine else 2)], refs[4 + (7 if mine else 2) :]
    (
        normed_h, x_h, act_h, dl_h, p_h, st_h, res_h, other_h, w1_h, *pack_h, stats_o, hs_o,
    ) = refs[: 12 if mine else 11]
    (
        normed_o, x_o, act_o, dl_o, p_o, st_o, res_o, other_o, w1, al_o, s_ref,
        lab, dm, u, cbd, hse, hso, gain_s, tokf, etab, turned, chan_s, sem, out_sem, send, recv, *links,
    ) = refs[12 if mine else 11 :]
    stream, place = lax.axis_index("dir"), lax.axis_index("wide")
    meta = views(count, offset, stream)
    if mine:
        stage, first, got, small, gots, second, pack, gsend, grecv, ssend, srecv, psend, precv, hsem = links
        fill_shares(stream, given, stage, first, small, second)
        got[place] = first[...]
        gots[place] = small[...]
        pack[place] = second[...]
        greet(stream, place, wide)
        early, next_, later = [], [], []
        for k in range(1, wide):
            where = dict(device_id=(stream, place ^ k), device_id_type=MESH)
            early.append(
                pltpu.make_async_remote_copy(
                    src_ref=first, dst_ref=got.at[place], send_sem=gsend.at[k], recv_sem=grecv.at[k], **where
                )
            )
            next_.append(
                pltpu.make_async_remote_copy(
                    src_ref=small, dst_ref=gots.at[place], send_sem=ssend.at[k], recv_sem=srecv.at[k], **where
                )
            )
            later.append(
                pltpu.make_async_remote_copy(
                    src_ref=second, dst_ref=pack.at[place], send_sem=psend.at[k], recv_sem=precv.at[k], **where
                )
            )
            early[-1].start()
        for c in next_:
            c.start()
    else:
        bar = pltpu.get_barrier_semaphore()
        pl.semaphore_signal(bar, inc=1, device_id=(1 - stream, place), device_id_type=MESH)
        pl.semaphore_wait(bar, 1)
        w1[...] = given[0][...]
        s_ref[...] = given[1][...]
    fill_embedding(stride, etab)
    lay_tokens(tok, tokf)
    fill_labels(meta, lab)

    def unit_tile(i):
        base = i * 32 if isinstance(i, int) else pl.multiple_of(i * 32, 32)
        res, _l = residual_tile(meta, tokf, etab, base, 32)
        scale = row_scale(res)
        for c in range(3):
            tokf[c, pl.ds(base, 32), :] = res[c] * scale

    pairs(R // 32, unit_tile)
    if mine:
        for c in early:
            c.wait_recv()
        take_shares(stream, wide, got, w1, chan_s, gain_s)
        cols = pl.ds(pl.multiple_of(stream * D, 128), D)
        half = pltpu.make_async_remote_copy(
            src_ref=w1.at[:, cols], dst_ref=w1.at[:, cols], send_sem=hsem.at[0], recv_sem=hsem.at[1],
            device_id=(1 - stream, place), device_id_type=MESH,
        )
        half.start()
    else:
        st_o[...] = s_ref[...].astype(F32).T
        gain_s[...] = gain_row(st_o, wide)
        chan_s[...] = st_o[ROW_CHAN : ROW_CHAN + 8, :]
    saves = [
        pltpu.make_async_copy(v, h, out_sem.at[k])
        for k, (v, h) in enumerate(
            zip(
                (normed_o, x_o, act_o, dl_o, p_o, st_o, w1, res_o, other_o),
                (normed_h, x_h, act_h, dl_h, p_h, st_h, w1_h, res_h, other_h),
            )
        )
    ]

    def norm_tile(i, _):
        base = pl.multiple_of(i * 32, 32)
        for c in range(3):
            cols = slice(c * 128, c * 128 + 128)
            normed_o[pl.ds(base, 32), cols] = (tokf[c, pl.ds(base, 32), :] * gain_s[7:8, cols]).astype(BF)
        return 0

    lax.fori_loop(0, R // 32, norm_tile, 0)
    if mine:
        half.wait()
    x_o[:, 0:HALO, :] = jnp.zeros((G6, HALO, 128), F32)
    x_o[:, HALO + R : XR, :] = jnp.zeros((G6, HALO, 128), F32)
    for h in range(2):
        for c in range(0, G6, 2):
            y = dot(normed_o[h * 592 : h * 592 + 592, :], w1[:, c * 128 : c * 128 + 256])
            x_o[c, HALO + h * 592 : HALO + h * 592 + 592, :] = y[:, :128]
            x_o[c + 1, HALO + h * 592 : HALO + h * 592 + 592, :] = y[:, 128:]

    def conv(rev):
        def tile(i, _):
            base = pl.multiple_of(i * 32, 32)
            for c in range(G6):
                total, _l = conv_tile(x_o, lab, chan_s, c, base, 32, rev)
                act = total * sigmoid(total)
                act_o[c, pl.ds(base, 32), :] = act
                al_o[pl.ds(base, 32), c * 128 : c * 128 + 128] = act.astype(BF)
            return 0

        lax.fori_loop(0, R // 32, tile, 0)

    @pl.when(stream == 0)
    def _():
        conv(False)

    @pl.when(stream == 1)
    def _():
        conv(True)

    if mine:
        for c in next_:
            c.wait_recv()
        for k in range(wide):
            s_ref[k * ROWS_S : (k + 1) * ROWS_S, :] = gots[k]
        for c in early + next_:
            c.wait_send()
        for c in later:
            c.start()
        st_o[...] = s_ref[...].astype(F32).T
        st_o[ROW_CHAN : ROW_CHAN + 8, :] = chan_s[...]
    p_o[R:, :] = jnp.zeros((1280 - R, 128), F32)
    col = lax.broadcasted_iota(jnp.int32, (128, 256), 1)
    row = lax.broadcasted_iota(jnp.int32, (128, 256), 0)
    spread_c = jnp.where(row == ROW_C + col % N, 1.0, 0.0).astype(BF)
    diag = (
        lax.broadcasted_iota(jnp.int32, (592, 256), 0) % N
        == lax.broadcasted_iota(jnp.int32, (592, 256), 1) // N
    )
    for h in range(2):
        rows = slice(h * 592, h * 592 + 592)
        proj = dot(al_o[rows, :], s_ref[...])
        p_o[rows, :] = proj
        low = proj.astype(BF)
        cbd[rows, :] = jnp.where(diag, dot(low, spread_c), 0.0).astype(BF)
        step_in = low[:, :RANK]
        for c in range(0, G6, 2):
            w = st_o[ROW_STEP : ROW_STEP + RANK, c * 128 : c * 128 + 256].astype(BF)
            y = dot(step_in, w)
            dl_o[c, rows, :] = y[:, :128]
            dl_o[c + 1, rows, :] = y[:, 128:]
    stats_o[...] = jnp.zeros(stats_o.shape, F32)
    turn(p_o, ROW_B, turned)

    def soft(rev):
        def tile(i, _):
            base = pl.multiple_of(i * 32, 32)
            here = lab[pl.ds(base + HALO, 32), :]
            before = lab[pl.ds(base + HALO + (1 if rev else -1), 32), :]
            cut = jnp.where(here == before, 0.0, CUT)
            live = jnp.where(here >= 0, 1.0, 0.0)
            real = jnp.where(here >= -1, 1.0, 0.0)
            for c in range(G6):
                cols = slice(c * 128, c * 128 + 128)
                rows = pl.ds(base, 32)
                v = dl_o[c, rows, :] + st_o[ROW_CHAN + 5 : ROW_CHAN + 6, cols]
                delta = jnp.maximum(v, 0.0) + jnp.log1p(jnp.exp(-jnp.abs(v)))
                dl_o[c, rows, :] = delta
                dm[c, rows, :] = delta + cut
                u[c, rows, :] = delta * act_o[c, rows, :] * real
                t1 = live * delta
                t2 = t1 * delta
                for s in range(4):
                    stats_o[0, :, cols] += t1[8 * s : 8 * s + 8]
                    stats_o[1, :, cols] += t2[8 * s : 8 * s + 8]
            return 0

        lax.fori_loop(0, R // 32, tile, 0)

    @pl.when(stream == 0)
    def _():
        soft(False)

    @pl.when(stream == 1)
    def _():
        soft(True)

    for c in saves[:7]:
        c.start()
    hs = (hse, hso)

    def save(k, i):
        slot = i % RING
        return pltpu.make_async_copy(hs[k].at[slot], hs_o.at[k, i], sem.at[k, slot])

    def give(i, rev):
        row = pl.multiple_of((NP - 1 - i if rev else i) * 32, 32)
        at = pl.multiple_of(row if rev else row - WBASE, 32)
        k = i - (NP - SENDS)
        return pltpu.make_async_remote_copy(
            src_ref=res_o.at[pl.ds(row, 32), :], dst_ref=other_o.at[pl.ds(at, 32), :],
            send_sem=send.at[k], recv_sem=recv.at[k], device_id=(1 - stream, place), device_id_type=MESH,
        )

    def scan(rev):
        rate = [
            -jnp.exp(st_o[ROW_DECAY : ROW_DECAY + N, c * 128 : c * 128 + 128]) * LOG2E
            for c in range(G6)
        ]

        def block_of(t):
            return NB - 1 - t if rev else t

        def emit(t, k, slot, c):
            rows = rows16(block_of(t))
            y = dot(cbd[rows, :], hs[k][slot, :, c * 128 : c * 128 + 256])
            for h in range(2):
                cols = slice((c + h) * 128, (c + h) * 128 + 128)
                skip = st_o[ROW_CHAN + 6 : ROW_CHAN + 7, cols]
                res_o[rows, cols] = (
                    y[:, h * 128 : h * 128 + 128] + skip * act_o[c + h, rows, :]
                ).astype(BF)

        def block(t, k, slot, state, late):
            b = block_of(t)
            wide_b = turned[b]
            state = list(state)
            for n, j in enumerate(range(15, -1, -1) if rev else range(16)):
                if n % 4 == 0 and late:
                    late.pop(0)()
                q = b * 16 + j
                drive = jnp.broadcast_to(wide_b[:, j : j + 1], (N, 128))
                for c in range(G6):
                    fade = jnp.exp2(dm[c, pl.ds(q, 1), :] * rate[c])
                    state[c] = fade * state[c] + u[c, pl.ds(q, 1), :] * drive
                    hs[k][slot, j * N : j * N + N, c * 128 : c * 128 + 128] = state[c].astype(BF)
            return tuple(state)

        def pair(i, state):
            slot = i % RING

            @pl.when(i >= RING)
            def _():
                save(0, i - RING).wait()
                save(1, i - RING).wait()

            before = jnp.maximum(2 * i - 1, 0)
            late = [
                functools.partial(emit, before, 1, jnp.maximum(i - 1, 0) % RING, c)
                for c in (0, 2, 4)
            ]
            one = 1 + i // 1048576
            state = lax.fori_loop(0, one, lambda _, v, late=late: block(2 * i, 0, slot, v, list(late)), state)
            late = [functools.partial(emit, 2 * i, 0, slot, c) for c in (0, 2, 4)]
            state = lax.fori_loop(0, one, lambda _, v, late=late: block(2 * i + 1, 1, slot, v, list(late)), state)
            save(0, i).start()
            save(1, i).start()

            @pl.when(i > NP - SENDS)
            def _():
                give(i - 1, rev).start()

            return state

        hso[0] = jnp.zeros((256, E), BF)
        lax.fori_loop(0, NP, pair, tuple(jnp.zeros((N, 128), F32) for _ in range(G6)))
        for c in (0, 2, 4):
            emit(NB - 1, 1, (NP - 1) % RING, c)
        give(NP - 1, rev).start()
        for i in range(NP - RING, NP):
            save(0, i).wait()
            save(1, i).wait()

        def settle(i, _):
            give(i, rev).wait()
            return 0

        lax.fori_loop(NP - SENDS, NP, settle, 0)

    @pl.when(stream == 0)
    def _():
        scan(False)

    @pl.when(stream == 1)
    def _():
        scan(True)

    for c in saves[7:]:
        c.start()
    if mine:
        for c in later:
            c.wait()
        packed = pltpu.make_async_copy(pack, pack_h[0], out_sem.at[9])
        packed.start()
        packed.wait()
    for c in saves:
        c.wait()


def forward(wide, mine, count, offset, stride, tok, *given):
    S = jax.ShapeDtypeStruct
    V = pltpu.VMEM
    kept = [
        ((R, D), BF), ((G6, XR, 128), F32), ((G6, R, 128), F32), ((G6, R, 128), F32), ((1280, 128), F32),
        ((128, E), F32), ((R, E), BF), ((WIN, E), BF), ((D, E), BF),
    ]
    pack = [((wide, 2 * D // wide, E), BF)] if mine else []
    dma = pltpu.SemaphoreType.DMA
    links = [
        V((128, 128), F32), V((ROWS_P, 128), BF), V((wide, ROWS_P, 128), BF), V((ROWS_S, 128), BF),
        V((wide, ROWS_S, 128), BF), V(pack[0][0][1:], BF), V(*pack[0]),
        dma((wide,)), dma((wide,)), dma((wide,)), dma((wide,)), dma((wide,)), dma((wide,)), dma((2,)),
    ] if mine else []
    return pl.pallas_call(
        functools.partial(fwd_kernel, wide, mine),
        out_shape=[S(*k) for k in kept + pack] + [S((2, 8, E), F32), S((2, NP, 256, E), BF)],
        in_specs=[SMEM] * 3 + [VMEM] * (1 + len(given)),
        out_specs=[ANY] * len(kept + pack) + [VMEM, ANY],
        scratch_shapes=[V(*k) for k in kept]
        + [
            V((R, E), BF), V((E, 128), BF), V((XR, 128), jnp.int32), V((G6, R, 128), F32), V((G6, R, 128), F32),
            V((R, 256), BF), V((RING, 256, E), BF), V((RING, 256, E), BF), V((8, D), F32),
            V((3, R, 128), F32), V((8, D), F32), V((NB, N, 128), F32), V((8, E), F32),
            dma((2, RING)), dma((10,)), dma((SENDS,)), dma((SENDS,)),
        ]
        + links,
        compiler_params=pltpu.CompilerParams(
            vmem_limit_bytes=60 * 2**20, collective_id=3, has_side_effects=True
        ),
        cost_estimate=pl.CostEstimate(flops=int(5e10), bytes_accessed=1 << 20, transcendentals=0),
        name="forward",
    )(count, offset, stride, tok, *given)


def middle(meta, wide, tokf, etab, cot, normed, own, other, w2, wo, cotw, gated, bgrad, ggrad, blk, mg, gpart, stage, sent, shared):
    stream = meta[4]
    wbase = pl.multiple_of(stream * WBASE, 32)
    lay_cotangent(stream, cot, cotw)
    win = pl.ds(wbase, WIN)

    def tile(i, _):
        base = pl.multiple_of(i * 32, 32)
        r = wbase + base + lax.broadcasted_iota(jnp.int32, (32, 128), 0)
        live = jnp.where(labels_of(meta, r)[0] >= 0, 1.0, 0.0)
        for c in range(3):
            v = live * cotw[c, pl.ds(base, 32), :]
            ref, col = (bgrad[0], c * 128) if c < 2 else (bgrad[1], 0)
            ref[pl.ds(base, 32), col : col + 128] = v.astype(BF)
        return 0

    lax.fori_loop(0, WIN // 32, tile, 0)

    def branch_grad():
        return jnp.concatenate([bgrad[0][0:WIN, :], bgrad[1][0:WIN, 0:128]], 1)

    for c in range(0, E, 256):
        cols = slice(c, c + 256)
        gate = dot(normed[win, :], w2[:, cols])
        mixed = own(cols) + other(cols)
        sig = sigmoid(gate)
        silu = gate * sig
        gated[0:WIN, cols] = (mixed * silu).astype(BF)
        up = dot_nt(branch_grad(), wo[cols, :])
        mg[:, cols] = (up * silu).astype(BF)
        ggrad[0:WIN, cols] = (up * mixed * sig * (1.0 + gate * (1.0 - sig))).astype(BF)
        sent(c // 256).start()
    drow, erow = D // wide, E // wide
    rows = 2 * drow
    pitch = -(-rows // 8) * 8
    for c in range(0, D, 128):
        g = dot_tn(normed[win, c : c + 128], ggrad[0:WIN, :])
        lay_rows(g, c, drow, lambda k, r, v: put(stage, pitch, k, r, 0, v))
    for c in range(0, E, 256):
        g = dot_tn(gated[0:WIN, c : c + 256], branch_grad())
        half = erow // 2
        lay_rows(g, c, half, lambda k, r, v: put(stage, pitch, k // 2, drow + r, (k % 2) * D, v))
    shared(rows, pitch)
    for c in range(0, D, 128):
        cols = slice(c, c + 128)
        blk[c // 128, 0:WIN, :] = dot(gated[0:WIN, :], wo[:, cols])
        gpart[:, cols] = dot_nt(ggrad[0:WIN, :], w2[cols, :])

    def out_tile(i, _):
        base = pl.multiple_of(i * 32, 32)
        at = pl.multiple_of(wbase + base, 32)
        res, live = residual_tile(meta, tokf, etab, at, 32)
        for c in range(3):
            blk[c, pl.ds(base, 32), :] = res[c] + live * blk[c, pl.ds(base, 32), :]
        return 0

    lax.fori_loop(0, WIN // 32, out_tile, 0)


WINDOWS = ((0, 0), (1, WIN - HALF - 8))


def lay_cotangent(stream, cot, cotw):
    cotw[:, 0:WIN, :] = jnp.zeros((3, WIN, 128), F32)
    for s, off in WINDOWS:

        @pl.when(stream == s)
        def _():
            for c in range(3):
                cotw[c, off : off + HALF, :] = cot[:, c * 128 : c * 128 + 128].astype(F32)


def take_half(stream, src, out, sem):
    def copy(off, c):
        return pltpu.make_async_copy(
            src.at[c, off : off + HALF, :], out.at[:, 0, c * 128 : c * 128 + 128], sem.at[c]
        )

    for s, off in WINDOWS:

        @pl.when(stream == s)
        def _():
            for c in range(3):
                copy(off, c).start()

    def wait():
        for c in range(3):
            copy(0, c).wait()

    return wait


def put(ref, pitch, k, r, col, v):
    for c in range(0, v.shape[1], 128):
        at = (k * G6 + (col + c) // 128) * pitch + r
        ref[at : at + v.shape[0], :] = v[:, c : c + 128]


def lay_rows(v, start, size, store):
    at = 0
    while at < v.shape[0]:
        k, r = divmod(start + at, size)
        n = min(size - r, v.shape[0] - at)
        store(k, r, v[at : at + n])
        at += n


def unpack(pack, w2, wo, wide):
    drow, half = D // wide, E // wide // 2
    per = max(1, 16 // math.gcd(16, drow))
    for k in range(0, wide, per):
        v = [pack[k + i].astype(F32) for i in range(per)]
        w2[k * drow : (k + per) * drow, :] = jnp.concatenate([t[0:drow] for t in v], 0).astype(BF)
        pieces = []
        for t in v:
            pieces += [t[drow : drow + half, 0:D], t[drow : drow + half, D : 2 * D]]
        wo[2 * k * half : 2 * (k + per) * half, :] = jnp.concatenate(pieces, 0).astype(BF)


def bwd_kernel(wide, mine, *refs):
    refs = list(refs)
    count, offset, stride, tok, cot, normed, pack, stats, w1, st, res_h, other_h, x_h, act_h, dl_h, p_h, hs_in = refs[:17]
    if mine:
        block_h, tg_h, own_o, twin_o, g2_o, g2x_o = refs[17:23]
    else:
        block_h, tg_h, gw1, gsm, gg_o, g2_o = refs[17:23]
    (
        x, act, dl, p, w2, wo, gpart, mg, mgx, nrecv,
        lab, dm, dy, dyb, ub, bb, bbd, dbm, dcm, dd, zs, dacc, hse, hso, g0, g1, z0, z1, pb0, pb1, pc0, pc1, sel, sums,
        etab, gain_s, acc, turned, sem, in_sem, out_sem, mgsend, mgrecv, swsend, swrecv, win_sem, *links,
    ) = refs[23:]
    if mine:
        g2s, g2r, gw1, gsm, pout, pin, out, got, sout, sin, gout, gin, *sems = links
    stream, place = lax.axis_index("dir"), lax.axis_index("wide")
    wbase = pl.multiple_of(stream * WBASE, 32)
    loads = [
        pltpu.make_async_copy(h, v, in_sem.at[k])
        for k, (h, v) in enumerate(zip((x_h, act_h, dl_h, p_h), (x, act, dl, p)))
    ]
    windows = []
    for i, (h, v, at) in enumerate(((res_h, hse, wbase), (other_h, hso, 0))):
        for k in range(0, WIN, 256):
            n = min(256, WIN - k)
            rows = pl.ds(pl.multiple_of(at + k, 32), n)
            windows.append(
                pltpu.make_async_copy(h.at[rows, :], v.at[k // 256, 0:n, :], win_sem.at[i, k // 256])
            )
    for c in windows + loads:
        c.start()

    def window(ref, cols):
        rows = [ref[k // 256, 0 : min(256, WIN - k), cols] for k in range(0, WIN, 256)]
        return jnp.concatenate(rows, 0).astype(F32)

    if mine:
        greet(stream, place, wide)
    else:
        bar = pltpu.get_barrier_semaphore()
        pl.semaphore_signal(bar, inc=1, device_id=(1 - stream, place), device_id_type=MESH)
        pl.semaphore_wait(bar, 1)
    meta = views(count, offset, stream)
    partner = dict(device_id=(1 - stream, place), device_id_type=MESH)
    fill_embedding(stride, etab)
    fill_labels(meta, lab)
    tokf, cotw, blk = zs.at[0:3], zs.at[3:6], dd.at[0:3]
    lay_tokens(tok, tokf)
    unpack(pack, w2, wo, wide)

    def sent(k):
        cols = slice(k * 256, k * 256 + 256)
        return pltpu.make_async_remote_copy(
            src_ref=mg.at[:, cols], dst_ref=mgx.at[:, cols], send_sem=mgsend.at[k], recv_sem=mgrecv.at[k], **partner
        )

    g2 = []
    if mine:
        for k in range(1, wide):
            g2.append(
                pltpu.make_async_remote_copy(
                    src_ref=g2s.at[place ^ k], dst_ref=g2r.at[k], send_sem=sems[0].at[k], recv_sem=sems[1].at[k],
                    device_id=(stream, place ^ k), device_id_type=MESH,
                )
            )

    def deal(src, dst, n):
        return [
            pltpu.make_async_remote_copy(
                src_ref=src.at[place ^ k], dst_ref=dst.at[k], send_sem=sems[n].at[k], recv_sem=sems[n + 1].at[k],
                device_id=(stream, place ^ k), device_id_type=MESH,
            )
            for k in range(1, wide)
        ]

    def collect(copies, src, dst):
        for c in copies:
            c.wait()
        total = src[place].astype(F32)
        for k in range(1, wide):
            total = total + dst[k].astype(F32)
        return total

    def shared(rows, pitch):
        for k in range(wide):
            for c in range(G6):
                at = (k * G6 + c) * pitch
                cols = slice(c * 128, c * 128 + 128)
                if mine:
                    g2s[k, :, cols] = bb[at : at + rows, :].astype(BF)
                else:
                    g2_o[k, :, cols] = bb[at : at + rows, :]
        for c in g2:
            c.start()

    for c in windows:
        c.wait()
    middle(
        meta, wide, tokf, etab, cot, normed, lambda cols: window(hse, cols), lambda cols: window(hso, cols),
        w2, wo, cotw, ub, (dbm, dcm), dyb, blk, mg, gpart, bb, sent, shared,
    )
    block_out = take_half(stream, blk, block_h, out_sem.at[0])
    for c in loads:
        c.wait()
    turn(p, ROW_C, turned)

    def prep(rev):
        def tile(i, _):
            base = pl.multiple_of(i * 32, 32)
            rows = pl.ds(base, 32)
            here = lab[pl.ds(base + HALO, 32), :]
            before = lab[pl.ds(base + HALO + (1 if rev else -1), 32), :]
            cut = jnp.where(here == before, 0.0, CUT)
            spread_tile(turned, 2 * i, bb)
            spread_tile(turned, 2 * i + 1, bb)
            for c in range(G6):
                dm[c, rows, :] = dl[c, rows, :] + cut
            return 0

        lax.fori_loop(0, R // 32, tile, 0)

    @pl.when(stream == 0)
    def _():
        prep(False)

    @pl.when(stream == 1)
    def _():
        prep(True)

    col = lax.broadcasted_iota(jnp.int32, (128, 256), 1)
    row = lax.broadcasted_iota(jnp.int32, (128, 256), 0)
    spread_b = jnp.where(row == ROW_B + col % N, 1.0, 0.0).astype(BF)
    diag = (
        lax.broadcasted_iota(jnp.int32, (592, 256), 0) % N
        == lax.broadcasted_iota(jnp.int32, (592, 256), 1) // N
    )
    for h in range(2):
        rows = slice(h * 592, h * 592 + 592)
        bbd[rows, :] = jnp.where(diag, dot(p[rows, :].astype(BF), spread_b), 0.0).astype(BF)
    for k in range(3):
        sent(k).wait()
    block_out()
    sums[...] = jnp.zeros(sums.shape, F32)

    for s, lowref, highref in ((0, mg, mgx), (1, mgx, mg)):

        @pl.when(stream == s)
        def _():
            def lay(i, _):
                base = pl.multiple_of(i * 32, 32)
                lowat = pl.multiple_of(jnp.minimum(base, WIN - 32), 32)
                highat = pl.multiple_of(jnp.maximum(base - WBASE, 0), 32)
                for c in range(G6):
                    cols = slice(c * 128, c * 128 + 128)
                    lowrow = lowref[pl.ds(lowat, 32), cols].astype(F32)
                    highrow = highref[pl.ds(highat, 32), cols].astype(F32)
                    v = jnp.where(base < WIN, lowrow, 0.0) + jnp.where(base >= WBASE, highrow, 0.0)
                    dy[c, pl.ds(base, 32), :] = v
                    t = v * act[c, pl.ds(base, 32), :]
                    sums[0, :, cols] += t[0:8] + t[8:16] + t[16:24] + t[24:32]
                return 0

            lax.fori_loop(0, R // 32, lay, 0)

    i = lax.broadcasted_iota(jnp.int32, (32, 256), 0)
    j = lax.broadcasted_iota(jnp.int32, (32, 256), 1)
    sel[...] = jnp.where(i == jnp.where(i < N, j // N, N + j % N), 1.0, 0.0).astype(BF)
    dacc[...] = jnp.zeros(dacc.shape, F32)
    hs, gs, zz, pb, pc = (hse, hso), (g0, g1), (z0, z1), (pb0, pb1), (pc0, pc1)

    def load(k, i):
        slot = i % RING
        return pltpu.make_async_copy(hs_in.at[k, i], hs[k].at[slot], sem.at[k, slot])

    def scan(rev):
        rate = [
            -jnp.exp(st[ROW_DECAY : ROW_DECAY + N, c * 128 : c * 128 + 128]) * LOG2E
            for c in range(G6)
        ]
        block_diag = (
            lax.broadcasted_iota(jnp.int32, (N, 256), 0)
            == lax.broadcasted_iota(jnp.int32, (N, 256), 1) // N
        )

        def block_of(t):
            return NB - 1 - t if rev else t

        def drive_dot(t, k, c):
            rows = rows16(block_of(t))
            y = dot(bbd[rows, :], gs[k][:, c * 128 : c * 128 + 256])
            dd[c, rows, :] = y[:, :128]
            dd[c + 1, rows, :] = y[:, 128:]

        def step_dot(t, k, c, first):
            rows = rows16(block_of(t))
            y = dot(sel[...], zz[k][:, c * 128 : c * 128 + 256])
            zs[c, rows, :] = y[:N, :128]
            zs[c + 1, rows, :] = y[:N, 128:]
            dacc[c] += jnp.where(first, 0.0, y[N:, :128])
            dacc[c + 1] += jnp.where(first, 0.0, y[N:, 128:])

        ones = jnp.ones((N, 128), BF)

        def b_dot(t, k):
            rows = rows16(block_of(t))
            dbm[rows, :] = jnp.where(block_diag, dot_nt(ones, pb[k][...]), 0.0).astype(BF)

        def c_dot(t, k):
            rows = rows16(block_of(t))
            dcm[rows, :] = jnp.where(block_diag, dot_nt(ones, pc[k][...]), 0.0).astype(BF)

        def block(t, k, slot, pslot, carry, late):
            b = block_of(t)
            carry = list(carry)
            late = list(late)
            start = 0 if rev else 15
            now = [hs[k][slot, start * N : start * N + N, c * 128 : c * 128 + 128] for c in range(G6)]
            for n, j in enumerate(range(16) if rev else range(15, -1, -1)):
                if n % 2 == 0 and late:
                    late.pop(0)()
                q = b * 16 + j
                cb = bb[pl.ds(pl.multiple_of(q * N, N), N), :]
                jp = j + 1 if rev else j - 1
                if 0 <= jp < 16:
                    old_ref, old_slot = hs[k], slot
                else:
                    jp = 0 if rev else 15
                    old_ref, old_slot = hs[1 - k], pslot
                sum_b = sum_c = None
                for c in range(G6):
                    cols = slice(c * 128, c * 128 + 128)
                    w = dm[c, pl.ds(q, 1), :] * rate[c]
                    fade = jnp.exp2(w)
                    up = dy[c, pl.ds(q, 1), :]
                    g = cb * up + carry[c]
                    carry[c] = fade * g
                    old = old_ref[old_slot, jp * N : jp * N + N, cols]
                    low = g.astype(BF)
                    gs[k][j * N : j * N + N, cols] = low
                    zz[k][j * N : j * N + N, cols] = (w * carry[c]).astype(BF) * old
                    drive = dl[c, pl.ds(q, 1), :] * act[c, pl.ds(q, 1), :]
                    tb = low * jnp.broadcast_to(drive, (N, 128)).astype(BF)
                    tc = now[c] * jnp.broadcast_to(up, (N, 128)).astype(BF)
                    sum_b = tb if sum_b is None else sum_b + tb
                    sum_c = tc if sum_c is None else sum_c + tc
                    now[c] = old
                pb[k][j * N : j * N + N, :] = sum_b
                pc[k][j * N : j * N + N, :] = sum_c
            return tuple(carry)

        def pair(ii, carry):
            i = NP - 1 - ii
            slot = i % RING
            pslot = jnp.maximum(i - 1, 0) % RING

            @pl.when(i >= 1)
            def _():
                load(0, i - 1).wait()
                load(1, i - 1).wait()

            @pl.when(i >= 3)
            def _():
                load(0, i - 3).start()
                load(1, i - 3).start()

            one = 1 + i // 1048576
            for k in (1, 0):
                t = 2 * i + k
                after = jnp.minimum(t + 1, NB - 1)
                first = t + 1 > NB - 1
                late = [functools.partial(b_dot, after, 1 - k), functools.partial(c_dot, after, 1 - k)]
                late += [functools.partial(drive_dot, after, 1 - k, c) for c in (0, 2, 4)]
                late += [functools.partial(step_dot, after, 1 - k, c, first) for c in (0, 2, 4)]
                ps = slot if k == 1 else pslot
                carry = lax.fori_loop(
                    0, one, lambda _, cc, t=t, k=k, ps=ps, late=late: block(t, k, slot, ps, cc, late), carry
                )
            return carry

        for i in range(NP - 1, NP - 4, -1):
            load(0, i).start()
            load(1, i).start()
        load(0, NP - 1).wait()
        load(1, NP - 1).wait()
        for ref in (g0, z0, pb0, pc0):
            ref[...] = jnp.zeros(ref.shape, BF)
        lax.fori_loop(0, NP, pair, tuple(jnp.zeros((N, 128), F32) for _ in range(G6)))
        for c in (0, 2, 4):
            drive_dot(0, 0, c)
            step_dot(0, 0, c, False)
        b_dot(0, 0)
        c_dot(0, 0)

    @pl.when(stream == 0)
    def _():
        scan(False)

    @pl.when(stream == 1)
    def _():
        scan(True)

    def step_tile(i, _):
        base = pl.multiple_of(i * 32, 32)
        rows = pl.ds(base, 32)
        for c in range(G6):
            cols = slice(c * 128, c * 128 + 128)
            delta, a, d = dl[c, rows, :], act[c, rows, :], dd[c, rows, :]
            near = 1.0 - delta * (0.5 - delta * (1.0 / 6.0 - delta * (1.0 / 24.0)))
            ratio = jnp.where(delta < 0.03, near, (1.0 - jnp.exp(-delta)) / delta)
            pre = ratio * (zs[c, rows, :] * LN2 + a * d * delta)
            ub[rows, cols] = pre.astype(BF)
            dm[c, rows, :] = delta * d + st[ROW_CHAN + 6 : ROW_CHAN + 7, cols] * dy[c, rows, :]
            sums[1, :, cols] += pre[0:8] + pre[8:16] + pre[16:24] + pre[24:32]
        return 0

    lax.fori_loop(0, R // 32, step_tile, 0)
    pgs = bbd.at[:, 0:128]
    w_step = st[ROW_STEP : ROW_STEP + RANK, :].astype(BF)
    w_b = jnp.concatenate([st[ROW_B : ROW_B + N, :]] * N, 0).astype(BF)
    w_c = jnp.concatenate([st[ROW_C : ROW_C + N, :]] * N, 0).astype(BF)
    w_s = st[0:RANK, :].astype(BF)
    for h in range(2):
        rows = slice(h * 592, h * 592 + 592)
        sg = dot_nt(ub[rows, :], w_step).astype(BF)
        pgs[rows, :] = jnp.concatenate([sg, jnp.zeros((592, 128 - RANK), BF)], 1)
        for c in range(0, G6, 2):
            cols = slice(c * 128, c * 128 + 256)
            y = dot(sg, w_s[:, cols]) + dot(dbm[rows, :], w_b[:, cols]) + dot(dcm[rows, :], w_c[:, cols])
            dm[c, rows, :] += y[:, :128]
            dm[c + 1, rows, :] += y[:, 128:]
    low = p[0:R, :].astype(BF)
    gstep = dot_tn(low, ub[...])[0:RANK]

    def activation(i, _):
        rows = pl.ds(pl.multiple_of(i * 32, 32), 32)
        for c in range(G6):
            ub[rows, c * 128 : c * 128 + 128] = act[c, rows, :].astype(BF)
        return 0

    lax.fori_loop(0, R // 32, activation, 0)
    top = dot_tn(pgs[...], ub[...])
    gb = dot_tn(dbm[...], ub[...])
    gc = dot_tn(dcm[...], ub[...])
    gb = sum(gb[k * N : k * N + N] for k in range(N))
    gc = sum(gc[k * N : k * N + N] for k in range(N))
    gdecay = jnp.concatenate([dacc[c] for c in range(G6)], 1) * LN2
    gt = jnp.concatenate([top[0:RANK], gb, gc, gstep, gdecay, jnp.zeros((128 - ROW_CHAN, E), F32)], 0)
    gsm[...] = gt.T
    if mine:
        for k in range(wide):
            sout[k] = gsm[k * ROWS_S : (k + 1) * ROWS_S, :].astype(BF)
        smalls = deal(sout, sin, 2)
        for c in smalls:
            c.start()
    dc = dd
    dc[:, 0:HALO, :] = jnp.zeros((G6, HALO, 128), F32)
    dc[:, HALO + R : XR, :] = jnp.zeros((G6, HALO, 128), F32)

    def conv(rev):
        def first(i, _):
            base = pl.multiple_of(i * 32, 32)
            for c in range(G6):
                cols = slice(c * 128, c * 128 + 128)
                total, lagged = conv_tile(x, lab, st.at[ROW_CHAN : ROW_CHAN + 8], c, base, 32, rev)
                sig = sigmoid(total)
                v = dm[c, pl.ds(base, 32), :] * sig * (1.0 + total * (1.0 - sig))
                dc[c, pl.ds(base + HALO, 32), :] = v
                sums[2, :, cols] += v[0:8] + v[8:16] + v[16:24] + v[24:32]
                for j in range(4):
                    t = v * lagged[j]
                    sums[3 + j, :, cols] += t[0:8] + t[8:16] + t[16:24] + t[24:32]
            return 0

        def second(i, _):
            base = pl.multiple_of(i * 32, 32)
            here = lab[pl.ds(base + HALO, 32), :]
            for c in range(G6):
                cols = slice(c * 128, c * 128 + 128)
                v = dc[c, pl.ds(base + HALO, 32), :] * st[ROW_CHAN : ROW_CHAN + 1, cols]
                for j in (1, 2, 3):
                    at = base + HALO + (-j if rev else j)
                    same = lab[pl.ds(at, 32), :] == here
                    later = jnp.where(same, dc[c, pl.ds(at, 32), :], 0.0)
                    v = v + later * st[ROW_CHAN + j : ROW_CHAN + j + 1, cols]
                dyb[pl.ds(base, 32), cols] = v.astype(BF)
            return 0

        lax.fori_loop(0, R // 32, first, 0)
        lax.fori_loop(0, R // 32, second, 0)

    @pl.when(stream == 0)
    def _():
        conv(False)

    @pl.when(stream == 1)
    def _():
        conv(True)

    theirs = pl.ds(pl.multiple_of((1 - stream) * WBASE, 32), WIN)
    nsend = mg.at[:, 0:D]
    nsend[...] = dot_nt(dyb[theirs, :], w1[...]).astype(BF)
    nswap = pltpu.make_async_remote_copy(
        src_ref=nsend, dst_ref=nrecv, send_sem=swsend.at[0], recv_sem=swrecv.at[0], **partner
    )
    nswap.start()
    for c in range(0, D, 128):
        gw1[c : c + 128, :] = dot_tn(normed[:, c : c + 128], dyb[...])
    if mine:
        for s in range(2):

            @pl.when(stream == s)
            def _():
                pout[...] = gw1[:, (1 - s) * D : (2 - s) * D].astype(BF)

        pre = pltpu.make_async_remote_copy(
            src_ref=pout, dst_ref=pin, send_sem=swsend.at[1], recv_sem=swrecv.at[1], **partner
        )
        pre.start()
    def total(k):
        return jnp.sum(sums[k], axis=0, keepdims=True)

    fine = [jnp.sum(stats[k], axis=0, keepdims=True) * (1.0 / VIEW_TOK) for k in range(2)]
    coarse = [v.astype(BF).astype(F32) for v in fine]
    fine = [a - b for a, b in zip(fine, coarse)]
    chan = [total(3 + k) for k in range(4)] + [total(2), total(1), total(0)]
    if mine:
        gpart[...] += dot_nt(dyb[pl.ds(wbase, WIN), :], w1[...])
        pre.wait()
        fill_owners(stream, wide, gw1, pin, out)
        shares = deal(out, got, 4)
        for c in shares:
            c.start()
    else:
        rest = chan + [jnp.zeros((1, E), F32)] + coarse + fine
        gsm[...] += jnp.concatenate([jnp.zeros((ROW_CHAN, E), F32)] + rest + [jnp.zeros((20, E), F32)], 0).T
        gpart[...] += dot_nt(dyb[pl.ds(wbase, WIN), :], w1[...])
    nswap.wait()
    ending(meta, wide, tok, etab, cot, nrecv, gpart, st, zs.at[0:3], zs.at[3:6], dd.at[0:3], gain_s, acc)
    token_out = take_half(stream, dd.at[0:3], tg_h, out_sem.at[1])
    if not mine:
        gg_o[...] = acc[...]
        token_out()
        return
    gain = jnp.sum(acc[...], axis=0, keepdims=True)
    rows = jnp.concatenate(chan + [jnp.zeros((1, E), F32)] + coarse + fine + [jnp.zeros((4, E), F32)], 0)
    for k in range(wide):
        piece = rows[:, k * ROWS_S : (k + 1) * ROWS_S]
        owned = jnp.concatenate([gain[:, k * ROWS_W : (k + 1) * ROWS_W], jnp.zeros((1, ROWS_S - ROWS_W), F32)], 1)
        at = lax.broadcasted_iota(jnp.int32, (ROWS_C, ROWS_S), 0)
        piece = jnp.where(at == 7, jnp.broadcast_to(owned, (ROWS_C, ROWS_S)), piece)
        gout[k] = jnp.concatenate([piece, jnp.zeros((ROWS_C, 128 - ROWS_S), F32)], 1).astype(BF)
    gains = deal(gout, gin, 6)
    for c in gains:
        c.start()
    for c in g2:
        c.wait()
    for r in range(0, g2_o.shape[0], 24):
        rows = slice(r, r + 24)
        total = g2s[place].astype(F32)[rows]
        for k in range(1, wide):
            total = total + g2r[k].astype(F32)[rows]
        g2_o[rows, :] = total
    g2swap = pltpu.make_async_remote_copy(
        src_ref=g2_o, dst_ref=g2x_o, send_sem=swsend.at[2], recv_sem=swrecv.at[2], **partner
    )
    g2swap.start()
    own_o[0:ROWS_S, :] = collect(smalls, sout, sin)
    own_o[ROWS_S:AT_C, :] = collect(shares, out, got)
    own_o[AT_C:PACK, :] = collect(gains, gout, gin)
    last = pltpu.make_async_remote_copy(
        src_ref=own_o, dst_ref=twin_o, send_sem=swsend.at[3], recv_sem=swrecv.at[3], **partner
    )
    last.start()
    token_out()
    g2swap.wait()
    last.wait()


def ending(meta, wide, tok, etab, cot, other, gpart, st, tokf, cotw, out, gain_s, acc):
    stream = meta[4]
    wbase = pl.multiple_of(stream * WBASE, 32)
    lay_tokens(tok, tokf)
    lay_cotangent(stream, cot, cotw)
    gain_s[...] = gain_row(st, wide)
    acc[...] = jnp.zeros(acc.shape, F32)
    lo = stream * HALF

    def tile(i):
        base = i * 32 if isinstance(i, int) else pl.multiple_of(i * 32, 32)
        at = pl.multiple_of(wbase + base, 32)
        rows = pl.ds(base, 32)
        res, _l = residual_tile(meta, tokf, etab, at, 32)
        scale = row_scale(res)
        r = at + lax.broadcasted_iota(jnp.int32, (32, 128), 0)
        mine = (r >= lo) & (r < lo + HALF)
        ng, un = [], []
        for c in range(3):
            cols = slice(c * 128, c * 128 + 128)
            v = gpart[rows, cols] + other[rows, cols].astype(F32)
            unit = res[c] * scale
            t = jnp.where(mine, v * unit, 0.0)
            acc[:, cols] += t[0:8] + t[8:16] + t[16:24] + t[24:32]
            ng.append(v * gain_s[0:1, cols])
            un.append(unit)
        mean = sum(jnp.sum(a * b, axis=1, keepdims=True) for a, b in zip(ng, un)) * (1.0 / D)
        for c in range(3):
            out[c, rows, :] = cotw[c, rows, :] + scale * (ng[c] - un[c] * mean)

    pairs(WIN // 32, tile)


def backward(wide, mine, *args):
    S = jax.ShapeDtypeStruct
    V = pltpu.VMEM
    dma = pltpu.SemaphoreType.DMA
    big = V((G6, R, 128), F32)
    rows = 2 * D // wide
    half = S((HALF, 1, D), F32)
    if mine:
        outs = [S((PACK, 128), F32), S((PACK, 128), F32), S((rows, E), F32), S((rows, E), F32)]
        links = [
            V((wide, rows, E), BF), V((wide, rows, E), BF), V((D, E), F32), V((E, 128), F32), V((D, D), BF), V((D, D), BF),
            V((wide, ROWS_P, 128), BF), V((wide, ROWS_P, 128), BF), V((wide, ROWS_S, 128), BF), V((wide, ROWS_S, 128), BF),
            V((wide, ROWS_C, 128), BF), V((wide, ROWS_C, 128), BF),
        ] + [dma((wide,))] * 8
    else:
        outs = [S((D, E), F32), S((E, 128), F32), S((8, D), F32), S((wide, rows, E), F32)]
        links = []
    return pl.pallas_call(
        functools.partial(bwd_kernel, wide, mine),
        out_shape=[half, half] + outs,
        in_specs=[SMEM] * 3 + [VMEM] * 7 + [ANY] * 7,
        out_specs=[ANY] * 2 + [VMEM] * 4,
        scratch_shapes=[
            V((G6, XR, 128), F32), big, big, V((1280, 128), F32),
            V((D, E), BF), V((E, D), BF), V((WIN, D), F32), V((WIN, E), BF), V((WIN, E), BF), V((WIN, D), BF),
            V((XR, 128), jnp.int32), big, big, V((R, E), BF), V((R, E), BF), V((R * N, 128), F32),
            V((R, 256), BF), V((R, 256), BF), V((R, 256), BF), V((G6, XR, 128), F32), big, V((G6, N, 128), F32),
            V((RING, 256, E), BF), V((RING, 256, E), BF),
            V((256, E), BF), V((256, E), BF), V((256, E), BF), V((256, E), BF),
            V((256, 128), BF), V((256, 128), BF), V((256, 128), BF), V((256, 128), BF), V((32, 256), BF), V((7, 8, E), F32),
            V((8, D), F32), V((8, D), F32), V((8, D), F32), V((NB, N, 128), F32),
            dma((2, RING)), dma((4,)), dma((2, 3)), dma((3,)), dma((3,)), dma((4,)), dma((4,)), dma((2, 3)),
        ]
        + links,
        compiler_params=pltpu.CompilerParams(
            vmem_limit_bytes=63 * 2**20, collective_id=4, has_side_effects=True
        ),
        cost_estimate=pl.CostEstimate(flops=int(9e10), bytes_accessed=1 << 20, transcendentals=0),
        name="backward",
    )(*args)


ROWS_W = 24
ROWS_P = 80
ROWS_S = 48
ROWS_C = 16
PACK = ROWS_S + ROWS_P + ROWS_C
AT_C = ROWS_S + ROWS_P


def greet(d, w, wide):
    bar = pltpu.get_barrier_semaphore()
    for k in range(1, wide):
        pl.semaphore_signal(bar, inc=1, device_id=(d, w ^ k), device_id_type=MESH)
    pl.semaphore_signal(bar, inc=1, device_id=(1 - d, w), device_id_type=MESH)
    pl.semaphore_wait(bar, wide)


def fill_shares(d, given, stage, first, small, second):
    inp, out, state, step, decay, chan, gain = given
    stage[...] = jnp.zeros(stage.shape, F32)
    stage[ROW_STEP:ROW_DECAY, 0:ROWS_S] = step[0]
    stage[ROW_DECAY:ROW_CHAN, 0:ROWS_S] = decay[0]
    for k in range(7):
        stage[ROW_CHAN + k : ROW_CHAN + k + 1, 0:ROWS_S] = chan[k]
    stage[ROW_GAIN : ROW_GAIN + 1, 0:ROWS_W] = gain[...]
    parts = []
    for c in range(3):
        low, high = inp[:, c * 128 : c * 128 + 128], inp[:, D + c * 128 : D + c * 128 + 128]
        parts.append(jnp.where(d == 0, low, high))
    first[...] = jnp.concatenate(parts + [stage[ROW_CHAN : ROW_CHAN + 8, :]], 0).astype(BF)
    turned = stage[...].T[0:ROWS_S]
    stage[0:ROWS_S, 0:ROW_STEP] = state[0]
    col = lax.broadcasted_iota(jnp.int32, (ROWS_S, 128), 1)
    small[...] = jnp.where(col < ROW_STEP, stage[0:ROWS_S, :], turned).astype(BF)
    pair = jnp.concatenate([out[0:ROWS_W, :], out[ROWS_W : 2 * ROWS_W, :]], 1)
    second[...] = jnp.concatenate([inp[:, E:], pair], 0).astype(BF)


def take_shares(d, wide, got, w1, chan_s, gain_s):
    lane = lax.broadcasted_iota(jnp.int32, (8, 128), 1)

    def lay(tiles, piece, at):
        t, r = divmod(at, 128)
        moved = pltpu.roll(piece, r, 1) if r else piece
        tiles[t] = tiles[t] + jnp.where(lane >= r, moved, 0.0)
        if t + 1 < len(tiles):
            tiles[t + 1] = tiles[t + 1] + jnp.where(lane < r, moved, 0.0)

    chan = [jnp.zeros((8, 128), F32) for _ in range(E // 128)]
    gain = [jnp.zeros((8, 128), F32) for _ in range(D // 128)]
    for k in range(0, wide, 2):
        v = [got[k + i].astype(F32) for i in range(2)]
        for c in range(3):
            piece = [t[c * ROWS_W : (c + 1) * ROWS_W] for t in v]
            piece = jnp.concatenate(piece, 0).astype(BF)
            for s in range(2):

                @pl.when(d == s)
                def _():
                    at = s * D + c * 128
                    w1[k * ROWS_W : (k + 2) * ROWS_W, at : at + 128] = piece

        for i in range(2):
            lay(chan, v[i][3 * ROWS_W : ROWS_P], (k + i) * ROWS_S)
            lay(gain, v[i][3 * ROWS_W : ROWS_P], (k + i) * ROWS_W)
    for c, v in enumerate(chan):
        chan_s[:, c * 128 : c * 128 + 128] = v
    for c, v in enumerate(gain):
        gain_s[:, c * 128 : c * 128 + 128] = v


def fill_owners(d, wide, gw1, pin, out):
    for k in range(wide):
        rows = slice(k * ROWS_W, (k + 1) * ROWS_W)
        parts = []
        at = k * ROWS_W % 16
        base = k * ROWS_W - at
        arrived = pin[base : base + 32, :].astype(F32)[at : at + ROWS_W]
        for c in range(3):
            low, high = gw1[rows, c * 128 : c * 128 + 128], gw1[rows, D + c * 128 : D + c * 128 + 128]
            parts.append(jnp.where(d == 0, low, high) + arrived[:, c * 128 : c * 128 + 128])
        parts.append(jnp.zeros((ROWS_P - 3 * ROWS_W, 128), F32))
        out[k] = jnp.concatenate(parts, 0).astype(BF)


def gather_plain(inp, state, step, decay, chan, gain):
    rows = state.shape[1]
    column = jnp.concatenate([gain, jnp.zeros((rows - gain.shape[0],), F32)])[:, None]
    small = [state[0], step[0].T, decay[0].T, chan[0].T, column, jnp.zeros((rows, 127 - ROW_GAIN), F32)]
    small = jnp.concatenate(small, 1).astype(BF)
    return (
        lax.all_gather(inp[:, :E].astype(BF), "wide", axis=0, tiled=True),
        lax.all_gather(small, "wide", axis=0, tiled=True),
    )


def reduce_plain(gw1, gs, gg):
    def total(v):
        return lax.psum_scatter(v, "wide", scatter_dimension=0, tiled=True)

    return total(lax.psum(gw1, "dir")), total(gs), total(lax.psum(gg.sum(0), "dir"))


def adam_step(weight, gradient, first_moment, second, step_rate, decay_rate):
    first_moment = BETA_ONE * first_moment + (1.0 - BETA_ONE) * gradient
    second = BETA_TWO * second + (1.0 - BETA_TWO) * gradient * gradient
    first_hat = first_moment / (1.0 - BETA_ONE**STEP)
    second_hat = second / (1.0 - BETA_TWO**STEP)
    weight = weight - step_rate * (
        first_hat / (jnp.sqrt(second_hat) + EPS_ADAM) + decay_rate * weight
    )
    return (weight, first_moment, second)


def update_kernel(got, twin, g2, g2x, *refs):
    stream = lax.axis_index("dir")
    masters, outs = refs[:21], refs[21:]

    def step(k, gradient, at=(slice(None),), out=None):
        new = adam_step(
            masters[3 * k][at], gradient, masters[3 * k + 1][at], masters[3 * k + 2][at], RATES[k], DECAYS[k]
        )
        for i in range(3):
            outs[1 + 3 * k + i][at] = new[i]

    mine, theirs = got[...], twin[...]
    low, high = jnp.where(stream == 0, mine, theirs), jnp.where(stream == 0, theirs, mine)
    for h, v in enumerate((low, high)):
        for c in range(3):
            at = ROWS_S + c * ROWS_W
            col = h * D + c * 128
            step(0, v[at : at + ROWS_W], (slice(None), slice(col, col + 128)))
    shared = g2[...] + g2x[...]
    step(0, shared[0:ROWS_W], (slice(None), slice(E, 2 * E)))
    step(1, shared[ROWS_W:, 0:D], (slice(0, ROWS_W), slice(None)))
    step(1, shared[ROWS_W:, D:], (slice(ROWS_W, 2 * ROWS_W), slice(None)))
    t = mine[0:128].T
    step(2, mine[AT_C + 7 : AT_C + 8, 0:ROWS_W] + theirs[AT_C + 7 : AT_C + 8, 0:ROWS_W])
    step(3, mine[0:ROWS_S, 0:ROW_STEP], (0,))
    step(4, t[ROW_STEP:ROW_DECAY, 0:ROWS_S], (0,))
    step(5, t[ROW_DECAY:ROW_CHAN, 0:ROWS_S], (0,))
    for k in range(7):
        step(6, mine[AT_C + k : AT_C + k + 1, 0:ROWS_S], (k,))
    outs[0][0] = mine[AT_C + 8 : AT_C + 10, 0:ROWS_S] + mine[AT_C + 10 : AT_C + 12, 0:ROWS_S]


def update(got, twin, g2, g2x, masters):
    S = jax.ShapeDtypeStruct
    masters = list(masters)
    masters[6:9] = [v[None] for v in masters[6:9]]
    masters[18:21] = [jnp.transpose(v, (1, 0, 2)) for v in masters[18:21]]
    outs = pl.pallas_call(
        update_kernel,
        out_shape=[S((1, 2, ROWS_S), F32)] + [S(v.shape, F32) for v in masters],
        in_specs=[VMEM] * 25,
        out_specs=[VMEM] * 22,
        name="update",
    )(got, twin, g2, g2x, *masters)
    stats, outs = outs[0], list(outs[1:])
    outs[6:9] = [v[0] for v in outs[6:9]]
    outs[18:21] = [jnp.transpose(v, (1, 0, 2)) for v in outs[18:21]]
    return stats, outs


def update_plain(gw1, gs, gg, g2, masters):
    drow = masters[0].shape[0]
    g1, small, gain = reduce_plain(gw1, gs, gg)
    t = small.T
    grads = (
        jnp.concatenate([g1, g2[:drow]], 1),
        jnp.concatenate([g2[drow:, :D], g2[drow:, D:]], 0),
        gain,
        small[None, :, :ROW_STEP],
        t[None, ROW_STEP:ROW_DECAY],
        t[None, ROW_DECAY:ROW_CHAN],
        t[None, ROW_CHAN:ROW_GAIN],
    )
    outs = []
    for k, g in enumerate(grads):
        w, f, s2 = masters[3 * k : 3 * k + 3]
        outs += adam_step(w, g, f, s2, RATES[k], DECAYS[k])
    return (t[ROW_STATS : ROW_STATS + 2] + t[ROW_STATS + 2 : ROW_STATS + 4])[None], outs


def local(tokens, cotangent, view_counts, view_strides, view_offsets, *masters):
    wide = lax.axis_size("wide")
    in_proj, out_proj, gain = masters[0], masters[3], masters[6]
    erow = out_proj.shape[0]
    mine = E // wide == ROWS_S and D // wide == ROWS_W
    about = (view_counts, view_offsets, view_strides)
    tok, cot = tokens[0], cotangent[0]
    small = masters[9], masters[12], masters[15]
    if mine:
        chan = jnp.transpose(masters[18], (1, 0, 2))
        *kept, pack, stats, hs = forward(wide, mine, *about, tok, in_proj, out_proj, *small, chan, gain[None])
    else:
        pair = jnp.concatenate([out_proj[: erow // 2], out_proj[erow // 2 :]], 1)
        pack = lax.all_gather(jnp.concatenate([in_proj[:, E:], pair], 0).astype(BF), "wide", axis=0)
        given = gather_plain(in_proj, *small, masters[18], gain)
        *kept, stats, hs = forward(wide, mine, *about, tok, *given)
    normed, x, act, dl, p, st, res, other, w1 = kept
    block, token_grad, *sums = backward(
        wide, mine, *about, tok, cot, normed, pack, stats, w1, st, res, other, x, act, dl, p, hs
    )
    if mine:
        stats, outs = update(*sums, masters)
    else:
        gw1, gs, gg, g2 = sums
        g2 = lax.psum(lax.psum_scatter(g2, "wide", scatter_dimension=0, tiled=True)[0], "dir")
        stats, outs = update_plain(gw1, gs, gg, g2, masters)
    return (jnp.transpose(block, (1, 0, 2)), jnp.transpose(token_grad, (1, 0, 2)), stats, *outs)


def solution(mesh):
    row, col = P("wide", None), P("dir", None, "wide")
    mat = P("dir", "wide", None)
    weights = [row] * 6 + [P("wide")] * 3 + [mat] * 3 + [col] * 9
    return jax.shard_map(
        local,
        mesh=mesh,
        in_specs=(
            P("wide", None, None), P("wide", "dir", None), P("wide"), row, row, *weights,
        ),
        out_specs=(P("wide", "dir", None), P("wide", "dir", None), col, *weights),
        check_vma=False,
    )
```

```python
import functools
import math

import jax
import jax.numpy as jnp
from jax import lax
from jax.experimental import pallas as pl
from jax.experimental.pallas import tpu as pltpu
from jax.sharding import PartitionSpec as P

PATCHES = 196
STEP = 10
VIEW_TOK = 392
EPS_NORM = 1e-06
BETA_ONE = 0.9
BETA_TWO = 0.95
EPS_ADAM = 1e-08
RATES = (0.15, 0.1, 2.5, 0.12, 0.2, 1.0, 2.5)
DECAYS = (0.1, 0.1, 0.0, 0.1, 0.1, 0.0, 0.0)

F32 = jnp.float32
BF = jnp.bfloat16
LN2 = math.log(2.0)
LOG2E = 1.0 / LN2

SLOTS = 1176
R = 1184
NB = R // 16
NP = NB // 2
HALF = 588
WIN = 608
WBASE = 576
D = 384
E = 768
G6 = E // 128
N = 16
RANK = 24
HALO = 8
XR = HALO + R + HALO
RING = 4
CUT = 1e4
SENDS = WIN // 32
MESH = pl.DeviceIdType.MESH
ROW_B, ROW_C, ROW_STEP, ROW_DECAY, ROW_CHAN, ROW_GAIN, ROW_STATS = 24, 40, 56, 80, 96, 103, 104
NT = (((1,), (1,)), ((), ()))
TN = (((0,), (0,)), ((), ()))
VMEM = pl.BlockSpec(memory_space=pltpu.VMEM)
SMEM = pl.BlockSpec(memory_space=pltpu.SMEM)
ANY = pl.BlockSpec(memory_space=pl.ANY)


def dot(a, b):
    return jnp.dot(a, b, preferred_element_type=F32)


def dot_nt(a, b):
    return lax.dot_general(a, b, NT, preferred_element_type=F32)


def dot_tn(a, b):
    return lax.dot_general(a, b, TN, preferred_element_type=F32)


def sigmoid(v):
    return 0.5 * jnp.tanh(0.5 * v) + 0.5


def rows16(b, n=16):
    return pl.ds(pl.multiple_of(b * 16, 16), n)


def labels_of(meta, r):
    lab = jnp.full(r.shape, -1, jnp.int32)
    late = jnp.zeros(r.shape, jnp.int32)
    for k in range(3):
        start = meta[1 + k]
        inside = (r >= start) & (r < start + VIEW_TOK) & (k < meta[0])
        lab = jnp.where(inside, k, lab)
        late = jnp.where(inside, jnp.where(r >= start + PATCHES, 1, 0), late)
    lab = jnp.where(r < 0, -2, lab)
    lab = jnp.where(r >= SLOTS, -3, lab)
    return lab, late


def residual_tile(meta, tok, etab, base, n):
    r = base + lax.broadcasted_iota(jnp.int32, (n, 128), 0)
    lab, late = labels_of(meta, r)
    live = jnp.where(lab >= 0, 1.0, 0.0)
    out = []
    for c in range(3):
        cols = slice(c * 128, c * 128 + 128)
        emb = jnp.where(lab >= 0, etab[3:4, cols], 0.0)
        for k in range(3):
            emb = jnp.where((lab == k) & (late == 1), etab[k : k + 1, cols], emb)
        out.append(tok[c, pl.ds(base, n), :] + emb)
    return out, live


def lay_tokens(tok, tokf):
    for c in range(3):
        tokf[c, 0:SLOTS, :] = tok[:, c * 128 : c * 128 + 128].astype(F32)
        tokf[c, SLOTS:R, :] = jnp.zeros((R - SLOTS, 128), F32)


def row_scale(res):
    total = sum(jnp.sum(v * v, axis=1, keepdims=True) for v in res)
    return lax.rsqrt(total * (1.0 / D) + EPS_NORM)


def fill_labels(meta, lab_ref):
    for base in range(0, XR, 8):
        r = base - HALO + lax.broadcasted_iota(jnp.int32, (8, 128), 0)
        lab_ref[base : base + 8, :] = labels_of(meta, r)[0]


def gain_row(st_ref, wide):
    per = E // wide
    own = D // wide
    i = lax.broadcasted_iota(jnp.int32, (E, D), 0)
    j = lax.broadcasted_iota(jnp.int32, (E, D), 1)
    pick = jnp.where(i == (j // own) * per + j % own, 1.0, 0.0).astype(BF)
    src = jnp.broadcast_to(st_ref[ROW_GAIN : ROW_GAIN + 1, :], (16, E)).astype(BF)
    return dot(src, pick)[0:8]


def turn(p_ref, lane, out_ref):
    for sb in range(-(-R // 128)):
        v = p_ref[sb * 128 : sb * 128 + 128, :].T[lane : lane + N]
        for k in range(8):
            if sb * 8 + k < NB:
                out_ref[sb * 8 + k] = v if k == 0 else pltpu.roll(v, 128 - 16 * k, 1)


def spread_tile(turned, b, out_ref):
    v = turned[b]
    for j in range(16):
        out_ref[pl.ds(pl.multiple_of((b * 16 + j) * N, N), N), :] = jnp.broadcast_to(v[:, j : j + 1], (N, 128))


def pairs(count, body):
    def two(i, _):
        body(2 * i)
        body(2 * i + 1)
        return 0

    lax.fori_loop(0, count // 2, two, 0)
    if count % 2:
        body(count - 1)


def conv_tile(x_ref, lab_ref, chan, c, base, n, rev):
    cols = slice(c * 128, c * 128 + 128)
    here = lab_ref[pl.ds(base + HALO, n), :]
    lagged = [x_ref[c, pl.ds(base + HALO, n), :]]
    for j in (1, 2, 3):
        at = base + HALO + (j if rev else -j)
        same = lab_ref[pl.ds(at, n), :] == here
        lagged.append(jnp.where(same, x_ref[c, pl.ds(at, n), :], 0.0))
    total = chan[4:5, cols]
    for j in range(4):
        total = total + chan[j : j + 1, cols] * lagged[j]
    return total, lagged


def views(count, offset, stream):
    return [count[0], offset[0, 0], offset[0, 1], offset[0, 2], stream]


def fill_embedding(stride, etab):
    lane = lax.broadcasted_iota(jnp.int32, (8, D), 1)
    row = lax.broadcasted_iota(jnp.int32, (8, D), 0)
    half = D // 2
    j = jnp.where(lane < half, lane, lane - half).astype(F32)
    freq = jnp.exp(-math.log(10000.0) * j / half)
    clock = jnp.zeros((8, D), F32)
    for k in range(3):
        clock = jnp.where(row == k, stride[0, k].astype(F32), clock)
    angle = clock * freq
    etab[...] = jnp.where(lane < half, jnp.sin(angle), jnp.cos(angle))


def fwd_kernel(wide, mine, *refs):
    refs = list(refs)
    count, offset, stride, tok = refs[:4]
    given, refs = refs[4 : 4 + (7 if mine else 2)], refs[4 + (7 if mine else 2) :]
    (
        normed_h, x_h, act_h, dl_h, p_h, st_h, res_h, other_h, w1_h, *pack_h, stats_o, hs_o,
    ) = refs[: 12 if mine else 11]
    (
        normed_o, x_o, act_o, dl_o, p_o, st_o, res_o, other_o, w1, al_o, s_ref,
        lab, dm, u, cbd, hse, hso, gain_s, tokf, etab, turned, chan_s, sem, out_sem, send, recv, *links,
    ) = refs[12 if mine else 11 :]
    stream, place = lax.axis_index("dir"), lax.axis_index("wide")
    meta = views(count, offset, stream)
    if mine:
        stage, first, got, small, gots, second, pack, gsend, grecv, ssend, srecv, psend, precv, hsem = links
        fill_shares(stream, given, stage, first, small, second)
        got[place] = first[...]
        gots[place] = small[...]
        pack[place] = second[...]
        greet(stream, place, wide)
        early, next_, later = [], [], []
        for k in range(1, wide):
            where = dict(device_id=(stream, place ^ k), device_id_type=MESH)
            early.append(
                pltpu.make_async_remote_copy(
                    src_ref=first, dst_ref=got.at[place], send_sem=gsend.at[k], recv_sem=grecv.at[k], **where
                )
            )
            next_.append(
                pltpu.make_async_remote_copy(
                    src_ref=small, dst_ref=gots.at[place], send_sem=ssend.at[k], recv_sem=srecv.at[k], **where
                )
            )
            later.append(
                pltpu.make_async_remote_copy(
                    src_ref=second, dst_ref=pack.at[place], send_sem=psend.at[k], recv_sem=precv.at[k], **where
                )
            )
            early[-1].start()
    else:
        bar = pltpu.get_barrier_semaphore()
        pl.semaphore_signal(bar, inc=1, device_id=(1 - stream, place), device_id_type=MESH)
        pl.semaphore_wait(bar, 1)
        w1[...] = given[0][...]
        s_ref[...] = given[1][...]
    fill_embedding(stride, etab)
    lay_tokens(tok, tokf)
    fill_labels(meta, lab)

    def unit_tile(i):
        base = i * 32 if isinstance(i, int) else pl.multiple_of(i * 32, 32)
        res, _l = residual_tile(meta, tokf, etab, base, 32)
        scale = row_scale(res)
        for c in range(3):
            tokf[c, pl.ds(base, 32), :] = res[c] * scale

    pairs(R // 32, unit_tile)
    if mine:
        for c in early:
            c.wait_recv()
        for c in next_:
            c.start()
        take_shares(stream, wide, got, w1, chan_s, gain_s)
        cols = pl.ds(pl.multiple_of(stream * D, 128), D)
        half = pltpu.make_async_remote_copy(
            src_ref=w1.at[:, cols], dst_ref=w1.at[:, cols], send_sem=hsem.at[0], recv_sem=hsem.at[1],
            device_id=(1 - stream, place), device_id_type=MESH,
        )
        half.start()
    else:
        st_o[...] = s_ref[...].astype(F32).T
        gain_s[...] = gain_row(st_o, wide)
        chan_s[...] = st_o[ROW_CHAN : ROW_CHAN + 8, :]
    saves = [
        pltpu.make_async_copy(v, h, out_sem.at[k])
        for k, (v, h) in enumerate(
            zip(
                (normed_o, x_o, act_o, dl_o, p_o, st_o, w1, res_o, other_o),
                (normed_h, x_h, act_h, dl_h, p_h, st_h, w1_h, res_h, other_h),
            )
        )
    ]

    def norm_tile(i, _):
        base = pl.multiple_of(i * 32, 32)
        for c in range(3):
            cols = slice(c * 128, c * 128 + 128)
            normed_o[pl.ds(base, 32), cols] = (tokf[c, pl.ds(base, 32), :] * gain_s[7:8, cols]).astype(BF)
        return 0

    lax.fori_loop(0, R // 32, norm_tile, 0)
    if mine:
        half.wait()
    x_o[:, 0:HALO, :] = jnp.zeros((G6, HALO, 128), F32)
    x_o[:, HALO + R : XR, :] = jnp.zeros((G6, HALO, 128), F32)
    for h in range(2):
        for c in range(0, G6, 2):
            y = dot(normed_o[h * 592 : h * 592 + 592, :], w1[:, c * 128 : c * 128 + 256])
            x_o[c, HALO + h * 592 : HALO + h * 592 + 592, :] = y[:, :128]
            x_o[c + 1, HALO + h * 592 : HALO + h * 592 + 592, :] = y[:, 128:]

    def conv(rev):
        def tile(i, _):
            base = pl.multiple_of(i * 32, 32)
            for c in range(G6):
                total, _l = conv_tile(x_o, lab, chan_s, c, base, 32, rev)
                act = total * sigmoid(total)
                act_o[c, pl.ds(base, 32), :] = act
                al_o[pl.ds(base, 32), c * 128 : c * 128 + 128] = act.astype(BF)
            return 0

        lax.fori_loop(0, R // 32, tile, 0)

    @pl.when(stream == 0)
    def _():
        conv(False)

    @pl.when(stream == 1)
    def _():
        conv(True)

    if mine:
        for c in next_:
            c.wait_recv()
        for k in range(wide):
            s_ref[k * ROWS_S : (k + 1) * ROWS_S, :] = gots[k]
        for c in early + next_:
            c.wait_send()
        for c in later:
            c.start()
        st_o[...] = s_ref[...].astype(F32).T
        st_o[ROW_CHAN : ROW_CHAN + 8, :] = chan_s[...]
    p_o[R:, :] = jnp.zeros((1280 - R, 128), F32)
    col = lax.broadcasted_iota(jnp.int32, (128, 256), 1)
    row = lax.broadcasted_iota(jnp.int32, (128, 256), 0)
    spread_c = jnp.where(row == ROW_C + col % N, 1.0, 0.0).astype(BF)
    diag = (
        lax.broadcasted_iota(jnp.int32, (592, 256), 0) % N
        == lax.broadcasted_iota(jnp.int32, (592, 256), 1) // N
    )
    for h in range(2):
        rows = slice(h * 592, h * 592 + 592)
        proj = dot(al_o[rows, :], s_ref[...])
        p_o[rows, :] = proj
        low = proj.astype(BF)
        cbd[rows, :] = jnp.where(diag, dot(low, spread_c), 0.0).astype(BF)
        step_in = low[:, :RANK]
        for c in range(0, G6, 2):
            w = st_o[ROW_STEP : ROW_STEP + RANK, c * 128 : c * 128 + 256].astype(BF)
            y = dot(step_in, w)
            dl_o[c, rows, :] = y[:, :128]
            dl_o[c + 1, rows, :] = y[:, 128:]
    stats_o[...] = jnp.zeros(stats_o.shape, F32)
    turn(p_o, ROW_B, turned)

    def soft(rev):
        def tile(i, _):
            base = pl.multiple_of(i * 32, 32)
            here = lab[pl.ds(base + HALO, 32), :]
            before = lab[pl.ds(base + HALO + (1 if rev else -1), 32), :]
            cut = jnp.where(here == before, 0.0, CUT)
            live = jnp.where(here >= 0, 1.0, 0.0)
            real = jnp.where(here >= -1, 1.0, 0.0)
            for c in range(G6):
                cols = slice(c * 128, c * 128 + 128)
                rows = pl.ds(base, 32)
                v = dl_o[c, rows, :] + st_o[ROW_CHAN + 5 : ROW_CHAN + 6, cols]
                delta = jnp.maximum(v, 0.0) + jnp.log1p(jnp.exp(-jnp.abs(v)))
                dl_o[c, rows, :] = delta
                dm[c, rows, :] = delta + cut
                u[c, rows, :] = delta * act_o[c, rows, :] * real
                t1 = live * delta
                t2 = t1 * delta
                for s in range(4):
                    stats_o[0, :, cols] += t1[8 * s : 8 * s + 8]
                    stats_o[1, :, cols] += t2[8 * s : 8 * s + 8]
            return 0

        lax.fori_loop(0, R // 32, tile, 0)

    @pl.when(stream == 0)
    def _():
        soft(False)

    @pl.when(stream == 1)
    def _():
        soft(True)

    for c in saves[:7]:
        c.start()
    hs = (hse, hso)

    def save(k, i):
        slot = i % RING
        return pltpu.make_async_copy(hs[k].at[slot], hs_o.at[k, i], sem.at[k, slot])

    def give(i, rev):
        row = pl.multiple_of((NP - 1 - i if rev else i) * 32, 32)
        at = pl.multiple_of(row if rev else row - WBASE, 32)
        k = i - (NP - SENDS)
        return pltpu.make_async_remote_copy(
            src_ref=res_o.at[pl.ds(row, 32), :], dst_ref=other_o.at[pl.ds(at, 32), :],
            send_sem=send.at[k], recv_sem=recv.at[k], device_id=(1 - stream, place), device_id_type=MESH,
        )

    def scan(rev):
        rate = [
            -jnp.exp(st_o[ROW_DECAY : ROW_DECAY + N, c * 128 : c * 128 + 128]) * LOG2E
            for c in range(G6)
        ]

        def block_of(t):
            return NB - 1 - t if rev else t

        def emit(t, k, slot, c):
            rows = rows16(block_of(t))
            y = dot(cbd[rows, :], hs[k][slot, :, c * 128 : c * 128 + 256])
            for h in range(2):
                cols = slice((c + h) * 128, (c + h) * 128 + 128)
                skip = st_o[ROW_CHAN + 6 : ROW_CHAN + 7, cols]
                res_o[rows, cols] = (
                    y[:, h * 128 : h * 128 + 128] + skip * act_o[c + h, rows, :]
                ).astype(BF)

        def block(t, k, slot, state, late):
            b = block_of(t)
            wide_b = turned[b]
            state = list(state)
            for n, j in enumerate(range(15, -1, -1) if rev else range(16)):
                if n % 4 == 0 and late:
                    late.pop(0)()
                q = b * 16 + j
                drive = jnp.broadcast_to(wide_b[:, j : j + 1], (N, 128))
                for c in range(G6):
                    fade = jnp.exp2(dm[c, pl.ds(q, 1), :] * rate[c])
                    state[c] = fade * state[c] + u[c, pl.ds(q, 1), :] * drive
                    hs[k][slot, j * N : j * N + N, c * 128 : c * 128 + 128] = state[c].astype(BF)
            return tuple(state)

        def pair(i, state):
            slot = i % RING

            @pl.when(i >= RING)
            def _():
                save(0, i - RING).wait()
                save(1, i - RING).wait()

            before = jnp.maximum(2 * i - 1, 0)
            late = [
                functools.partial(emit, before, 1, jnp.maximum(i - 1, 0) % RING, c)
                for c in (0, 2, 4)
            ]
            one = 1 + i // 1048576
            state = lax.fori_loop(0, one, lambda _, v, late=late: block(2 * i, 0, slot, v, list(late)), state)
            late = [functools.partial(emit, 2 * i, 0, slot, c) for c in (0, 2, 4)]
            state = lax.fori_loop(0, one, lambda _, v, late=late: block(2 * i + 1, 1, slot, v, list(late)), state)
            save(0, i).start()
            save(1, i).start()

            @pl.when(i > NP - SENDS)
            def _():
                give(i - 1, rev).start()

            return state

        hso[0] = jnp.zeros((256, E), BF)
        lax.fori_loop(0, NP, pair, tuple(jnp.zeros((N, 128), F32) for _ in range(G6)))
        for c in (0, 2, 4):
            emit(NB - 1, 1, (NP - 1) % RING, c)
        give(NP - 1, rev).start()
        for i in range(NP - RING, NP):
            save(0, i).wait()
            save(1, i).wait()

        def settle(i, _):
            give(i, rev).wait()
            return 0

        lax.fori_loop(NP - SENDS, NP, settle, 0)

    @pl.when(stream == 0)
    def _():
        scan(False)

    @pl.when(stream == 1)
    def _():
        scan(True)

    for c in saves[7:]:
        c.start()
    if mine:
        for c in later:
            c.wait()
        packed = pltpu.make_async_copy(pack, pack_h[0], out_sem.at[9])
        packed.start()
        packed.wait()
    for c in saves:
        c.wait()


def forward(wide, mine, count, offset, stride, tok, *given):
    S = jax.ShapeDtypeStruct
    V = pltpu.VMEM
    kept = [
        ((R, D), BF), ((G6, XR, 128), F32), ((G6, R, 128), F32), ((G6, R, 128), F32), ((1280, 128), F32),
        ((128, E), F32), ((R, E), BF), ((WIN, E), BF), ((D, E), BF),
    ]
    pack = [((wide, 2 * D // wide, E), BF)] if mine else []
    dma = pltpu.SemaphoreType.DMA
    links = [
        V((128, 128), F32), V((ROWS_P, 128), BF), V((wide, ROWS_P, 128), BF), V((ROWS_S, 128), BF),
        V((wide, ROWS_S, 128), BF), V(pack[0][0][1:], BF), V(*pack[0]),
        dma((wide,)), dma((wide,)), dma((wide,)), dma((wide,)), dma((wide,)), dma((wide,)), dma((2,)),
    ] if mine else []
    return pl.pallas_call(
        functools.partial(fwd_kernel, wide, mine),
        out_shape=[S(*k) for k in kept + pack] + [S((2, 8, E), F32), S((2, NP, 256, E), BF)],
        in_specs=[SMEM] * 3 + [VMEM] * (1 + len(given)),
        out_specs=[ANY] * len(kept + pack) + [VMEM, ANY],
        scratch_shapes=[V(*k) for k in kept]
        + [
            V((R, E), BF), V((E, 128), BF), V((XR, 128), jnp.int32), V((G6, R, 128), F32), V((G6, R, 128), F32),
            V((R, 256), BF), V((RING, 256, E), BF), V((RING, 256, E), BF), V((8, D), F32),
            V((3, R, 128), F32), V((8, D), F32), V((NB, N, 128), F32), V((8, E), F32),
            dma((2, RING)), dma((10,)), dma((SENDS,)), dma((SENDS,)),
        ]
        + links,
        compiler_params=pltpu.CompilerParams(
            vmem_limit_bytes=60 * 2**20, collective_id=3, has_side_effects=True
        ),
        cost_estimate=pl.CostEstimate(flops=int(5e10), bytes_accessed=1 << 20, transcendentals=0),
        name="forward",
    )(count, offset, stride, tok, *given)


def middle(meta, wide, tokf, etab, cot, normed, own, other, w2, wo, cotw, gated, bgrad, ggrad, blk, mg, gpart, stage, sent, shared):
    stream = meta[4]
    wbase = pl.multiple_of(stream * WBASE, 32)
    lay_cotangent(stream, cot, cotw)
    win = pl.ds(wbase, WIN)

    def tile(i, _):
        base = pl.multiple_of(i * 32, 32)
        r = wbase + base + lax.broadcasted_iota(jnp.int32, (32, 128), 0)
        live = jnp.where(labels_of(meta, r)[0] >= 0, 1.0, 0.0)
        for c in range(3):
            v = live * cotw[c, pl.ds(base, 32), :]
            ref, col = (bgrad[0], c * 128) if c < 2 else (bgrad[1], 0)
            ref[pl.ds(base, 32), col : col + 128] = v.astype(BF)
        return 0

    lax.fori_loop(0, WIN // 32, tile, 0)

    def branch_grad():
        return jnp.concatenate([bgrad[0][0:WIN, :], bgrad[1][0:WIN, 0:128]], 1)

    for c in range(0, E, 256):
        cols = slice(c, c + 256)
        gate = dot(normed[win, :], w2[:, cols])
        mixed = own(cols) + other(cols)
        sig = sigmoid(gate)
        silu = gate * sig
        gated[0:WIN, cols] = (mixed * silu).astype(BF)
        up = dot_nt(branch_grad(), wo[cols, :])
        mg[:, cols] = (up * silu).astype(BF)
        ggrad[0:WIN, cols] = (up * mixed * sig * (1.0 + gate * (1.0 - sig))).astype(BF)
        sent(c // 256).start()
    drow, erow = D // wide, E // wide
    rows = 2 * drow
    pitch = -(-rows // 8) * 8
    for c in range(0, D, 128):
        g = dot_tn(normed[win, c : c + 128], ggrad[0:WIN, :])
        lay_rows(g, c, drow, lambda k, r, v: put(stage, pitch, k, r, 0, v))
    for c in range(0, E, 256):
        g = dot_tn(gated[0:WIN, c : c + 256], branch_grad())
        half = erow // 2
        lay_rows(g, c, half, lambda k, r, v: put(stage, pitch, k // 2, drow + r, (k % 2) * D, v))
    shared(rows, pitch)
    for c in range(0, D, 128):
        cols = slice(c, c + 128)
        blk[c // 128, 0:WIN, :] = dot(gated[0:WIN, :], wo[:, cols])
        gpart[:, cols] = dot_nt(ggrad[0:WIN, :], w2[cols, :])

    def out_tile(i, _):
        base = pl.multiple_of(i * 32, 32)
        at = pl.multiple_of(wbase + base, 32)
        res, live = residual_tile(meta, tokf, etab, at, 32)
        for c in range(3):
            blk[c, pl.ds(base, 32), :] = res[c] + live * blk[c, pl.ds(base, 32), :]
        return 0

    lax.fori_loop(0, WIN // 32, out_tile, 0)


WINDOWS = ((0, 0), (1, WIN - HALF - 8))


def lay_cotangent(stream, cot, cotw):
    cotw[:, 0:WIN, :] = jnp.zeros((3, WIN, 128), F32)
    for s, off in WINDOWS:

        @pl.when(stream == s)
        def _():
            for c in range(3):
                cotw[c, off : off + HALF, :] = cot[:, c * 128 : c * 128 + 128].astype(F32)


def take_half(stream, src, out, sem):
    def copy(off, c):
        return pltpu.make_async_copy(
            src.at[c, off : off + HALF, :], out.at[:, 0, c * 128 : c * 128 + 128], sem.at[c]
        )

    for s, off in WINDOWS:

        @pl.when(stream == s)
        def _():
            for c in range(3):
                copy(off, c).start()

    def wait():
        for c in range(3):
            copy(0, c).wait()

    return wait


def put(ref, pitch, k, r, col, v):
    for c in range(0, v.shape[1], 128):
        at = (k * G6 + (col + c) // 128) * pitch + r
        ref[at : at + v.shape[0], :] = v[:, c : c + 128]


def lay_rows(v, start, size, store):
    at = 0
    while at < v.shape[0]:
        k, r = divmod(start + at, size)
        n = min(size - r, v.shape[0] - at)
        store(k, r, v[at : at + n])
        at += n


def unpack(pack, w2, wo, wide):
    drow, half = D // wide, E // wide // 2
    per = max(1, 16 // math.gcd(16, drow))
    for k in range(0, wide, per):
        v = [pack[k + i].astype(F32) for i in range(per)]
        w2[k * drow : (k + per) * drow, :] = jnp.concatenate([t[0:drow] for t in v], 0).astype(BF)
        pieces = []
        for t in v:
            pieces += [t[drow : drow + half, 0:D], t[drow : drow + half, D : 2 * D]]
        wo[2 * k * half : 2 * (k + per) * half, :] = jnp.concatenate(pieces, 0).astype(BF)


def bwd_kernel(wide, mine, *refs):
    refs = list(refs)
    count, offset, stride, tok, cot, normed, pack, stats, w1, st, res_h, other_h, x_h, act_h, dl_h, p_h, hs_in = refs[:17]
    if mine:
        block_h, tg_h, own_o, twin_o, g2_o, g2x_o = refs[17:23]
    else:
        block_h, tg_h, gw1, gsm, gg_o, g2_o = refs[17:23]
    (
        x, act, dl, p, w2, wo, gpart, mg, mgx, nrecv,
        lab, dm, dy, dyb, ub, bb, bbd, dbm, dcm, dd, zs, dacc, hse, hso, g0, g1, z0, z1, pb0, pb1, pc0, pc1, sel, sums,
        etab, gain_s, acc, turned, sem, in_sem, out_sem, mgsend, mgrecv, swsend, swrecv, win_sem, *links,
    ) = refs[23:]
    if mine:
        g2s, g2r, gw1, gsm, pout, pin, out, got, sout, sin, gout, gin, *sems = links
    stream, place = lax.axis_index("dir"), lax.axis_index("wide")
    wbase = pl.multiple_of(stream * WBASE, 32)
    loads = [
        pltpu.make_async_copy(h, v, in_sem.at[k])
        for k, (h, v) in enumerate(zip((x_h, act_h, dl_h, p_h), (x, act, dl, p)))
    ]
    windows = []
    for i, (h, v, at) in enumerate(((res_h, hse, wbase), (other_h, hso, 0))):
        for k in range(0, WIN, 256):
            n = min(256, WIN - k)
            rows = pl.ds(pl.multiple_of(at + k, 32), n)
            windows.append(
                pltpu.make_async_copy(h.at[rows, :], v.at[k // 256, 0:n, :], win_sem.at[i, k // 256])
            )
    for c in windows + loads:
        c.start()

    def window(ref, cols):
        rows = [ref[k // 256, 0 : min(256, WIN - k), cols] for k in range(0, WIN, 256)]
        return jnp.concatenate(rows, 0).astype(F32)

    if mine:
        greet(stream, place, wide)
    else:
        bar = pltpu.get_barrier_semaphore()
        pl.semaphore_signal(bar, inc=1, device_id=(1 - stream, place), device_id_type=MESH)
        pl.semaphore_wait(bar, 1)
    meta = views(count, offset, stream)
    partner = dict(device_id=(1 - stream, place), device_id_type=MESH)
    fill_embedding(stride, etab)
    fill_labels(meta, lab)
    tokf, cotw, blk = zs.at[0:3], zs.at[3:6], dd.at[0:3]
    lay_tokens(tok, tokf)
    unpack(pack, w2, wo, wide)

    def sent(k):
        cols = slice(k * 256, k * 256 + 256)
        return pltpu.make_async_remote_copy(
            src_ref=mg.at[:, cols], dst_ref=mgx.at[:, cols], send_sem=mgsend.at[k], recv_sem=mgrecv.at[k], **partner
        )

    g2 = []
    if mine:
        for k in range(1, wide):
            g2.append(
                pltpu.make_async_remote_copy(
                    src_ref=g2s.at[place ^ k], dst_ref=g2r.at[k], send_sem=sems[0].at[k], recv_sem=sems[1].at[k],
                    device_id=(stream, place ^ k), device_id_type=MESH,
                )
            )

    def deal(src, dst, n):
        return [
            pltpu.make_async_remote_copy(
                src_ref=src.at[place ^ k], dst_ref=dst.at[k], send_sem=sems[n].at[k], recv_sem=sems[n + 1].at[k],
                device_id=(stream, place ^ k), device_id_type=MESH,
            )
            for k in range(1, wide)
        ]

    def collect(copies, src, dst):
        for c in copies:
            c.wait()
        total = src[place].astype(F32)
        for k in range(1, wide):
            total = total + dst[k].astype(F32)
        return total

    def shared(rows, pitch):
        for k in range(wide):
            for c in range(G6):
                at = (k * G6 + c) * pitch
                cols = slice(c * 128, c * 128 + 128)
                if mine:
                    g2s[k, :, cols] = bb[at : at + rows, :].astype(BF)
                else:
                    g2_o[k, :, cols] = bb[at : at + rows, :]
        for c in g2:
            c.start()

    for c in windows:
        c.wait()
    middle(
        meta, wide, tokf, etab, cot, normed, lambda cols: window(hse, cols), lambda cols: window(hso, cols),
        w2, wo, cotw, ub, (dbm, dcm), dyb, blk, mg, gpart, bb, sent, shared,
    )
    block_out = take_half(stream, blk, block_h, out_sem.at[0])
    for c in loads:
        c.wait()
    turn(p, ROW_C, turned)

    def prep(rev):
        def tile(i, _):
            base = pl.multiple_of(i * 32, 32)
            rows = pl.ds(base, 32)
            here = lab[pl.ds(base + HALO, 32), :]
            before = lab[pl.ds(base + HALO + (1 if rev else -1), 32), :]
            cut = jnp.where(here == before, 0.0, CUT)
            spread_tile(turned, 2 * i, bb)
            spread_tile(turned, 2 * i + 1, bb)
            for c in range(G6):
                dm[c, rows, :] = dl[c, rows, :] + cut
            return 0

        lax.fori_loop(0, R // 32, tile, 0)

    @pl.when(stream == 0)
    def _():
        prep(False)

    @pl.when(stream == 1)
    def _():
        prep(True)

    col = lax.broadcasted_iota(jnp.int32, (128, 256), 1)
    row = lax.broadcasted_iota(jnp.int32, (128, 256), 0)
    spread_b = jnp.where(row == ROW_B + col % N, 1.0, 0.0).astype(BF)
    diag = (
        lax.broadcasted_iota(jnp.int32, (592, 256), 0) % N
        == lax.broadcasted_iota(jnp.int32, (592, 256), 1) // N
    )
    for h in range(2):
        rows = slice(h * 592, h * 592 + 592)
        bbd[rows, :] = jnp.where(diag, dot(p[rows, :].astype(BF), spread_b), 0.0).astype(BF)
    for k in range(3):
        sent(k).wait()
    block_out()
    sums[...] = jnp.zeros(sums.shape, F32)

    for s, lowref, highref in ((0, mg, mgx), (1, mgx, mg)):

        @pl.when(stream == s)
        def _():
            def lay(i, _):
                base = pl.multiple_of(i * 32, 32)
                lowat = pl.multiple_of(jnp.minimum(base, WIN - 32), 32)
                highat = pl.multiple_of(jnp.maximum(base - WBASE, 0), 32)
                for c in range(G6):
                    cols = slice(c * 128, c * 128 + 128)
                    lowrow = lowref[pl.ds(lowat, 32), cols].astype(F32)
                    highrow = highref[pl.ds(highat, 32), cols].astype(F32)
                    v = jnp.where(base < WIN, lowrow, 0.0) + jnp.where(base >= WBASE, highrow, 0.0)
                    dy[c, pl.ds(base, 32), :] = v
                    t = v * act[c, pl.ds(base, 32), :]
                    sums[0, :, cols] += t[0:8] + t[8:16] + t[16:24] + t[24:32]
                return 0

            lax.fori_loop(0, R // 32, lay, 0)

    i = lax.broadcasted_iota(jnp.int32, (32, 256), 0)
    j = lax.broadcasted_iota(jnp.int32, (32, 256), 1)
    sel[...] = jnp.where(i == jnp.where(i < N, j // N, N + j % N), 1.0, 0.0).astype(BF)
    dacc[...] = jnp.zeros(dacc.shape, F32)
    hs, gs, zz, pb, pc = (hse, hso), (g0, g1), (z0, z1), (pb0, pb1), (pc0, pc1)

    def load(k, i):
        slot = i % RING
        return pltpu.make_async_copy(hs_in.at[k, i], hs[k].at[slot], sem.at[k, slot])

    def scan(rev):
        rate = [
            -jnp.exp(st[ROW_DECAY : ROW_DECAY + N, c * 128 : c * 128 + 128]) * LOG2E
            for c in range(G6)
        ]
        block_diag = (
            lax.broadcasted_iota(jnp.int32, (N, 256), 0)
            == lax.broadcasted_iota(jnp.int32, (N, 256), 1) // N
        )

        def block_of(t):
            return NB - 1 - t if rev else t

        def drive_dot(t, k, c):
            rows = rows16(block_of(t))
            y = dot(bbd[rows, :], gs[k][:, c * 128 : c * 128 + 256])
            dd[c, rows, :] = y[:, :128]
            dd[c + 1, rows, :] = y[:, 128:]

        def step_dot(t, k, c, first):
            rows = rows16(block_of(t))
            y = dot(sel[...], zz[k][:, c * 128 : c * 128 + 256])
            zs[c, rows, :] = y[:N, :128]
            zs[c + 1, rows, :] = y[:N, 128:]
            dacc[c] += jnp.where(first, 0.0, y[N:, :128])
            dacc[c + 1] += jnp.where(first, 0.0, y[N:, 128:])

        ones = jnp.ones((N, 128), BF)

        def b_dot(t, k):
            rows = rows16(block_of(t))
            dbm[rows, :] = jnp.where(block_diag, dot_nt(ones, pb[k][...]), 0.0).astype(BF)

        def c_dot(t, k):
            rows = rows16(block_of(t))
            dcm[rows, :] = jnp.where(block_diag, dot_nt(ones, pc[k][...]), 0.0).astype(BF)

        def block(t, k, slot, pslot, carry, late):
            b = block_of(t)
            carry = list(carry)
            late = list(late)
            start = 0 if rev else 15
            now = [hs[k][slot, start * N : start * N + N, c * 128 : c * 128 + 128] for c in range(G6)]
            for n, j in enumerate(range(16) if rev else range(15, -1, -1)):
                if n % 2 == 0 and late:
                    late.pop(0)()
                q = b * 16 + j
                cb = bb[pl.ds(pl.multiple_of(q * N, N), N), :]
                jp = j + 1 if rev else j - 1
                if 0 <= jp < 16:
                    old_ref, old_slot = hs[k], slot
                else:
                    jp = 0 if rev else 15
                    old_ref, old_slot = hs[1 - k], pslot
                sum_b = sum_c = None
                for c in range(G6):
                    cols = slice(c * 128, c * 128 + 128)
                    w = dm[c, pl.ds(q, 1), :] * rate[c]
                    fade = jnp.exp2(w)
                    up = dy[c, pl.ds(q, 1), :]
                    g = cb * up + carry[c]
                    carry[c] = fade * g
                    old = old_ref[old_slot, jp * N : jp * N + N, cols]
                    low = g.astype(BF)
                    gs[k][j * N : j * N + N, cols] = low
                    zz[k][j * N : j * N + N, cols] = (w * carry[c]).astype(BF) * old
                    drive = dl[c, pl.ds(q, 1), :] * act[c, pl.ds(q, 1), :]
                    tb = low * jnp.broadcast_to(drive, (N, 128)).astype(BF)
                    tc = now[c] * jnp.broadcast_to(up, (N, 128)).astype(BF)
                    sum_b = tb if sum_b is None else sum_b + tb
                    sum_c = tc if sum_c is None else sum_c + tc
                    now[c] = old
                pb[k][j * N : j * N + N, :] = sum_b
                pc[k][j * N : j * N + N, :] = sum_c
            return tuple(carry)

        def pair(ii, carry):
            i = NP - 1 - ii
            slot = i % RING
            pslot = jnp.maximum(i - 1, 0) % RING

            @pl.when(i >= 1)
            def _():
                load(0, i - 1).wait()
                load(1, i - 1).wait()

            @pl.when(i >= 3)
            def _():
                load(0, i - 3).start()
                load(1, i - 3).start()

            one = 1 + i // 1048576
            for k in (1, 0):
                t = 2 * i + k
                after = jnp.minimum(t + 1, NB - 1)
                first = t + 1 > NB - 1
                late = [functools.partial(b_dot, after, 1 - k), functools.partial(c_dot, after, 1 - k)]
                late += [functools.partial(drive_dot, after, 1 - k, c) for c in (0, 2, 4)]
                late += [functools.partial(step_dot, after, 1 - k, c, first) for c in (0, 2, 4)]
                ps = slot if k == 1 else pslot
                carry = lax.fori_loop(
                    0, one, lambda _, cc, t=t, k=k, ps=ps, late=late: block(t, k, slot, ps, cc, late), carry
                )
            return carry

        for i in range(NP - 1, NP - 4, -1):
            load(0, i).start()
            load(1, i).start()
        load(0, NP - 1).wait()
        load(1, NP - 1).wait()
        for ref in (g0, z0, pb0, pc0):
            ref[...] = jnp.zeros(ref.shape, BF)
        lax.fori_loop(0, NP, pair, tuple(jnp.zeros((N, 128), F32) for _ in range(G6)))
        for c in (0, 2, 4):
            drive_dot(0, 0, c)
            step_dot(0, 0, c, False)
        b_dot(0, 0)
        c_dot(0, 0)

    @pl.when(stream == 0)
    def _():
        scan(False)

    @pl.when(stream == 1)
    def _():
        scan(True)

    def step_tile(i, _):
        base = pl.multiple_of(i * 32, 32)
        rows = pl.ds(base, 32)
        for c in range(G6):
            cols = slice(c * 128, c * 128 + 128)
            delta, a, d = dl[c, rows, :], act[c, rows, :], dd[c, rows, :]
            near = 1.0 - delta * (0.5 - delta * (1.0 / 6.0 - delta * (1.0 / 24.0)))
            ratio = jnp.where(delta < 0.03, near, (1.0 - jnp.exp(-delta)) / delta)
            pre = ratio * (zs[c, rows, :] * LN2 + a * d * delta)
            ub[rows, cols] = pre.astype(BF)
            dm[c, rows, :] = delta * d + st[ROW_CHAN + 6 : ROW_CHAN + 7, cols] * dy[c, rows, :]
            sums[1, :, cols] += pre[0:8] + pre[8:16] + pre[16:24] + pre[24:32]
        return 0

    lax.fori_loop(0, R // 32, step_tile, 0)
    pgs = bbd.at[:, 0:128]
    w_step = st[ROW_STEP : ROW_STEP + RANK, :].astype(BF)
    w_b = jnp.concatenate([st[ROW_B : ROW_B + N, :]] * N, 0).astype(BF)
    w_c = jnp.concatenate([st[ROW_C : ROW_C + N, :]] * N, 0).astype(BF)
    w_s = st[0:RANK, :].astype(BF)
    for h in range(2):
        rows = slice(h * 592, h * 592 + 592)
        sg = dot_nt(ub[rows, :], w_step).astype(BF)
        pgs[rows, :] = jnp.concatenate([sg, jnp.zeros((592, 128 - RANK), BF)], 1)
        for c in range(0, G6, 2):
            cols = slice(c * 128, c * 128 + 256)
            y = dot(sg, w_s[:, cols]) + dot(dbm[rows, :], w_b[:, cols]) + dot(dcm[rows, :], w_c[:, cols])
            dm[c, rows, :] += y[:, :128]
            dm[c + 1, rows, :] += y[:, 128:]
    low = p[0:R, :].astype(BF)
    gstep = dot_tn(low, ub[...])[0:RANK]

    def activation(i, _):
        rows = pl.ds(pl.multiple_of(i * 32, 32), 32)
        for c in range(G6):
            ub[rows, c * 128 : c * 128 + 128] = act[c, rows, :].astype(BF)
        return 0

    lax.fori_loop(0, R // 32, activation, 0)
    top = dot_tn(pgs[...], ub[...])
    gb = dot_tn(dbm[...], ub[...])
    gc = dot_tn(dcm[...], ub[...])
    gb = sum(gb[k * N : k * N + N] for k in range(N))
    gc = sum(gc[k * N : k * N + N] for k in range(N))
    gdecay = jnp.concatenate([dacc[c] for c in range(G6)], 1) * LN2
    gt = jnp.concatenate([top[0:RANK], gb, gc, gstep, gdecay, jnp.zeros((128 - ROW_CHAN, E), F32)], 0)
    gsm[...] = gt.T
    if mine:
        for k in range(wide):
            sout[k] = gsm[k * ROWS_S : (k + 1) * ROWS_S, :].astype(BF)
        smalls = deal(sout, sin, 2)
        for c in smalls:
            c.start()
    dc = dd
    dc[:, 0:HALO, :] = jnp.zeros((G6, HALO, 128), F32)
    dc[:, HALO + R : XR, :] = jnp.zeros((G6, HALO, 128), F32)

    def conv(rev):
        def first(i, _):
            base = pl.multiple_of(i * 32, 32)
            for c in range(G6):
                cols = slice(c * 128, c * 128 + 128)
                total, lagged = conv_tile(x, lab, st.at[ROW_CHAN : ROW_CHAN + 8], c, base, 32, rev)
                sig = sigmoid(total)
                v = dm[c, pl.ds(base, 32), :] * sig * (1.0 + total * (1.0 - sig))
                dc[c, pl.ds(base + HALO, 32), :] = v
                sums[2, :, cols] += v[0:8] + v[8:16] + v[16:24] + v[24:32]
                for j in range(4):
                    t = v * lagged[j]
                    sums[3 + j, :, cols] += t[0:8] + t[8:16] + t[16:24] + t[24:32]
            return 0

        def second(i, _):
            base = pl.multiple_of(i * 32, 32)
            here = lab[pl.ds(base + HALO, 32), :]
            for c in range(G6):
                cols = slice(c * 128, c * 128 + 128)
                v = dc[c, pl.ds(base + HALO, 32), :] * st[ROW_CHAN : ROW_CHAN + 1, cols]
                for j in (1, 2, 3):
                    at = base + HALO + (-j if rev else j)
                    same = lab[pl.ds(at, 32), :] == here
                    later = jnp.where(same, dc[c, pl.ds(at, 32), :], 0.0)
                    v = v + later * st[ROW_CHAN + j : ROW_CHAN + j + 1, cols]
                dyb[pl.ds(base, 32), cols] = v.astype(BF)
            return 0

        lax.fori_loop(0, R // 32, first, 0)
        lax.fori_loop(0, R // 32, second, 0)

    @pl.when(stream == 0)
    def _():
        conv(False)

    @pl.when(stream == 1)
    def _():
        conv(True)

    theirs = pl.ds(pl.multiple_of((1 - stream) * WBASE, 32), WIN)
    nsend = mg.at[:, 0:D]
    nsend[...] = dot_nt(dyb[theirs, :], w1[...]).astype(BF)
    nswap = pltpu.make_async_remote_copy(
        src_ref=nsend, dst_ref=nrecv, send_sem=swsend.at[0], recv_sem=swrecv.at[0], **partner
    )
    nswap.start()
    for c in range(0, D, 128):
        gw1[c : c + 128, :] = dot_tn(normed[:, c : c + 128], dyb[...])
    if mine:
        for s in range(2):

            @pl.when(stream == s)
            def _():
                pout[...] = gw1[:, (1 - s) * D : (2 - s) * D].astype(BF)

        pre = pltpu.make_async_remote_copy(
            src_ref=pout, dst_ref=pin, send_sem=swsend.at[1], recv_sem=swrecv.at[1], **partner
        )
        pre.start()
    def total(k):
        return jnp.sum(sums[k], axis=0, keepdims=True)

    fine = [jnp.sum(stats[k], axis=0, keepdims=True) * (1.0 / VIEW_TOK) for k in range(2)]
    coarse = [v.astype(BF).astype(F32) for v in fine]
    fine = [a - b for a, b in zip(fine, coarse)]
    chan = [total(3 + k) for k in range(4)] + [total(2), total(1), total(0)]
    if mine:
        gpart[...] += dot_nt(dyb[pl.ds(wbase, WIN), :], w1[...])
        pre.wait()
        fill_owners(stream, wide, gw1, pin, out)
        shares = deal(out, got, 4)
        for c in shares:
            c.start()
    else:
        rest = chan + [jnp.zeros((1, E), F32)] + coarse + fine
        gsm[...] += jnp.concatenate([jnp.zeros((ROW_CHAN, E), F32)] + rest + [jnp.zeros((20, E), F32)], 0).T
        gpart[...] += dot_nt(dyb[pl.ds(wbase, WIN), :], w1[...])
    nswap.wait()
    ending(meta, wide, tok, etab, cot, nrecv, gpart, st, zs.at[0:3], zs.at[3:6], dd.at[0:3], gain_s, acc)
    token_out = take_half(stream, dd.at[0:3], tg_h, out_sem.at[1])
    if not mine:
        gg_o[...] = acc[...]
        token_out()
        return
    gain = jnp.sum(acc[...], axis=0, keepdims=True)
    rows = jnp.concatenate(chan + [jnp.zeros((1, E), F32)] + coarse + fine + [jnp.zeros((4, E), F32)], 0)
    for k in range(wide):
        piece = rows[:, k * ROWS_S : (k + 1) * ROWS_S]
        owned = jnp.concatenate([gain[:, k * ROWS_W : (k + 1) * ROWS_W], jnp.zeros((1, ROWS_S - ROWS_W), F32)], 1)
        at = lax.broadcasted_iota(jnp.int32, (ROWS_C, ROWS_S), 0)
        piece = jnp.where(at == 7, jnp.broadcast_to(owned, (ROWS_C, ROWS_S)), piece)
        gout[k] = jnp.concatenate([piece, jnp.zeros((ROWS_C, 128 - ROWS_S), F32)], 1).astype(BF)
    gains = deal(gout, gin, 6)
    for c in gains:
        c.start()
    for c in g2:
        c.wait()
    for r in range(0, g2_o.shape[0], 24):
        rows = slice(r, r + 24)
        total = g2s[place].astype(F32)[rows]
        for k in range(1, wide):
            total = total + g2r[k].astype(F32)[rows]
        g2_o[rows, :] = total
    g2swap = pltpu.make_async_remote_copy(
        src_ref=g2_o, dst_ref=g2x_o, send_sem=swsend.at[2], recv_sem=swrecv.at[2], **partner
    )
    g2swap.start()
    own_o[0:ROWS_S, :] = collect(smalls, sout, sin)
    own_o[ROWS_S:AT_C, :] = collect(shares, out, got)
    own_o[AT_C:PACK, :] = collect(gains, gout, gin)
    last = pltpu.make_async_remote_copy(
        src_ref=own_o, dst_ref=twin_o, send_sem=swsend.at[3], recv_sem=swrecv.at[3], **partner
    )
    last.start()
    token_out()
    g2swap.wait()
    last.wait()


def ending(meta, wide, tok, etab, cot, other, gpart, st, tokf, cotw, out, gain_s, acc):
    stream = meta[4]
    wbase = pl.multiple_of(stream * WBASE, 32)
    lay_tokens(tok, tokf)
    lay_cotangent(stream, cot, cotw)
    gain_s[...] = gain_row(st, wide)
    acc[...] = jnp.zeros(acc.shape, F32)
    lo = stream * HALF

    def tile(i):
        base = i * 32 if isinstance(i, int) else pl.multiple_of(i * 32, 32)
        at = pl.multiple_of(wbase + base, 32)
        rows = pl.ds(base, 32)
        res, _l = residual_tile(meta, tokf, etab, at, 32)
        scale = row_scale(res)
        r = at + lax.broadcasted_iota(jnp.int32, (32, 128), 0)
        mine = (r >= lo) & (r < lo + HALF)
        ng, un = [], []
        for c in range(3):
            cols = slice(c * 128, c * 128 + 128)
            v = gpart[rows, cols] + other[rows, cols].astype(F32)
            unit = res[c] * scale
            t = jnp.where(mine, v * unit, 0.0)
            acc[:, cols] += t[0:8] + t[8:16] + t[16:24] + t[24:32]
            ng.append(v * gain_s[0:1, cols])
            un.append(unit)
        mean = sum(jnp.sum(a * b, axis=1, keepdims=True) for a, b in zip(ng, un)) * (1.0 / D)
        for c in range(3):
            out[c, rows, :] = cotw[c, rows, :] + scale * (ng[c] - un[c] * mean)

    pairs(WIN // 32, tile)


def backward(wide, mine, *args):
    S = jax.ShapeDtypeStruct
    V = pltpu.VMEM
    dma = pltpu.SemaphoreType.DMA
    big = V((G6, R, 128), F32)
    rows = 2 * D // wide
    half = S((HALF, 1, D), F32)
    if mine:
        outs = [S((PACK, 128), F32), S((PACK, 128), F32), S((rows, E), F32), S((rows, E), F32)]
        links = [
            V((wide, rows, E), BF), V((wide, rows, E), BF), V((D, E), F32), V((E, 128), F32), V((D, D), BF), V((D, D), BF),
            V((wide, ROWS_P, 128), BF), V((wide, ROWS_P, 128), BF), V((wide, ROWS_S, 128), BF), V((wide, ROWS_S, 128), BF),
            V((wide, ROWS_C, 128), BF), V((wide, ROWS_C, 128), BF),
        ] + [dma((wide,))] * 8
    else:
        outs = [S((D, E), F32), S((E, 128), F32), S((8, D), F32), S((wide, rows, E), F32)]
        links = []
    return pl.pallas_call(
        functools.partial(bwd_kernel, wide, mine),
        out_shape=[half, half] + outs,
        in_specs=[SMEM] * 3 + [VMEM] * 7 + [ANY] * 7,
        out_specs=[ANY] * 2 + [VMEM] * 4,
        scratch_shapes=[
            V((G6, XR, 128), F32), big, big, V((1280, 128), F32),
            V((D, E), BF), V((E, D), BF), V((WIN, D), F32), V((WIN, E), BF), V((WIN, E), BF), V((WIN, D), BF),
            V((XR, 128), jnp.int32), big, big, V((R, E), BF), V((R, E), BF), V((R * N, 128), F32),
            V((R, 256), BF), V((R, 256), BF), V((R, 256), BF), V((G6, XR, 128), F32), big, V((G6, N, 128), F32),
            V((RING, 256, E), BF), V((RING, 256, E), BF),
            V((256, E), BF), V((256, E), BF), V((256, E), BF), V((256, E), BF),
            V((256, 128), BF), V((256, 128), BF), V((256, 128), BF), V((256, 128), BF), V((32, 256), BF), V((7, 8, E), F32),
            V((8, D), F32), V((8, D), F32), V((8, D), F32), V((NB, N, 128), F32),
            dma((2, RING)), dma((4,)), dma((2, 3)), dma((3,)), dma((3,)), dma((4,)), dma((4,)), dma((2, 3)),
        ]
        + links,
        compiler_params=pltpu.CompilerParams(
            vmem_limit_bytes=63 * 2**20, collective_id=4, has_side_effects=True
        ),
        cost_estimate=pl.CostEstimate(flops=int(9e10), bytes_accessed=1 << 20, transcendentals=0),
        name="backward",
    )(*args)


ROWS_W = 24
ROWS_P = 80
ROWS_S = 48
ROWS_C = 16
PACK = ROWS_S + ROWS_P + ROWS_C
AT_C = ROWS_S + ROWS_P


def greet(d, w, wide):
    bar = pltpu.get_barrier_semaphore()
    for k in range(1, wide):
        pl.semaphore_signal(bar, inc=1, device_id=(d, w ^ k), device_id_type=MESH)
    pl.semaphore_signal(bar, inc=1, device_id=(1 - d, w), device_id_type=MESH)
    pl.semaphore_wait(bar, wide)


def fill_shares(d, given, stage, first, small, second):
    inp, out, state, step, decay, chan, gain = given
    stage[...] = jnp.zeros(stage.shape, F32)
    stage[ROW_STEP:ROW_DECAY, 0:ROWS_S] = step[0]
    stage[ROW_DECAY:ROW_CHAN, 0:ROWS_S] = decay[0]
    for k in range(7):
        stage[ROW_CHAN + k : ROW_CHAN + k + 1, 0:ROWS_S] = chan[k]
    stage[ROW_GAIN : ROW_GAIN + 1, 0:ROWS_W] = gain[...]
    parts = []
    for c in range(3):
        low, high = inp[:, c * 128 : c * 128 + 128], inp[:, D + c * 128 : D + c * 128 + 128]
        parts.append(jnp.where(d == 0, low, high))
    first[...] = jnp.concatenate(parts + [stage[ROW_CHAN : ROW_CHAN + 8, :]], 0).astype(BF)
    turned = stage[...].T[0:ROWS_S]
    stage[0:ROWS_S, 0:ROW_STEP] = state[0]
    col = lax.broadcasted_iota(jnp.int32, (ROWS_S, 128), 1)
    small[...] = jnp.where(col < ROW_STEP, stage[0:ROWS_S, :], turned).astype(BF)
    pair = jnp.concatenate([out[0:ROWS_W, :], out[ROWS_W : 2 * ROWS_W, :]], 1)
    second[...] = jnp.concatenate([inp[:, E:], pair], 0).astype(BF)


def take_shares(d, wide, got, w1, chan_s, gain_s):
    lane = lax.broadcasted_iota(jnp.int32, (8, 128), 1)

    def lay(tiles, piece, at):
        t, r = divmod(at, 128)
        moved = pltpu.roll(piece, r, 1) if r else piece
        tiles[t] = tiles[t] + jnp.where(lane >= r, moved, 0.0)
        if t + 1 < len(tiles):
            tiles[t + 1] = tiles[t + 1] + jnp.where(lane < r, moved, 0.0)

    chan = [jnp.zeros((8, 128), F32) for _ in range(E // 128)]
    gain = [jnp.zeros((8, 128), F32) for _ in range(D // 128)]
    for k in range(0, wide, 2):
        v = [got[k + i].astype(F32) for i in range(2)]
        for c in range(3):
            piece = [t[c * ROWS_W : (c + 1) * ROWS_W] for t in v]
            piece = jnp.concatenate(piece, 0).astype(BF)
            for s in range(2):

                @pl.when(d == s)
                def _():
                    at = s * D + c * 128
                    w1[k * ROWS_W : (k + 2) * ROWS_W, at : at + 128] = piece

        for i in range(2):
            lay(chan, v[i][3 * ROWS_W : ROWS_P], (k + i) * ROWS_S)
            lay(gain, v[i][3 * ROWS_W : ROWS_P], (k + i) * ROWS_W)
    for c, v in enumerate(chan):
        chan_s[:, c * 128 : c * 128 + 128] = v
    for c, v in enumerate(gain):
        gain_s[:, c * 128 : c * 128 + 128] = v


def fill_owners(d, wide, gw1, pin, out):
    for k in range(wide):
        rows = slice(k * ROWS_W, (k + 1) * ROWS_W)
        parts = []
        at = k * ROWS_W % 16
        base = k * ROWS_W - at
        arrived = pin[base : base + 32, :].astype(F32)[at : at + ROWS_W]
        for c in range(3):
            low, high = gw1[rows, c * 128 : c * 128 + 128], gw1[rows, D + c * 128 : D + c * 128 + 128]
            parts.append(jnp.where(d == 0, low, high) + arrived[:, c * 128 : c * 128 + 128])
        parts.append(jnp.zeros((ROWS_P - 3 * ROWS_W, 128), F32))
        out[k] = jnp.concatenate(parts, 0).astype(BF)


def gather_plain(inp, state, step, decay, chan, gain):
    rows = state.shape[1]
    column = jnp.concatenate([gain, jnp.zeros((rows - gain.shape[0],), F32)])[:, None]
    small = [state[0], step[0].T, decay[0].T, chan[0].T, column, jnp.zeros((rows, 127 - ROW_GAIN), F32)]
    small = jnp.concatenate(small, 1).astype(BF)
    return (
        lax.all_gather(inp[:, :E].astype(BF), "wide", axis=0, tiled=True),
        lax.all_gather(small, "wide", axis=0, tiled=True),
    )


def reduce_plain(gw1, gs, gg):
    def total(v):
        return lax.psum_scatter(v, "wide", scatter_dimension=0, tiled=True)

    return total(lax.psum(gw1, "dir")), total(gs), total(lax.psum(gg.sum(0), "dir"))


def adam_step(weight, gradient, first_moment, second, step_rate, decay_rate):
    first_moment = BETA_ONE * first_moment + (1.0 - BETA_ONE) * gradient
    second = BETA_TWO * second + (1.0 - BETA_TWO) * gradient * gradient
    first_hat = first_moment / (1.0 - BETA_ONE**STEP)
    second_hat = second / (1.0 - BETA_TWO**STEP)
    weight = weight - step_rate * (
        first_hat / (jnp.sqrt(second_hat) + EPS_ADAM) + decay_rate * weight
    )
    return (weight, first_moment, second)


def update_kernel(got, twin, g2, g2x, *refs):
    stream = lax.axis_index("dir")
    masters, outs = refs[:21], refs[21:]

    def step(k, gradient, at=(slice(None),), out=None):
        new = adam_step(
            masters[3 * k][at], gradient, masters[3 * k + 1][at], masters[3 * k + 2][at], RATES[k], DECAYS[k]
        )
        for i in range(3):
            outs[1 + 3 * k + i][at] = new[i]

    mine, theirs = got[...], twin[...]
    low, high = jnp.where(stream == 0, mine, theirs), jnp.where(stream == 0, theirs, mine)
    for h, v in enumerate((low, high)):
        for c in range(3):
            at = ROWS_S + c * ROWS_W
            col = h * D + c * 128
            step(0, v[at : at + ROWS_W], (slice(None), slice(col, col + 128)))
    shared = g2[...] + g2x[...]
    step(0, shared[0:ROWS_W], (slice(None), slice(E, 2 * E)))
    step(1, shared[ROWS_W:, 0:D], (slice(0, ROWS_W), slice(None)))
    step(1, shared[ROWS_W:, D:], (slice(ROWS_W, 2 * ROWS_W), slice(None)))
    t = mine[0:128].T
    step(2, mine[AT_C + 7 : AT_C + 8, 0:ROWS_W] + theirs[AT_C + 7 : AT_C + 8, 0:ROWS_W])
    step(3, mine[0:ROWS_S, 0:ROW_STEP], (0,))
    step(4, t[ROW_STEP:ROW_DECAY, 0:ROWS_S], (0,))
    step(5, t[ROW_DECAY:ROW_CHAN, 0:ROWS_S], (0,))
    for k in range(7):
        step(6, mine[AT_C + k : AT_C + k + 1, 0:ROWS_S], (k,))
    outs[0][0] = mine[AT_C + 8 : AT_C + 10, 0:ROWS_S] + mine[AT_C + 10 : AT_C + 12, 0:ROWS_S]


def update(got, twin, g2, g2x, masters):
    S = jax.ShapeDtypeStruct
    masters = list(masters)
    masters[6:9] = [v[None] for v in masters[6:9]]
    masters[18:21] = [jnp.transpose(v, (1, 0, 2)) for v in masters[18:21]]
    outs = pl.pallas_call(
        update_kernel,
        out_shape=[S((1, 2, ROWS_S), F32)] + [S(v.shape, F32) for v in masters],
        in_specs=[VMEM] * 25,
        out_specs=[VMEM] * 22,
        name="update",
    )(got, twin, g2, g2x, *masters)
    stats, outs = outs[0], list(outs[1:])
    outs[6:9] = [v[0] for v in outs[6:9]]
    outs[18:21] = [jnp.transpose(v, (1, 0, 2)) for v in outs[18:21]]
    return stats, outs


def update_plain(gw1, gs, gg, g2, masters):
    drow = masters[0].shape[0]
    g1, small, gain = reduce_plain(gw1, gs, gg)
    t = small.T
    grads = (
        jnp.concatenate([g1, g2[:drow]], 1),
        jnp.concatenate([g2[drow:, :D], g2[drow:, D:]], 0),
        gain,
        small[None, :, :ROW_STEP],
        t[None, ROW_STEP:ROW_DECAY],
        t[None, ROW_DECAY:ROW_CHAN],
        t[None, ROW_CHAN:ROW_GAIN],
    )
    outs = []
    for k, g in enumerate(grads):
        w, f, s2 = masters[3 * k : 3 * k + 3]
        outs += adam_step(w, g, f, s2, RATES[k], DECAYS[k])
    return (t[ROW_STATS : ROW_STATS + 2] + t[ROW_STATS + 2 : ROW_STATS + 4])[None], outs


def local(tokens, cotangent, view_counts, view_strides, view_offsets, *masters):
    wide = lax.axis_size("wide")
    in_proj, out_proj, gain = masters[0], masters[3], masters[6]
    erow = out_proj.shape[0]
    mine = E // wide == ROWS_S and D // wide == ROWS_W
    about = (view_counts, view_offsets, view_strides)
    tok, cot = tokens[0], cotangent[0]
    small = masters[9], masters[12], masters[15]
    if mine:
        chan = jnp.transpose(masters[18], (1, 0, 2))
        *kept, pack, stats, hs = forward(wide, mine, *about, tok, in_proj, out_proj, *small, chan, gain[None])
    else:
        pair = jnp.concatenate([out_proj[: erow // 2], out_proj[erow // 2 :]], 1)
        pack = lax.all_gather(jnp.concatenate([in_proj[:, E:], pair], 0).astype(BF), "wide", axis=0)
        given = gather_plain(in_proj, *small, masters[18], gain)
        *kept, stats, hs = forward(wide, mine, *about, tok, *given)
    normed, x, act, dl, p, st, res, other, w1 = kept
    block, token_grad, *sums = backward(
        wide, mine, *about, tok, cot, normed, pack, stats, w1, st, res, other, x, act, dl, p, hs
    )
    if mine:
        stats, outs = update(*sums, masters)
    else:
        gw1, gs, gg, g2 = sums
        g2 = lax.psum(lax.psum_scatter(g2, "wide", scatter_dimension=0, tiled=True)[0], "dir")
        stats, outs = update_plain(gw1, gs, gg, g2, masters)
    return (jnp.transpose(block, (1, 0, 2)), jnp.transpose(token_grad, (1, 0, 2)), stats, *outs)


def solution(mesh):
    row, col = P("wide", None), P("dir", None, "wide")
    mat = P("dir", "wide", None)
    weights = [row] * 6 + [P("wide")] * 3 + [mat] * 3 + [col] * 9
    return jax.shard_map(
        local,
        mesh=mesh,
        in_specs=(
            P("wide", None, None), P("wide", "dir", None), P("wide"), row, row, *weights,
        ),
        out_specs=(P("wide", "dir", None), P("wide", "dir", None), col, *weights),
        check_vma=False,
    )
```
